32 devices in a mesh: row: 4 (over z), col: 8 (over y, x, core).
Axes of the slice: x: 2, y: 2, z: 4, core: 2. Of those that a mesh axis runs over, the one named last changes fastest.
Arguments:
- layer_input: bfloat16 [512, 8192], P('col', 'row'), may hold values from -6 to 6
- out_grad: bfloat16 [512, 8192], P('col', 'row'), may hold values from -6 to 6
- gate_saved: bfloat16 [512, 14336], P('row', 'col'), may hold values from -8 to 8
- up_saved: bfloat16 [512, 14336], P('row', 'col'), may hold values from -6 to 6
- gate_weight: bfloat16 [8192, 14336], P('row', 'col'), may hold values from -0.0625 to 0.0625
- up_weight: bfloat16 [8192, 14336], P('row', 'col'), may hold values from -0.0625 to 0.0625
- down_weight: bfloat16 [14336, 8192], P('col', 'row'), may hold values from -0.046875 to 0.046875
Outputs:
- input_grad: bfloat16 [512, 8192], P('col', 'row')
- gate_weight_grad: float32 [8192, 14336], P('row', 'col')
- up_weight_grad: float32 [8192, 14336], P('row', 'col')
- down_weight_grad: float32 [14336, 8192], P('col', 'row')
The draws below stay inside these ranges and needn't reach their ends.
All inputs are finite; a program needn't handle non-finite values.
Results may differ from the reference program's by a relative error of at most 0.02.
Values may be sent and summed in bfloat16 or wider, within the bound.
No kernel may reach another device: no remote copies, remote signals or barrier semaphores. Data moves between devices by JAX's collectives and lax.ppermute only.
A program may use at most 128 MiB of HBM per device.

```python
import jax
import jax.numpy as jnp
from jax import lax

D = 8192
FF = 14336
TOKENS = 512
N_COL = 8


def shard_levels(own_key, dims, shards, smallest, top_value):
    loudness, own = 1.0, jax.random.fold_in(own_key, 6)
    for axis_at, blocks in shards:
        draws = jnp.exp(jax.random.uniform(jax.random.fold_in(own, axis_at), (blocks,), jnp.float32, smallest / len(shards), top_value / len(shards)))
        loudness = loudness * jnp.repeat(draws, dims[axis_at] // blocks).reshape([-1 if axis == axis_at else 1 for axis in range(len(dims))])
    return loudness


def centred(rng, shape, spread, limit, cuts=(), kind=jnp.bfloat16):
    level = shard_levels(rng, shape, cuts, -0.22, 0.18) if cuts else 1.0
    values = jax.random.normal(rng, shape, jnp.float32) * spread * level
    return jnp.minimum(jnp.maximum(values, -limit), limit).astype(kind)


def setup_inputs(seed: int = 0) -> dict:
    key_of = jax.random.split(jax.random.key(seed), 8)
    layer_input = centred(key_of[0], (TOKENS, D), 1.0, 6.0, ((0, 8), (1, 4)))
    out_grad = centred(key_of[1], (TOKENS, D), 1.0, 6.0, ((0, 8), (1, 4)))
    gate_saved = centred(key_of[2], (TOKENS, FF), 1.5, 8.0, ((0, 4), (1, 8)))
    up_saved = centred(key_of[3], (TOKENS, FF), 1.0, 6.0, ((0, 4), (1, 8)))
    gate_weight = centred(key_of[4], (D, FF), D ** -0.5, 0.0625, ((0, 4), (1, 8)))
    up_weight = centred(key_of[5], (D, FF), D ** -0.5, 0.0625, ((0, 4), (1, 8)))
    down_weight = centred(key_of[6], (FF, D), FF ** -0.5, 0.046875, ((0, 8), (1, 4)))
    return dict(layer_input=layer_input, out_grad=out_grad, gate_saved=gate_saved, up_saved=up_saved, gate_weight=gate_weight, up_weight=up_weight, down_weight=down_weight)


def contract_last(left, right):
    return lax.dot_general(left, right, (((1,), (1,)), ((), ())), preferred_element_type=jnp.float32)


def contract_first(left, right):
    return lax.dot_general(left, right, (((0,), (0,)), ((), ())), preferred_element_type=jnp.float32)


def reference(layer_input, out_grad, gate_saved, up_saved, gate_weight, up_weight, down_weight):
    hidden_grad = contract_last(out_grad, down_weight)
    gate_val = gate_saved.astype(jnp.float32)
    up_val = up_saved.astype(jnp.float32)
    sigma = 1.0 / (1.0 + jnp.exp(-gate_val))
    silu_val = gate_val * sigma
    hidden = (silu_val * up_val).astype(jnp.bfloat16)
    gate_grad = (hidden_grad * up_val * sigma * (1.0 + gate_val * (1.0 - sigma))).astype(jnp.bfloat16)
    up_grad = (hidden_grad * silu_val).astype(jnp.bfloat16)
    ff_block = FF // N_COL
    input_total = jnp.zeros((TOKENS, D), jnp.float32)
    for block in range(N_COL):
        lower = block * ff_block
        upper = lower + ff_block
        block_term = contract_last(gate_grad[:, lower:upper], gate_weight[:, lower:upper]) + contract_last(up_grad[:, lower:upper], up_weight[:, lower:upper])
        input_total = input_total + block_term.astype(jnp.bfloat16).astype(jnp.float32)
    input_grad = input_total.astype(jnp.bfloat16)
    scale = float(TOKENS) ** -0.5
    gate_weight_grad = scale * contract_first(layer_input, gate_grad)
    up_weight_grad = scale * contract_first(layer_input, up_grad)
    down_weight_grad = scale * contract_first(hidden, out_grad)
    return input_grad, gate_weight_grad, up_weight_grad, down_weight_grad
```

```python
import jax
import jax.numpy as jnp
from jax import lax
from jax.experimental import pallas as pl
from jax.experimental.pallas import tpu as pltpu
from jax.sharding import PartitionSpec as P

CHUNKS = 4
VMEM = 56 * 1024 * 1024


def tile_of(size, limit):
    return max(t for t in range(128, limit + 1, 128) if size % t == 0)


def params():
    return pltpu.CompilerParams(vmem_limit_bytes=VMEM)


def cost(flops, moved):
    return pl.CostEstimate(flops=flops, bytes_accessed=moved, transcendentals=0)


def dot(left, right, dims):
    return lax.dot_general(left, right, (dims, ((), ())), preferred_element_type=jnp.float32)


def sigmoid(gate):
    return 1.0 / (1.0 + jnp.exp(-gate))


def hidden_grad_terms(grad, down):
    cols, chunks, rows, depth = grad.shape
    wide = down.shape[0]
    tile = tile_of(wide, 256)

    def body(grad_ref, down_ref, *out_refs):
        left = grad_ref[...].reshape(cols * chunks * rows, depth)
        res = dot(left, down_ref[...], ((1,), (1,))).reshape(cols, chunks, rows, tile)
        for q in range(chunks):
            out_refs[q][...] = res[:, q].reshape(cols * rows, tile).astype(jnp.bfloat16)

    return pl.pallas_call(
        body,
        grid=(wide // tile,),
        in_specs=[
            pl.BlockSpec((cols, chunks, rows, depth), lambda i: (0, 0, 0, 0)),
            pl.BlockSpec((tile, depth), lambda i: (i, 0)),
        ],
        out_specs=[pl.BlockSpec((cols * rows, tile), lambda i: (0, i))] * chunks,
        out_shape=[jax.ShapeDtypeStruct((cols * rows, wide), jnp.bfloat16)] * chunks,
        compiler_params=params(),
        cost_estimate=cost(2 * cols * chunks * rows * depth * wide, 2 * (down.size + grad.size)),
        name="hidden_grad_terms",
    )(grad, down)


def arrange(own, lefts, rights, axis, cols, chunks):
    shards = len(lefts) + 1
    blocks, _, rows, wide = own[0].shape
    n = len(own)
    flat = []
    for j in range(n):
        flat += [own[j]] + [x[j] for x in lefts] + [x[j] for x in rights]

    def body(*refs):
        ins, outs, sem = refs[: len(flat)], refs[len(flat) : len(flat) + n], refs[-1]
        here = lax.axis_index(axis)
        per = 2 * shards - 1

        def put(j, shard, src):
            for q in range(chunks):
                pltpu.make_async_copy(
                    src.at[:, q], outs[j].at[q, pl.ds(shard * blocks, blocks)], sem.at[j, shard, q]
                ).start()

        for j in range(n):
            group = ins[j * per : (j + 1) * per]
            for shard in range(shards):

                @pl.when(here == shard)
                def _():
                    put(j, shard, group[0])

                for k in range(shards - 1):

                    @pl.when(here - 1 - k == shard)
                    def _():
                        put(j, shard, group[1 + k])

                    @pl.when(here + 1 + k == shard)
                    def _():
                        put(j, shard, group[shards + k])

        for j in range(n):
            for shard in range(shards):
                for q in range(chunks):
                    pltpu.make_async_copy(
                        ins[j * per].at[:, q],
                        outs[j].at[q, pl.ds(shard * blocks, blocks)],
                        sem.at[j, shard, q],
                    ).wait()

    return pl.pallas_call(
        body,
        in_specs=[pl.BlockSpec(memory_space=pl.ANY)] * len(flat),
        out_specs=[pl.BlockSpec(memory_space=pl.ANY)] * n,
        out_shape=[jax.ShapeDtypeStruct((chunks, cols, rows, wide), jnp.bfloat16)] * n,
        scratch_shapes=[pltpu.SemaphoreType.DMA((n, shards, chunks))],
        compiler_params=params(),
        cost_estimate=cost(0, 4 * n * chunks * cols * rows * wide),
        name="arrange",
    )(*flat)


def down_weight_grads(gate, up, grad, scale):
    chunks, cols, rows, wide = gate.shape
    depth = grad.shape[-1]
    tokens = chunks * cols * rows
    tile = tile_of(wide, 256)

    def body(gate_ref, up_ref, grad_ref, out_ref, hidden_ref):
        for q in range(chunks):
            gate_val = gate_ref[q].astype(jnp.float32)
            up_val = up_ref[q].astype(jnp.float32)
            hidden_ref[:, q] = (gate_val * sigmoid(gate_val) * up_val).astype(jnp.bfloat16)
        left = hidden_ref[...].reshape(tokens, tile)
        right = grad_ref[...].reshape(tokens, depth)
        out_ref[...] = scale * dot(left, right, ((0,), (0,)))

    return pl.pallas_call(
        body,
        grid=(wide // tile,),
        in_specs=[
            pl.BlockSpec((chunks, cols, rows, tile), lambda i: (0, 0, 0, i)),
            pl.BlockSpec((chunks, cols, rows, tile), lambda i: (0, 0, 0, i)),
            pl.BlockSpec((cols, chunks, rows, depth), lambda i: (0, 0, 0, 0)),
        ],
        out_specs=pl.BlockSpec((tile, depth), lambda i: (i, 0)),
        out_shape=jax.ShapeDtypeStruct((wide, depth), jnp.float32),
        scratch_shapes=[pltpu.VMEM((cols, chunks, rows, tile), jnp.bfloat16)],
        compiler_params=params(),
        cost_estimate=cost(2 * tokens * wide * depth, 4 * wide * depth),
        name="down_weight_grads",
    )(gate, up, grad)


def input_grad_terms(q, sums, gate, up, gate_weight, up_weight, made):
    chunks, cols, rows, wide = gate.shape
    depth = gate_weight.shape[0]
    tokens = cols * rows
    tile = tile_of(depth, 256)

    def body(sums_ref, gate_ref, up_ref, gate_w_ref, up_w_ref, *refs):
        gate_out, up_out, out_ref = refs[-3:]

        @pl.when(pl.program_id(0) == 0)
        def _():
            hidden_grad = sums_ref[...].astype(jnp.float32)
            gate_val = gate_ref[...].reshape(tokens, wide).astype(jnp.float32)
            up_val = up_ref[...].reshape(tokens, wide).astype(jnp.float32)
            sigma = sigmoid(gate_val)
            gate_out[...] = (
                hidden_grad * up_val * sigma * (1.0 + gate_val * (1.0 - sigma))
            ).astype(jnp.bfloat16)
            up_out[...] = (hidden_grad * (gate_val * sigma)).astype(jnp.bfloat16)

        out_ref[...] = (
            dot(gate_out[...], gate_w_ref[...], ((1,), (1,)))
            + dot(up_out[...], up_w_ref[...], ((1,), (1,)))
        ).astype(jnp.bfloat16)

    once = pl.BlockSpec((None, cols, rows, wide), lambda i: (q, 0, 0, 0))
    into = pl.BlockSpec((None, tokens, wide), lambda i: (q, 0, 0))
    weight = pl.BlockSpec((tile, wide), lambda i: (i, 0))
    anywhere = pl.BlockSpec(memory_space=pl.ANY)
    whole = jax.ShapeDtypeStruct((chunks, tokens, wide), jnp.bfloat16)
    return pl.pallas_call(
        body,
        grid=(depth // tile,),
        in_specs=[pl.BlockSpec((tokens, wide), lambda i: (0, 0)), once, once, weight, weight]
        + [anywhere] * len(made),
        out_specs=[into, into, pl.BlockSpec((tokens, tile), lambda i: (0, i))],
        out_shape=[whole, whole, jax.ShapeDtypeStruct((tokens, depth), jnp.bfloat16)],
        input_output_aliases={5 + j: j for j in range(len(made))},
        compiler_params=params(),
        cost_estimate=cost(4 * tokens * wide * depth, 4 * wide * depth),
        name="input_grad_terms",
    )(sums, gate, up, gate_weight, up_weight, *made)


def projection_grads(inputs, gate_grad, up_grad, scale):
    depth, tokens = inputs.shape
    wide = gate_grad.shape[1]
    tile = tile_of(depth, 256)

    def body(inputs_ref, gate_ref, up_ref, gate_out, up_out):
        left = inputs_ref[...]
        gate_out[...] = scale * dot(left, gate_ref[...], ((1,), (0,)))
        up_out[...] = scale * dot(left, up_ref[...], ((1,), (0,)))

    once = pl.BlockSpec((tokens, wide), lambda i: (0, 0))
    out = pl.BlockSpec((tile, wide), lambda i: (i, 0))
    return pl.pallas_call(
        body,
        grid=(depth // tile,),
        in_specs=[pl.BlockSpec((tile, tokens), lambda i: (i, 0)), once, once],
        out_specs=[out, out],
        out_shape=[jax.ShapeDtypeStruct((depth, wide), jnp.float32)] * 2,
        compiler_params=params(),
        cost_estimate=cost(4 * tokens * wide * depth, 8 * wide * depth),
        name="projection_grads",
    )(inputs, gate_grad, up_grad)


def gather_line(shard, axis, size):
    up = [(i, i + 1) for i in range(size - 1)]
    down = [(i + 1, i) for i in range(size - 1)]
    lefts, rights = [], []
    from_left = from_right = shard
    for step in range(size - 1):
        from_left = lax.ppermute(from_left, axis, up[step:])
        from_right = lax.ppermute(from_right, axis, down[: size - 1 - step])
        lefts.append(from_left)
        rights.append(from_right)
    return lefts, rights


def sum_line(term, axis, size):
    here = lax.axis_index(axis)
    half = size // 2
    total = term
    for k in range(half - 1):
        got = lax.ppermute(total, axis, [(k, k + 1), (size - 1 - k, size - 2 - k)])
        total = (term.astype(jnp.float32) + got.astype(jnp.float32)).astype(jnp.bfloat16)
    got = lax.ppermute(total, axis, [(half - 1, half), (half, half - 1)])
    total = (total.astype(jnp.float32) + got.astype(jnp.float32)).astype(jnp.bfloat16)
    for k in reversed(range(half - 1)):
        got = lax.ppermute(total, axis, [(k + 1, k), (size - 2 - k, size - 1 - k)])
        outer = (here == k) | (here == size - 1 - k)
        total = jnp.where(outer, got, total)
    return total


def scatter_sum(term, axis, size):
    here = lax.axis_index(axis)
    rows, depth = term.shape[1:]
    left = size
    bit = 1
    while left > 1:
        pairs = term.reshape(left // 2, 2, rows, depth)
        mine = (here // bit) % 2
        keep = lax.dynamic_index_in_dim(pairs, mine, 1, keepdims=False)
        send = lax.dynamic_index_in_dim(pairs, 1 - mine, 1, keepdims=False)
        got = lax.ppermute(send, axis, [(i, i ^ bit) for i in range(size)])
        term = (keep.astype(jnp.float32) + got.astype(jnp.float32)).astype(jnp.bfloat16)
        left //= 2
        bit *= 2
    return term[0]


def solution(mesh):
    n_row, n_col = mesh.shape["row"], mesh.shape["col"]

    def shards(layer_input, out_grad, gate_saved, up_saved, gate_weight, up_weight, down_weight):
        block, depth = layer_input.shape
        row_tokens, wide = gate_saved.shape
        tokens = block * n_col
        rows = block // CHUNKS
        scale = float(tokens) ** (-0.5)

        grad = lax.all_gather(out_grad, "col", axis=0, tiled=True).reshape(
            n_col, CHUNKS, rows, depth
        )
        view = (row_tokens // block, CHUNKS, rows, wide)
        lefts, rights, own = [], [], []
        for saved in (gate_saved, up_saved):
            saved = saved.reshape(view)
            from_left, from_right = gather_line(saved, "row", n_row)
            own.append(saved)
            lefts.append(from_left)
            rights.append(from_right)
        gate, up = arrange(own, list(zip(*lefts)), list(zip(*rights)), "row", n_col, CHUNKS)

        terms = hidden_grad_terms(grad, down_weight)
        sums = [sum_line(term, "row", n_row) for term in terms]

        down_weight_grad = down_weight_grads(gate, up, grad, scale)

        inputs = lax.all_gather(layer_input, "col", axis=0, tiled=True)
        inputs = inputs.reshape(n_col, CHUNKS, rows, depth).transpose(3, 1, 0, 2)
        inputs = inputs.reshape(depth, tokens)

        made, parts = (), []
        for q in range(CHUNKS):
            *made, term = input_grad_terms(q, sums[q], gate, up, gate_weight, up_weight, made)
            parts.append(scatter_sum(term.reshape(n_col, rows, depth), "col", n_col))
        input_grad = jnp.concatenate(parts, axis=0)

        gate_grad, up_grad = (x.reshape(tokens, wide) for x in made)
        gate_weight_grad, up_weight_grad = projection_grads(inputs, gate_grad, up_grad, scale)
        return input_grad, gate_weight_grad, up_weight_grad, down_weight_grad

    by_token, by_unit = P("col", "row"), P("row", "col")
    return jax.shard_map(
        shards,
        mesh=mesh,
        in_specs=(by_token, by_token, by_unit, by_unit, by_unit, by_unit, by_token),
        out_specs=(by_token, by_unit, by_unit, by_token),
        check_vma=False,
    )
```

```python
import jax
import jax.numpy as jnp
from jax import lax
from jax.experimental import pallas as pl
from jax.experimental.pallas import tpu as pltpu
from jax.sharding import PartitionSpec as P

CHUNKS = 4
VMEM = 56 * 1024 * 1024


def tile_of(size, limit):
    return max(t for t in range(128, limit + 1, 128) if size % t == 0)


def params():
    return pltpu.CompilerParams(vmem_limit_bytes=VMEM)


def cost(flops, moved):
    return pl.CostEstimate(flops=flops, bytes_accessed=moved, transcendentals=0)


def dot(left, right, dims):
    return lax.dot_general(left, right, (dims, ((), ())), preferred_element_type=jnp.float32)


def sigmoid(gate):
    return 1.0 / (1.0 + jnp.exp(-gate))


def hidden_grad_terms(grad, down):
    cols, chunks, rows, depth = grad.shape
    tokens = cols * chunks * rows
    wide = down.shape[0]
    tile = tile_of(wide, 256)

    def body(grad_ref, down_ref, *refs):
        out_refs, turned = refs[:-1], refs[-1]

        @pl.when(pl.program_id(0) == 0)
        def _():
            turned[...] = grad_ref[...].reshape(tokens, depth).T

        res = dot(down_ref[...], turned[...], ((1,), (0,)))
        res = res.astype(jnp.bfloat16).T.reshape(cols, chunks, rows, tile)
        for q in range(chunks):
            out_refs[q][...] = res[:, q].reshape(cols * rows, tile)

    return pl.pallas_call(
        body,
        grid=(wide // tile,),
        in_specs=[
            pl.BlockSpec((cols, chunks, rows, depth), lambda i: (0, 0, 0, 0)),
            pl.BlockSpec((tile, depth), lambda i: (i, 0)),
        ],
        out_specs=[pl.BlockSpec((cols * rows, tile), lambda i: (0, i))] * chunks,
        out_shape=[jax.ShapeDtypeStruct((cols * rows, wide), jnp.bfloat16)] * chunks,
        scratch_shapes=[pltpu.VMEM((depth, tokens), jnp.bfloat16)],
        compiler_params=params(),
        cost_estimate=cost(2 * tokens * depth * wide, 2 * (down.size + grad.size)),
        name="hidden_grad_terms",
    )(grad, down)


def down_weight_grads(gates, ups, places, grad, axis, scale):
    blocks, _, _, wide = gates[0].shape
    cols, chunks, rows, depth = grad.shape
    tokens = chunks * cols * rows
    tile = tile_of(wide, 256)
    n = len(gates)

    def body(*refs):
        gate_refs, up_refs = refs[:n], refs[n : 2 * n]
        grad_ref, out_ref, hidden_ref = refs[2 * n :]
        for k, (shard, there) in enumerate(places(lax.axis_index(axis))):

            @pl.when(there)
            def _():
                gate_val = gate_refs[k][...].astype(jnp.float32)
                up_val = up_refs[k][...].astype(jnp.float32)
                hidden = (gate_val * sigmoid(gate_val) * up_val).astype(jnp.bfloat16)
                hidden_ref[pl.ds(shard * blocks, blocks)] = hidden

        left = hidden_ref[...].reshape(tokens, tile)
        right = grad_ref[...].reshape(tokens, depth)
        out_ref[...] = scale * dot(left, right, ((0,), (0,)))

    saved = pl.BlockSpec((blocks, chunks, rows, tile), lambda i: (0, 0, 0, i))
    return pl.pallas_call(
        body,
        grid=(wide // tile,),
        in_specs=[saved] * (2 * n)
        + [pl.BlockSpec((cols, chunks, rows, depth), lambda i: (0, 0, 0, 0))],
        out_specs=pl.BlockSpec((tile, depth), lambda i: (i, 0)),
        out_shape=jax.ShapeDtypeStruct((wide, depth), jnp.float32),
        scratch_shapes=[pltpu.VMEM((cols, chunks, rows, tile), jnp.bfloat16)],
        compiler_params=params(),
        cost_estimate=cost(2 * tokens * wide * depth, 4 * wide * depth),
        name="down_weight_grads",
    )(*gates, *ups, grad)


def input_grad_terms(q, sums, gates, ups, places, gate_weight, up_weight, axis, made):
    blocks, chunks, rows, wide = gates[0].shape
    depth = gate_weight.shape[0]
    tokens = sums.shape[0]
    cols = tokens // rows
    tile = tile_of(depth, 256)
    part = blocks * rows
    n = len(gates)

    def body(sums_ref, *refs):
        gate_refs, up_refs = refs[:n], refs[n : 2 * n]
        gate_w_ref, up_w_ref = refs[2 * n : 2 * n + 2]
        gate_out, up_out, out_ref, gate_turned, up_turned = refs[-5:]

        @pl.when(pl.program_id(0) == 0)
        def _():
            for k, (shard, there) in enumerate(places(lax.axis_index(axis))):

                @pl.when(there)
                def _():
                    first = pl.multiple_of(shard * part, part)
                    hidden_grad = sums_ref[pl.ds(first, part)].astype(jnp.float32)
                    gate_val = gate_refs[k][...].reshape(part, wide).astype(jnp.float32)
                    up_val = up_refs[k][...].reshape(part, wide).astype(jnp.float32)
                    sigma = sigmoid(gate_val)
                    gate_grad = hidden_grad * up_val * sigma * (1.0 + gate_val * (1.0 - sigma))
                    up_grad = hidden_grad * (gate_val * sigma)
                    to = pl.ds(shard * blocks, blocks)
                    shape = (blocks, rows, wide)
                    gate_out[to] = gate_grad.astype(jnp.bfloat16).reshape(shape)
                    up_out[to] = up_grad.astype(jnp.bfloat16).reshape(shape)

            gate_turned[...] = gate_out[...].reshape(tokens, wide).T
            up_turned[...] = up_out[...].reshape(tokens, wide).T

        res = dot(gate_w_ref[...], gate_turned[...], ((1,), (0,)))
        res += dot(up_w_ref[...], up_turned[...], ((1,), (0,)))
        out_ref[...] = res.astype(jnp.bfloat16).T

    saved = pl.BlockSpec((blocks, None, rows, wide), lambda i: (0, q, 0, 0))
    into = pl.BlockSpec((cols, None, rows, wide), lambda i: (0, q, 0, 0))
    weight = pl.BlockSpec((tile, wide), lambda i: (i, 0))
    anywhere = pl.BlockSpec(memory_space=pl.ANY)
    whole = jax.ShapeDtypeStruct((cols, chunks, rows, wide), jnp.bfloat16)
    return pl.pallas_call(
        body,
        grid=(depth // tile,),
        in_specs=[pl.BlockSpec((tokens, wide), lambda i: (0, 0))]
        + [saved] * (2 * n)
        + [weight, weight]
        + [anywhere] * len(made),
        out_specs=[into, into, pl.BlockSpec((tokens, tile), lambda i: (0, i))],
        out_shape=[whole, whole, jax.ShapeDtypeStruct((tokens, depth), jnp.bfloat16)],
        input_output_aliases={3 + 2 * n + j: j for j in range(len(made))},
        scratch_shapes=[pltpu.VMEM((wide, tokens), jnp.bfloat16)] * 2,
        compiler_params=params(),
        cost_estimate=cost(4 * tokens * wide * depth, 4 * wide * depth),
        name="input_grad_terms",
    )(sums, *gates, *ups, gate_weight, up_weight, *made)


def projection_grads(inputs, gate_grad, up_grad, scale):
    depth, tokens = inputs.shape
    wide = gate_grad.shape[1]
    tile = tile_of(depth, 256)

    def body(inputs_ref, gate_ref, up_ref, gate_out, up_out):
        left = inputs_ref[...]
        gate_out[...] = scale * dot(left, gate_ref[...], ((1,), (0,)))
        up_out[...] = scale * dot(left, up_ref[...], ((1,), (0,)))

    once = pl.BlockSpec((tokens, wide), lambda i: (0, 0))
    out = pl.BlockSpec((tile, wide), lambda i: (i, 0))
    return pl.pallas_call(
        body,
        grid=(depth // tile,),
        in_specs=[pl.BlockSpec((tile, tokens), lambda i: (i, 0)), once, once],
        out_specs=[out, out],
        out_shape=[jax.ShapeDtypeStruct((depth, wide), jnp.float32)] * 2,
        compiler_params=params(),
        cost_estimate=cost(4 * tokens * wide * depth, 8 * wide * depth),
        name="projection_grads",
    )(inputs, gate_grad, up_grad)


def gather_line(shard, axis, size):
    found = [shard]
    if size == 4:
        swap1 = [(i, i ^ 1) for i in range(size)]
        swap2 = [(i, i ^ 2) for i in range(size)]
        second = lax.ppermute(shard, axis, swap2)
        first = lax.ppermute(shard, axis, swap1)
        middle = lax.ppermute(shard, axis, [(1, 2), (2, 1)])
        far = lax.ppermute(second, axis, [(2, 3), (1, 0)])

        def places(here):
            outer = (here == 0) | (here == 3)
            return [
                (here, True),
                (here ^ 1, True),
                (here ^ 2, True),
                (here ^ 3, outer),
                (here ^ 3, jnp.logical_not(outer)),
            ]

        return [shard, first, second, far, middle], places

    up = [(i, i + 1) for i in range(size - 1)]
    down = [(i + 1, i) for i in range(size - 1)]
    from_left = from_right = shard
    for step in range(size - 1):
        from_left = lax.ppermute(from_left, axis, up[step:])
        from_right = lax.ppermute(from_right, axis, down[: size - 1 - step])
        found += [from_left, from_right]

    def places(here):
        out = [(here, True)]
        for k in range(1, size):
            out += [(here - k, here >= k), (here + k, here + k < size)]
        return out

    return found, places


def sum_line(term, axis, size):
    here = lax.axis_index(axis)
    half = size // 2
    total = term
    for k in range(half - 1):
        got = lax.ppermute(total, axis, [(k, k + 1), (size - 1 - k, size - 2 - k)])
        total = (term.astype(jnp.float32) + got.astype(jnp.float32)).astype(jnp.bfloat16)
    got = lax.ppermute(total, axis, [(half - 1, half), (half, half - 1)])
    total = (total.astype(jnp.float32) + got.astype(jnp.float32)).astype(jnp.bfloat16)
    for k in reversed(range(half - 1)):
        got = lax.ppermute(total, axis, [(k + 1, k), (size - 2 - k, size - 1 - k)])
        outer = (here == k) | (here == size - 1 - k)
        total = jnp.where(outer, got, total)
    return total


def solution(mesh):
    n_row, n_col = mesh.shape["row"], mesh.shape["col"]

    def shards(layer_input, out_grad, gate_saved, up_saved, gate_weight, up_weight, down_weight):
        block, depth = layer_input.shape
        row_tokens, wide = gate_saved.shape
        tokens = block * n_col
        rows = block // CHUNKS
        scale = float(tokens) ** (-0.5)

        grad = lax.all_gather(out_grad, "col", axis=0, tiled=True).reshape(
            n_col, CHUNKS, rows, depth
        )
        view = (row_tokens // block, CHUNKS, rows, wide)
        gates, places = gather_line(gate_saved.reshape(view), "row", n_row)
        ups, _ = gather_line(up_saved.reshape(view), "row", n_row)

        terms = hidden_grad_terms(grad, down_weight)
        sums = [sum_line(term, "row", n_row) for term in terms]

        down_weight_grad = down_weight_grads(gates, ups, places, grad, "row", scale)
        inputs = lax.all_gather(layer_input, "col", axis=0, tiled=True).T

        made, parts = (), []
        for q in range(CHUNKS):
            *made, term = input_grad_terms(
                q, sums[q], gates, ups, places, gate_weight, up_weight, "row", made
            )
            parts.append(lax.psum_scatter(term, "col", scatter_dimension=0, tiled=True))
        input_grad = jnp.concatenate(parts, axis=0)

        gate_grad, up_grad = (x.reshape(tokens, wide) for x in made)
        gate_weight_grad, up_weight_grad = projection_grads(inputs, gate_grad, up_grad, scale)
        return input_grad, gate_weight_grad, up_weight_grad, down_weight_grad

    by_token, by_unit = P("col", "row"), P("row", "col")
    return jax.shard_map(
        shards,
        mesh=mesh,
        in_specs=(by_token, by_token, by_unit, by_unit, by_unit, by_unit, by_token),
        out_specs=(by_token, by_unit, by_unit, by_token),
        check_vma=False,
    )
```

```python
import jax
import jax.numpy as jnp
from jax import lax
from jax.experimental import pallas as pl
from jax.experimental.pallas import tpu as pltpu
from jax.sharding import PartitionSpec as P

CHUNKS = 4
VMEM = 20 * 1024 * 1024


def tile_of(size, limit):
    return max(t for t in range(128, limit + 1, 128) if size % t == 0)


def params():
    return pltpu.CompilerParams(vmem_limit_bytes=VMEM)


def cost(flops, moved):
    return pl.CostEstimate(flops=flops, bytes_accessed=moved, transcendentals=0)


def dot(left, right, dims):
    return lax.dot_general(left, right, (dims, ((), ())), preferred_element_type=jnp.float32)


def sigmoid(gate):
    return 1.0 / (1.0 + jnp.exp(-gate))


def hidden_grad_terms(grad, down):
    cols, chunks, rows, depth = grad.shape
    tokens = cols * chunks * rows
    wide = down.shape[0]
    tile = tile_of(wide, 256)

    def body(grad_ref, down_ref, *refs):
        out_refs, turned = refs[:-1], refs[-1]

        @pl.when(pl.program_id(0) == 0)
        def _():
            turned[...] = grad_ref[...].reshape(tokens, depth).T

        res = dot(down_ref[...], turned[...], ((1,), (0,)))
        res = res.astype(jnp.bfloat16).T.reshape(cols, chunks, rows, tile)
        for q in range(chunks):
            out_refs[q][...] = res[:, q].reshape(cols * rows, tile)

    return pl.pallas_call(
        body,
        grid=(wide // tile,),
        in_specs=[
            pl.BlockSpec((cols, chunks, rows, depth), lambda i: (0, 0, 0, 0)),
            pl.BlockSpec((tile, depth), lambda i: (i, 0)),
        ],
        out_specs=[pl.BlockSpec((cols * rows, tile), lambda i: (0, i))] * chunks,
        out_shape=[jax.ShapeDtypeStruct((cols * rows, wide), jnp.bfloat16)] * chunks,
        scratch_shapes=[pltpu.VMEM((depth, tokens), jnp.bfloat16)],
        compiler_params=params(),
        cost_estimate=cost(2 * tokens * depth * wide, 2 * (down.size + grad.size)),
        name="hidden_grad_terms",
    )(grad, down)


def down_weight_grads(gates, ups, places, grad, axis, scale):
    blocks, _, _, wide = gates[0].shape
    cols, chunks, rows, depth = grad.shape
    tokens = chunks * cols * rows
    tile = tile_of(wide, 256)
    n = len(gates)

    def body(*refs):
        gate_refs, up_refs = refs[:n], refs[n : 2 * n]
        grad_ref, out_ref, hidden_ref = refs[2 * n :]
        for k, (shard, there) in enumerate(places(lax.axis_index(axis))):

            @pl.when(there)
            def _():
                gate_val = gate_refs[k][...].astype(jnp.float32)
                up_val = up_refs[k][...].astype(jnp.float32)
                hidden = (gate_val * sigmoid(gate_val) * up_val).astype(jnp.bfloat16)
                hidden_ref[pl.ds(shard * blocks, blocks)] = hidden

        left = hidden_ref[...].reshape(tokens, tile)
        right = grad_ref[...].reshape(tokens, depth)
        out_ref[...] = scale * dot(left, right, ((0,), (0,)))

    saved = pl.BlockSpec((blocks, chunks, rows, tile), lambda i: (0, 0, 0, i))
    return pl.pallas_call(
        body,
        grid=(wide // tile,),
        in_specs=[saved] * (2 * n)
        + [pl.BlockSpec((cols, chunks, rows, depth), lambda i: (0, 0, 0, 0))],
        out_specs=pl.BlockSpec((tile, depth), lambda i: (i, 0)),
        out_shape=jax.ShapeDtypeStruct((wide, depth), jnp.float32),
        scratch_shapes=[pltpu.VMEM((cols, chunks, rows, tile), jnp.bfloat16)],
        compiler_params=params(),
        cost_estimate=cost(2 * tokens * wide * depth, 4 * wide * depth),
        name="down_weight_grads",
    )(*gates, *ups, grad)


def input_grad_terms(q, at, of, sums, gates, ups, places, gate_weight, up_weight, axes, made):
    blocks, chunks, rows, wide = gates[0].shape
    depth = gate_weight.shape[0]
    tokens = sums[0].shape[0]
    levels = len(sums)
    cols = tokens // rows
    tile = tile_of(depth, 256)
    part = blocks * rows
    n = len(gates)

    def body(*refs):
        sums_refs, refs = refs[:levels], refs[levels:]
        gate_refs, up_refs = refs[:n], refs[n : 2 * n]
        gate_w_ref, up_w_ref = refs[2 * n : 2 * n + 2]
        gate_out, up_out, keep_ref, send_ref, gate_turned, up_turned = refs[-6:]

        @pl.when(pl.program_id(0) == 0)
        def _():
            here = lax.axis_index(axes[0])
            for k, (shard, there) in enumerate(places(here)):

                @pl.when(there)
                def _():
                    first = pl.multiple_of(shard * part, part)
                    hidden_grad = sums_refs[0][pl.ds(first, part)].astype(jnp.float32)
                    for level in range(1, levels):
                        at_level = (here == levels - 1 - level) | (here == levels + level)
                        other = sums_refs[level][pl.ds(first, part)].astype(jnp.float32)
                        hidden_grad = jnp.where(at_level, other, hidden_grad)
                    gate_val = gate_refs[k][...].reshape(part, wide).astype(jnp.float32)
                    up_val = up_refs[k][...].reshape(part, wide).astype(jnp.float32)
                    sigma = sigmoid(gate_val)
                    gate_grad = hidden_grad * up_val * sigma * (1.0 + gate_val * (1.0 - sigma))
                    up_grad = hidden_grad * (gate_val * sigma)
                    to = pl.ds(shard * blocks, blocks)
                    shape = (blocks, rows, wide)
                    gate_out[to] = gate_grad.astype(jnp.bfloat16).reshape(shape)
                    up_out[to] = up_grad.astype(jnp.bfloat16).reshape(shape)

            gate_turned[...] = gate_out[...].reshape(tokens, wide).T
            up_turned[...] = up_out[...].reshape(tokens, wide).T

        res = dot(gate_w_ref[...], gate_turned[...], ((1,), (0,)))
        res += dot(up_w_ref[...], up_turned[...], ((1,), (0,)))
        res = res.astype(jnp.bfloat16).T.reshape(cols // 2, 2, rows, tile)
        odd = lax.axis_index(axes[1]) % 2 == 1
        keep_ref[...] = jnp.where(odd, res[:, 1], res[:, 0])
        send_ref[...] = jnp.where(odd, res[:, 0], res[:, 1])

    saved = pl.BlockSpec((blocks, None, rows, wide), lambda i: (0, q, 0, 0))
    into = pl.BlockSpec((cols, None, rows, wide), lambda i: (0, q, 0, 0))
    weight = pl.BlockSpec((tile, wide), lambda i: (i, 0))
    anywhere = pl.BlockSpec(memory_space=pl.ANY)
    half = pl.BlockSpec((cols // 2, None, rows, tile), lambda i: (0, at, 0, i))
    halves = jax.ShapeDtypeStruct((cols // 2, of, rows, depth), jnp.bfloat16)
    whole = jax.ShapeDtypeStruct((cols, chunks, rows, wide), jnp.bfloat16)
    return pl.pallas_call(
        body,
        grid=(depth // tile,),
        in_specs=[pl.BlockSpec((tokens, wide), lambda i: (0, 0))] * levels
        + [saved] * (2 * n)
        + [weight, weight]
        + [anywhere] * sum(x is not None for x in made),
        out_specs=[into, into, half, half],
        out_shape=[whole, whole, halves, halves],
        input_output_aliases={levels + 2 + 2 * n + j: j for j in range(4) if made[j] is not None},
        scratch_shapes=[pltpu.VMEM((wide, tokens), jnp.bfloat16)] * 2,
        compiler_params=params(),
        cost_estimate=cost(4 * tokens * wide * depth, 4 * wide * depth),
        name="input_grad_terms",
    )(*sums, *gates, *ups, gate_weight, up_weight, *[x for x in made if x is not None])


def projection_grads(inputs, gate_grad, up_grad, scale):
    depth, tokens = inputs.shape
    wide = gate_grad.shape[1]
    tile = tile_of(depth, 256)

    def body(inputs_ref, gate_ref, up_ref, gate_out, up_out):
        left = inputs_ref[...]
        gate_out[...] = scale * dot(left, gate_ref[...], ((1,), (0,)))
        up_out[...] = scale * dot(left, up_ref[...], ((1,), (0,)))

    once = pl.BlockSpec((tokens, wide), lambda i: (0, 0))
    out = pl.BlockSpec((tile, wide), lambda i: (i, 0))
    return pl.pallas_call(
        body,
        grid=(depth // tile,),
        in_specs=[pl.BlockSpec((tile, tokens), lambda i: (i, 0)), once, once],
        out_specs=[out, out],
        out_shape=[jax.ShapeDtypeStruct((depth, wide), jnp.float32)] * 2,
        compiler_params=params(),
        cost_estimate=cost(4 * tokens * wide * depth, 8 * wide * depth),
        name="projection_grads",
    )(inputs, gate_grad, up_grad)


def gather_line(shard, axis, size):
    found = [shard]
    if size == 4:
        swap1 = [(i, i ^ 1) for i in range(size)]
        swap2 = [(i, i ^ 2) for i in range(size)]
        second = lax.ppermute(shard, axis, swap2)
        first = lax.ppermute(shard, axis, swap1)
        middle = lax.ppermute(shard, axis, [(1, 2), (2, 1)])
        far = lax.ppermute(second, axis, [(2, 3), (1, 0)])

        def places(here):
            outer = (here == 0) | (here == 3)
            return [
                (here, True),
                (here ^ 1, True),
                (here ^ 2, True),
                (here ^ 3, outer),
                (here ^ 3, jnp.logical_not(outer)),
            ]

        return [shard, first, second, far, middle], places

    up = [(i, i + 1) for i in range(size - 1)]
    down = [(i + 1, i) for i in range(size - 1)]
    from_left = from_right = shard
    for step in range(size - 1):
        from_left = lax.ppermute(from_left, axis, up[step:])
        from_right = lax.ppermute(from_right, axis, down[: size - 1 - step])
        found += [from_left, from_right]

    def places(here):
        out = [(here, True)]
        for k in range(1, size):
            out += [(here - k, here >= k), (here + k, here + k < size)]
        return out

    return found, places


def both(left, right):
    return (left.astype(jnp.float32) + right.astype(jnp.float32)).astype(jnp.bfloat16)


def sum_in(term, axis, size):
    total = term
    for k in range(size // 2 - 1):
        got = lax.ppermute(total, axis, [(k, k + 1), (size - 1 - k, size - 2 - k)])
        total = both(term, got)
    return total


def sum_swap(total, axis, size):
    half = size // 2
    return both(total, lax.ppermute(total, axis, [(half - 1, half), (half, half - 1)]))


def sum_out(total, axis, size):
    found = [total]
    for k in reversed(range(size // 2 - 1)):
        found.append(lax.ppermute(found[-1], axis, [(k + 1, k), (size - 2 - k, size - 1 - k)]))
    return found


def scatter_halves(keep, send, axis, size):
    return both(keep, lax.ppermute(send, axis, [(i, i ^ 1) for i in range(size)]))


def scatter_sum(half, axis, size):
    here = lax.axis_index(axis)

    def block(k):
        return lax.dynamic_index_in_dim(half, (here // 2) ^ k, 0, keepdims=False)

    total = block(0).astype(jnp.float32)
    for k in range(1, size // 2):
        got = lax.ppermute(block(k), axis, [(i, i ^ (2 * k)) for i in range(size)])
        total += got.astype(jnp.float32)
    return total.astype(jnp.bfloat16)


def solution(mesh):
    n_row, n_col = mesh.shape["row"], mesh.shape["col"]

    def shards(layer_input, out_grad, gate_saved, up_saved, gate_weight, up_weight, down_weight):
        block, depth = layer_input.shape
        row_tokens, wide = gate_saved.shape
        tokens = block * n_col
        rows = block // CHUNKS
        scale = float(tokens) ** (-0.5)

        grad = lax.all_gather(out_grad, "col", axis=0, tiled=True).reshape(
            n_col, CHUNKS, rows, depth
        )
        view = (row_tokens // block, CHUNKS, rows, wide)
        gates, places = gather_line(gate_saved.reshape(view), "row", n_row)
        ups, _ = gather_line(up_saved.reshape(view), "row", n_row)

        terms = hidden_grad_terms(grad, down_weight)
        terms, gates[1], gates[2], ups[1], ups[2] = lax.optimization_barrier(
            (terms, gates[1], gates[2], ups[1], ups[2])
        )
        weights = (gate_weight, up_weight)
        groups = (range(CHUNKS - 1), range(CHUNKS - 1, CHUNKS))
        made = [None] * 4

        def input_grad_of(q, found):
            group = groups[q >= CHUNKS - 1]
            if q == group[0]:
                made[2:] = [None, None]
            made[:] = input_grad_terms(
                q, q - group[0], len(group), found, gates, ups, places, *weights, ("row", "col"), made
            )

        sums = []
        for q in range(CHUNKS):
            term = terms[q]
            if q >= 2:
                term, sums[q - 2][0] = lax.optimization_barrier((term, sums[q - 2][0]))
            total = sum_in(term, "row", n_row)
            if q >= 2:
                total, sums[q - 2][-1] = lax.optimization_barrier((total, sums[q - 2][-1]))
            if q == CHUNKS - 1:
                input_grad_of(0, sums[0])
                total, made[2] = lax.optimization_barrier((total, made[2]))
            total = sum_swap(total, "row", n_row)
            if q == 0:
                later, total = lax.optimization_barrier((grad, total))
                down_weight_grad = down_weight_grads(gates, ups, places, later, "row", scale)
            if q == 1:
                inputs = lax.all_gather(layer_input, "col", axis=0, tiled=True)
                inputs, total = lax.optimization_barrier((inputs, total))
                inputs = inputs.T
            if q == CHUNKS - 1:
                sums[1][-1], down_weight_grad, inputs = lax.optimization_barrier(
                    (sums[1][-1], down_weight_grad, inputs)
                )
                input_grad_of(1, sums[1])
                total, made[2] = lax.optimization_barrier((total, made[2]))
            sums.append(sum_out(total, "row", n_row))

        input_grad_of(2, sums[2])
        early = scatter_halves(*made[2:], "col", n_col)
        sums[3][-1], early = lax.optimization_barrier((sums[3][-1], early))
        early = scatter_sum(early, "col", n_col)
        input_grad_of(3, sums[3])
        late = scatter_sum(scatter_halves(*made[2:], "col", n_col), "col", n_col)
        input_grad = jnp.concatenate([early, late], axis=0).reshape(block, depth)

        gate_grad, up_grad = made[:2]
        gate_grad, up_grad = gate_grad.reshape(tokens, wide), up_grad.reshape(tokens, wide)
        gate_weight_grad, up_weight_grad = projection_grads(inputs, gate_grad, up_grad, scale)
        return input_grad, gate_weight_grad, up_weight_grad, down_weight_grad

    by_token, by_unit = P("col", "row"), P("row", "col")
    return jax.shard_map(
        shards,
        mesh=mesh,
        in_specs=(by_token, by_token, by_unit, by_unit, by_unit, by_unit, by_token),
        out_specs=(by_token, by_unit, by_unit, by_token),
        check_vma=False,
    )
```

```python
import jax
import jax.numpy as jnp
from jax import lax
from jax.experimental import pallas as pl
from jax.experimental.pallas import tpu as pltpu
from jax.sharding import PartitionSpec as P

CHUNKS = 2
VMEM = 56 * 1024 * 1024


def tile_of(size, limit):
    return max(t for t in range(128, limit + 1, 128) if size % t == 0)


def params():
    return pltpu.CompilerParams(vmem_limit_bytes=VMEM)


def cost(flops, moved):
    return pl.CostEstimate(flops=flops, bytes_accessed=moved, transcendentals=0)


def dot(left, right, dims):
    return lax.dot_general(left, right, (dims, ((), ())), preferred_element_type=jnp.float32)


def sigmoid(gate):
    return 1.0 / (1.0 + jnp.exp(-gate))


def hidden_grad_terms(grad, down):
    cols, chunks, rows, depth = grad.shape
    tokens = cols * chunks * rows
    wide = down.shape[0]
    tile = tile_of(wide, 256)

    def body(grad_ref, down_ref, *refs):
        out_refs, turned = refs[:-1], refs[-1]

        @pl.when(pl.program_id(0) == 0)
        def _():
            turned[...] = grad_ref[...].reshape(tokens, depth).T

        res = dot(down_ref[...], turned[...], ((1,), (0,)))
        res = res.astype(jnp.bfloat16).T.reshape(cols, chunks, rows, tile)
        for q in range(chunks):
            out_refs[q][...] = res[:, q].reshape(cols * rows, tile)

    return pl.pallas_call(
        body,
        grid=(wide // tile,),
        in_specs=[
            pl.BlockSpec((cols, chunks, rows, depth), lambda i: (0, 0, 0, 0)),
            pl.BlockSpec((tile, depth), lambda i: (i, 0)),
        ],
        out_specs=[pl.BlockSpec((cols * rows, tile), lambda i: (0, i))] * chunks,
        out_shape=[jax.ShapeDtypeStruct((cols * rows, wide), jnp.bfloat16)] * chunks,
        scratch_shapes=[pltpu.VMEM((depth, tokens), jnp.bfloat16)],
        compiler_params=params(),
        cost_estimate=cost(2 * tokens * depth * wide, 2 * (down.size + grad.size)),
        name="hidden_grad_terms",
    )(grad, down)


def down_weight_grads(gates, ups, places, grad, axis, scale):
    blocks, _, _, wide = gates[0].shape
    cols, chunks, rows, depth = grad.shape
    tokens = chunks * cols * rows
    tile = tile_of(wide, 256)
    n = len(gates)

    def body(*refs):
        gate_refs, up_refs = refs[:n], refs[n : 2 * n]
        grad_ref, out_ref, by_gate_ref, by_up_ref, hidden_ref = refs[2 * n :]
        for k, (shard, there) in enumerate(places(lax.axis_index(axis))):

            @pl.when(there)
            def _():
                gate_val = gate_refs[k][...].astype(jnp.float32)
                up_val = up_refs[k][...].astype(jnp.float32)
                sigma = sigmoid(gate_val)
                silu = gate_val * sigma
                slope = sigma * (1.0 + gate_val * (1.0 - sigma))
                to = pl.ds(shard * blocks, blocks)
                hidden_ref[to] = (silu * up_val).astype(jnp.bfloat16)
                by_gate_ref[to] = (up_val * slope).astype(jnp.bfloat16)
                by_up_ref[to] = silu.astype(jnp.bfloat16)

        left = hidden_ref[...].reshape(tokens, tile)
        right = grad_ref[...].reshape(tokens, depth)
        out_ref[...] = scale * dot(left, right, ((0,), (0,)))

    saved = pl.BlockSpec((blocks, chunks, rows, tile), lambda i: (0, 0, 0, i))
    factor = pl.BlockSpec((cols, chunks, rows, tile), lambda i: (0, 0, 0, i))
    factors = jax.ShapeDtypeStruct((cols, chunks, rows, wide), jnp.bfloat16)
    return pl.pallas_call(
        body,
        grid=(wide // tile,),
        in_specs=[saved] * (2 * n)
        + [pl.BlockSpec((cols, chunks, rows, depth), lambda i: (0, 0, 0, 0))],
        out_specs=[pl.BlockSpec((tile, depth), lambda i: (i, 0)), factor, factor],
        out_shape=[jax.ShapeDtypeStruct((wide, depth), jnp.float32), factors, factors],
        scratch_shapes=[pltpu.VMEM((cols, chunks, rows, tile), jnp.bfloat16)],
        compiler_params=params(),
        cost_estimate=cost(2 * tokens * wide * depth, 4 * wide * depth),
        name="down_weight_grads",
    )(*gates, *ups, grad)


def input_grad_terms(q, sums, by_gate, by_up, gate_weight, up_weight, axes, made):
    cols, chunks, rows, wide = by_gate.shape
    depth = gate_weight.shape[0]
    tokens = cols * rows
    levels = len(sums)
    tile = tile_of(depth, 256)

    def body(*refs):
        sums_refs, refs = refs[:levels], refs[levels:]
        by_gate_ref, by_up_ref, gate_w_ref, up_w_ref = refs[:4]
        gate_out, up_out, keep_ref, send_ref, gate_turned, up_turned = refs[-6:]

        @pl.when(pl.program_id(0) == 0)
        def _():
            here = lax.axis_index(axes[0])
            hidden_grad = sums_refs[0][...].astype(jnp.float32)
            for level in range(1, levels):
                at_level = (here == levels - 1 - level) | (here == levels + level)
                other = sums_refs[level][...].astype(jnp.float32)
                hidden_grad = jnp.where(at_level, other, hidden_grad)
            for by_ref, turned, out in (
                (by_gate_ref, gate_turned, gate_out),
                (by_up_ref, up_turned, up_out),
            ):
                by = by_ref[...].reshape(tokens, wide).astype(jnp.float32)
                value = (hidden_grad * by).astype(jnp.bfloat16)
                out[...] = value.reshape(cols, rows, wide)
                turned[...] = value.T

        res = dot(gate_w_ref[...], gate_turned[...], ((1,), (0,)))
        res += dot(up_w_ref[...], up_turned[...], ((1,), (0,)))
        res = res.astype(jnp.bfloat16).T.reshape(cols // 2, 2, rows, tile)
        odd = lax.axis_index(axes[1]) % 2 == 1
        keep_ref[...] = jnp.where(odd, res[:, 1], res[:, 0])
        send_ref[...] = jnp.where(odd, res[:, 0], res[:, 1])

    into = pl.BlockSpec((cols, None, rows, wide), lambda i: (0, q, 0, 0))
    weight = pl.BlockSpec((tile, wide), lambda i: (i, 0))
    half = pl.BlockSpec((cols // 2, rows, tile), lambda i: (0, 0, i))
    halves = jax.ShapeDtypeStruct((cols // 2, rows, depth), jnp.bfloat16)
    whole = jax.ShapeDtypeStruct((cols, chunks, rows, wide), jnp.bfloat16)
    return pl.pallas_call(
        body,
        grid=(depth // tile,),
        in_specs=[pl.BlockSpec((tokens, wide), lambda i: (0, 0))] * levels
        + [into, into, weight, weight]
        + [pl.BlockSpec(memory_space=pl.ANY)] * len(made),
        out_specs=[into, into, half, half],
        out_shape=[whole, whole, halves, halves],
        input_output_aliases={levels + 4 + j: j for j in range(len(made))},
        scratch_shapes=[pltpu.VMEM((wide, tokens), jnp.bfloat16)] * 2,
        compiler_params=params(),
        cost_estimate=cost(4 * tokens * wide * depth, 4 * wide * depth),
        name="input_grad_terms",
    )(*sums, by_gate, by_up, gate_weight, up_weight, *made)


def projection_grad(inputs, grads, scale, name):
    depth, tokens = inputs.shape
    wide = grads.shape[1]
    tile = tile_of(depth, 256)

    def body(inputs_ref, grads_ref, out_ref):
        out_ref[...] = scale * dot(inputs_ref[...], grads_ref[...], ((1,), (0,)))

    return pl.pallas_call(
        body,
        grid=(depth // tile,),
        in_specs=[
            pl.BlockSpec((tile, tokens), lambda i: (i, 0)),
            pl.BlockSpec((tokens, wide), lambda i: (0, 0)),
        ],
        out_specs=pl.BlockSpec((tile, wide), lambda i: (i, 0)),
        out_shape=jax.ShapeDtypeStruct((depth, wide), jnp.float32),
        compiler_params=params(),
        cost_estimate=cost(2 * tokens * wide * depth, 4 * wide * depth),
        name=name,
    )(inputs, grads)


def gather_first(shard, axis, size):
    near = range(1, 3 if size == 4 else size)
    return [shard] + [lax.ppermute(shard, axis, [(i, i ^ k) for i in range(size)]) for k in near]


def gather_rest(found, axis, size):
    if size != 4:
        return found
    middle = lax.ppermute(found[0], axis, [(1, 2), (2, 1)])
    far = lax.ppermute(found[2], axis, [(2, 3), (1, 0)])
    return found + [far, middle]


def gather_places(size):
    def places(here):
        if size != 4:
            return [(here ^ k, True) for k in range(size)]
        outer = (here == 0) | (here == 3)
        inner = jnp.logical_not(outer)
        return [(here, True), (here ^ 1, True), (here ^ 2, True), (here ^ 3, outer), (here ^ 3, inner)]

    return places


def both(left, right):
    return (left.astype(jnp.float32) + right.astype(jnp.float32)).astype(jnp.bfloat16)


def sum_in(term, axis, size):
    total = term
    for k in range(size // 2 - 1):
        got = lax.ppermute(total, axis, [(k, k + 1), (size - 1 - k, size - 2 - k)])
        total = both(term, got)
    return total


def sum_swap(total, axis, size):
    half = size // 2
    return both(total, lax.ppermute(total, axis, [(half - 1, half), (half, half - 1)]))


def sum_out(total, axis, size):
    found = [total]
    for k in reversed(range(size // 2 - 1)):
        found.append(lax.ppermute(found[-1], axis, [(k + 1, k), (size - 2 - k, size - 1 - k)]))
    return found


def scatter_halves(keep, send, axis, size):
    return both(keep, lax.ppermute(send, axis, [(i, i ^ 1) for i in range(size)]))


def scatter_sum(half, axis, size):
    here = lax.axis_index(axis)

    def block(k):
        return lax.dynamic_index_in_dim(half, (here // 2) ^ k, 0, keepdims=False)

    total = block(0).astype(jnp.float32)
    for k in range(1, size // 2):
        got = lax.ppermute(block(k), axis, [(i, i ^ (2 * k)) for i in range(size)])
        total += got.astype(jnp.float32)
    return total.astype(jnp.bfloat16)


def hold(*values):
    return lax.optimization_barrier(values)


def solution(mesh):
    n_row, n_col = mesh.shape["row"], mesh.shape["col"]

    def shards(layer_input, out_grad, gate_saved, up_saved, gate_weight, up_weight, down_weight):
        block, depth = layer_input.shape
        row_tokens, wide = gate_saved.shape
        tokens = block * n_col
        rows = block // CHUNKS
        scale = float(tokens) ** (-0.5)

        grad = lax.all_gather(out_grad, "col", axis=0, tiled=True)
        grad = grad.reshape(n_col, CHUNKS, rows, depth)
        view = (row_tokens // block, CHUNKS, rows, wide)
        gates = gather_first(gate_saved.reshape(view), "row", n_row)
        ups = gather_first(up_saved.reshape(view), "row", n_row)
        terms = hidden_grad_terms(grad, down_weight)
        terms, gates, ups = hold(terms, gates, ups)

        terms = list(terms)
        swapped, sums = [None] * CHUNKS, [None] * CHUNKS
        made, halves = (), [None] * CHUNKS
        for step in range(CHUNKS + 2):
            if step < CHUNKS:
                terms[step] = sum_in(terms[step], "row", n_row)
            if 0 <= step - 1 < CHUNKS:
                swapped[step - 1] = sum_swap(terms[step - 1], "row", n_row)
            if 0 <= step - 2:
                sums[step - 2] = sum_out(swapped[step - 2], "row", n_row)
            held = (terms, swapped, sums)
            if step == 0:
                gates = gather_rest(gates, "row", n_row)
                ups = gather_rest(ups, "row", n_row)
                inputs = lax.all_gather(layer_input, "col", axis=0, tiled=True)
                (terms, swapped, sums), gates, ups, grad, inputs = hold(
                    held, gates, ups, grad, inputs
                )
            elif step == 1:
                down_weight_grad, by_gate, by_up = down_weight_grads(
                    gates, ups, gather_places(n_row), grad, "row", scale
                )
                (terms, swapped, sums), down_weight_grad, by_gate, by_up, inputs = hold(
                    held, down_weight_grad, by_gate, by_up, inputs
                )
            elif step == 2:
                inputs = inputs.T
                (terms, swapped, sums), inputs = hold(held, inputs)
            else:
                q = step - 3
                *made, keep, send = input_grad_terms(
                    q, sums[q], by_gate, by_up, gate_weight, up_weight, ("row", "col"), made
                )
                (terms, swapped, sums), *halves[q] = hold(held, keep, send)

        halves = [scatter_halves(*half, "col", n_col) for half in halves[:-1]]
        q = CHUNKS - 1
        *made, keep, send = input_grad_terms(
            q, sums[q], by_gate, by_up, gate_weight, up_weight, ("row", "col"), made
        )
        gate_grad, up_grad = (x.reshape(tokens, wide) for x in made)
        keep, send, halves = hold(keep, send, halves)
        parts = [scatter_sum(half, "col", n_col) for half in halves]
        last = scatter_halves(keep, send, "col", n_col)
        gate_weight_grad = projection_grad(inputs, gate_grad, scale, "gate_weight_grads")
        last, gate_weight_grad, inputs, parts = hold(last, gate_weight_grad, inputs, parts)
        parts.append(scatter_sum(last, "col", n_col))
        up_weight_grad = projection_grad(inputs, up_grad, scale, "up_weight_grads")
        input_grad = jnp.concatenate(parts, axis=0)
        return input_grad, gate_weight_grad, up_weight_grad, down_weight_grad

    by_token, by_unit = P("col", "row"), P("row", "col")
    return jax.shard_map(
        shards,
        mesh=mesh,
        in_specs=(by_token, by_token, by_unit, by_unit, by_unit, by_unit, by_token),
        out_specs=(by_token, by_unit, by_unit, by_token),
        check_vma=False,
    )
```

```python
import jax
import jax.numpy as jnp
from jax import lax
from jax.experimental import pallas as pl
from jax.experimental.pallas import tpu as pltpu
from jax.sharding import PartitionSpec as P

CHUNKS = 2
VMEM = 56 * 1024 * 1024


def tile_of(size, limit):
    return max(t for t in range(128, limit + 1, 128) if size % t == 0)


def params():
    return pltpu.CompilerParams(vmem_limit_bytes=VMEM)


def cost(flops, moved):
    return pl.CostEstimate(flops=flops, bytes_accessed=moved, transcendentals=0)


def dot(left, right, dims):
    return lax.dot_general(left, right, (dims, ((), ())), preferred_element_type=jnp.float32)


def halves_of(size):
    cut = max(size // 2 // 256 * 256, 128)
    return slice(0, size - cut), slice(size - cut, size)


def sigmoid(gate):
    return 1.0 / (1.0 + jnp.exp(-gate))


def hidden_grad_terms(grad, down):
    cols, chunks, rows, depth = grad.shape
    tokens = cols * chunks * rows
    wide = down.shape[0]
    tile = tile_of(wide, 256)

    def body(grad_ref, down_ref, *refs):
        out_refs, turned = refs[:-1], refs[-1]

        @pl.when(pl.program_id(0) == 0)
        def _():
            turned[...] = grad_ref[...].reshape(tokens, depth).T

        half = cols // 2
        for part in range(2):
            right = turned[:, part * tokens // 2 : (part + 1) * tokens // 2]
            res = dot(down_ref[...], right, ((1,), (0,)))
            res = res.astype(jnp.bfloat16).T.reshape(half, chunks, rows, tile)
            for q in range(chunks):
                out_refs[q][pl.ds(part * half * rows, half * rows)] = res[:, q].reshape(half * rows, tile)

    return pl.pallas_call(
        body,
        grid=(wide // tile,),
        in_specs=[
            pl.BlockSpec((cols, chunks, rows, depth), lambda i: (0, 0, 0, 0)),
            pl.BlockSpec((tile, depth), lambda i: (i, 0)),
        ],
        out_specs=[pl.BlockSpec((cols * rows, tile), lambda i: (0, i))] * chunks,
        out_shape=[jax.ShapeDtypeStruct((cols * rows, wide), jnp.bfloat16)] * chunks,
        scratch_shapes=[pltpu.VMEM((depth, tokens), jnp.bfloat16)],
        compiler_params=params(),
        cost_estimate=cost(2 * tokens * depth * wide, 2 * (down.size + grad.size)),
        name="hidden_grad_terms",
    )(grad, down)


def down_weight_grads(saved, places, grad, axis, scale):
    _, blocks, _, _, wide = saved[0].shape
    cols, chunks, rows, depth = grad.shape
    tokens = chunks * cols * rows
    tile = tile_of(wide, 256)
    n = len(saved)

    def body(*refs):
        saved_refs = refs[:n]
        grad_ref, out_ref, by_gate_ref, by_up_ref, hidden_ref = refs[n:]
        for k, (shard, there) in enumerate(places(lax.axis_index(axis))):

            @pl.when(there)
            def _():
                gate_val = saved_refs[k][0].astype(jnp.float32)
                up_val = saved_refs[k][1].astype(jnp.float32)
                sigma = sigmoid(gate_val)
                silu = gate_val * sigma
                slope = sigma * (1.0 + gate_val * (1.0 - sigma))
                to = pl.ds(shard * blocks, blocks)
                hidden_ref[to] = (silu * up_val).astype(jnp.bfloat16)
                by_gate_ref[to] = (up_val * slope).astype(jnp.bfloat16)
                by_up_ref[to] = silu.astype(jnp.bfloat16)

        left = hidden_ref[...].reshape(tokens, tile)
        for part in halves_of(depth):
            right = grad_ref[:, :, :, part].reshape(tokens, part.stop - part.start)
            out_ref[:, part] = scale * dot(left, right, ((0,), (0,)))

    shard = pl.BlockSpec((2, blocks, chunks, rows, tile), lambda i: (0, 0, 0, 0, i))
    factor = pl.BlockSpec((cols, chunks, rows, tile), lambda i: (0, 0, 0, i))
    factors = jax.ShapeDtypeStruct((cols, chunks, rows, wide), jnp.bfloat16)
    return pl.pallas_call(
        body,
        grid=(wide // tile,),
        in_specs=[shard] * n
        + [pl.BlockSpec((cols, chunks, rows, depth), lambda i: (0, 0, 0, 0))],
        out_specs=[pl.BlockSpec((tile, depth), lambda i: (i, 0)), factor, factor],
        out_shape=[jax.ShapeDtypeStruct((wide, depth), jnp.float32), factors, factors],
        scratch_shapes=[pltpu.VMEM((cols, chunks, rows, tile), jnp.bfloat16)],
        compiler_params=params(),
        cost_estimate=cost(2 * tokens * wide * depth, 4 * wide * depth),
        name="down_weight_grads",
    )(*saved, grad)


def input_grad_terms(q, sums, by_gate, by_up, gate_weight, up_weight, axes, made):
    cols, chunks, rows, wide = by_gate.shape
    depth = gate_weight.shape[0]
    tokens = cols * rows
    levels = len(sums)
    tile = tile_of(depth, 512)

    def body(*refs):
        sums_refs, refs = refs[:levels], refs[levels:]
        by_gate_ref, by_up_ref, gate_w_ref, up_w_ref = refs[:4]
        gate_out, up_out, keep_ref, send_ref, gate_turned, up_turned = refs[-6:]

        @pl.when(pl.program_id(0) == 0)
        def _():
            here = lax.axis_index(axes[0])
            hidden_grad = sums_refs[0][...].astype(jnp.float32)
            for level in range(1, levels):
                at_level = (here == levels - 1 - level) | (here == levels + level)
                other = sums_refs[level][...].astype(jnp.float32)
                hidden_grad = jnp.where(at_level, other, hidden_grad)
            for by_ref, turned, out in (
                (by_gate_ref, gate_turned, gate_out),
                (by_up_ref, up_turned, up_out),
            ):
                by = by_ref[...].reshape(tokens, wide).astype(jnp.float32)
                value = (hidden_grad * by).astype(jnp.bfloat16)
                out[...] = value.reshape(cols, rows, wide)
                turned[...] = value.T

        odd = lax.axis_index(axes[1]) % 2 == 1
        for part in halves_of(tile):
            res = dot(gate_w_ref[part], gate_turned[...], ((1,), (0,)))
            res += dot(up_w_ref[part], up_turned[...], ((1,), (0,)))
            res = res.astype(jnp.bfloat16).T.reshape(cols // 2, 2, rows, part.stop - part.start)
            keep_ref[:, :, part] = jnp.where(odd, res[:, 1], res[:, 0])
            send_ref[:, :, part] = jnp.where(odd, res[:, 0], res[:, 1])

    into = pl.BlockSpec((cols, None, rows, wide), lambda i: (0, q, 0, 0))
    weight = pl.BlockSpec((tile, wide), lambda i: (i, 0))
    half = pl.BlockSpec((cols // 2, rows, tile), lambda i: (0, 0, i))
    halves = jax.ShapeDtypeStruct((cols // 2, rows, depth), jnp.bfloat16)
    whole = jax.ShapeDtypeStruct((cols, chunks, rows, wide), jnp.bfloat16)
    return pl.pallas_call(
        body,
        grid=(depth // tile,),
        in_specs=[pl.BlockSpec((tokens, wide), lambda i: (0, 0))] * levels
        + [into, into, weight, weight]
        + [pl.BlockSpec(memory_space=pl.ANY)] * len(made),
        out_specs=[into, into, half, half],
        out_shape=[whole, whole, halves, halves],
        input_output_aliases={levels + 4 + j: j for j in range(len(made))},
        scratch_shapes=[pltpu.VMEM((wide, tokens), jnp.bfloat16)] * 2,
        compiler_params=params(),
        cost_estimate=cost(4 * tokens * wide * depth, 4 * wide * depth),
        name="input_grad_terms",
    )(*sums, by_gate, by_up, gate_weight, up_weight, *made)


def projection_grad(inputs, grads, scale, name):
    depth, tokens = inputs.shape
    wide = grads.shape[1]
    tile = tile_of(depth, 256)

    def body(inputs_ref, grads_ref, out_ref):
        for part in halves_of(wide):
            out_ref[:, part] = scale * dot(inputs_ref[...], grads_ref[:, part], ((1,), (0,)))

    return pl.pallas_call(
        body,
        grid=(depth // tile,),
        in_specs=[
            pl.BlockSpec((tile, tokens), lambda i: (i, 0)),
            pl.BlockSpec((tokens, wide), lambda i: (0, 0)),
        ],
        out_specs=pl.BlockSpec((tile, wide), lambda i: (i, 0)),
        out_shape=jax.ShapeDtypeStruct((depth, wide), jnp.float32),
        compiler_params=params(),
        cost_estimate=cost(2 * tokens * wide * depth, 4 * wide * depth),
        name=name,
    )(inputs, grads)


def gather_first(shard, axis, size):
    near = range(1, 3 if size == 4 else size)
    return [shard] + [lax.ppermute(shard, axis, [(i, i ^ k) for i in range(size)]) for k in near]


def gather_rest(found, axis, size):
    if size != 4:
        return found
    middle = lax.ppermute(found[0], axis, [(1, 2), (2, 1)])
    far = lax.ppermute(found[2], axis, [(2, 3), (1, 0)])
    return found + [far, middle]


def gather_places(size):
    def places(here):
        if size != 4:
            return [(here ^ k, True) for k in range(size)]
        outer = (here == 0) | (here == 3)
        inner = jnp.logical_not(outer)
        return [(here, True), (here ^ 1, True), (here ^ 2, True), (here ^ 3, outer), (here ^ 3, inner)]

    return places


def both(left, right):
    return (left.astype(jnp.float32) + right.astype(jnp.float32)).astype(jnp.bfloat16)


def sum_in(term, axis, size):
    total = term
    for k in range(size // 2 - 1):
        got = lax.ppermute(total, axis, [(k, k + 1), (size - 1 - k, size - 2 - k)])
        total = both(term, got)
    return total


def sum_swap(total, axis, size):
    half = size // 2
    return both(total, lax.ppermute(total, axis, [(half - 1, half), (half, half - 1)]))


def sum_out(total, axis, size):
    found = [total]
    for k in reversed(range(size // 2 - 1)):
        found.append(lax.ppermute(found[-1], axis, [(k + 1, k), (size - 2 - k, size - 1 - k)]))
    return found


def scatter_halves(keep, send, axis, size):
    return both(keep, lax.ppermute(send, axis, [(i, i ^ 1) for i in range(size)]))


def scatter_sum(half, axis, size):
    here = lax.axis_index(axis)

    def block(k):
        return lax.dynamic_index_in_dim(half, (here // 2) ^ k, 0, keepdims=False)

    total = block(0).astype(jnp.float32)
    for k in range(1, size // 2):
        got = lax.ppermute(block(k), axis, [(i, i ^ (2 * k)) for i in range(size)])
        total += got.astype(jnp.float32)
    return total.astype(jnp.bfloat16)


def hold(*values):
    return lax.optimization_barrier(values)


def solution(mesh):
    n_row, n_col = mesh.shape["row"], mesh.shape["col"]

    def shards(layer_input, out_grad, gate_saved, up_saved, gate_weight, up_weight, down_weight):
        block, depth = layer_input.shape
        row_tokens, wide = gate_saved.shape
        tokens = block * n_col
        rows = block // CHUNKS
        scale = float(tokens) ** (-0.5)

        grad = lax.all_gather(out_grad, "col", axis=0, tiled=True)
        grad = grad.reshape(n_col, CHUNKS, rows, depth)
        saved = jnp.stack([gate_saved, up_saved])
        saved = saved.reshape(2, row_tokens // block, CHUNKS, rows, wide)
        saved = gather_first(saved, "row", n_row)
        terms = hidden_grad_terms(grad, down_weight)
        terms, saved = hold(terms, saved)

        terms = list(terms)
        swapped, sums = [None] * CHUNKS, [None] * CHUNKS
        made, halves = (), [None] * CHUNKS
        for step in range(CHUNKS + 2):
            if step < CHUNKS:
                terms[step] = sum_in(terms[step], "row", n_row)
            if 0 <= step - 1 < CHUNKS:
                swapped[step - 1] = sum_swap(terms[step - 1], "row", n_row)
            if 0 <= step - 2:
                sums[step - 2] = sum_out(swapped[step - 2], "row", n_row)
            held = (terms, swapped, sums)
            if step == 0:
                saved = gather_rest(saved, "row", n_row)
                inputs = lax.all_gather(layer_input, "col", axis=0, tiled=True)
                (terms, swapped, sums), saved, grad, inputs = hold(held, saved, grad, inputs)
            elif step == 1:
                down_weight_grad, by_gate, by_up = down_weight_grads(
                    saved, gather_places(n_row), grad, "row", scale
                )
                (terms, swapped, sums), down_weight_grad, by_gate, by_up, inputs = hold(
                    held, down_weight_grad, by_gate, by_up, inputs
                )
            elif step == 2:
                inputs = inputs.T
                (terms, swapped, sums), inputs = hold(held, inputs)
            else:
                q = step - 3
                *made, keep, send = input_grad_terms(
                    q, sums[q], by_gate, by_up, gate_weight, up_weight, ("row", "col"), made
                )
                (terms, swapped, sums), *halves[q] = hold(held, keep, send)

        halves = [scatter_halves(*half, "col", n_col) for half in halves[:-1]]
        q = CHUNKS - 1
        *made, keep, send = input_grad_terms(
            q, sums[q], by_gate, by_up, gate_weight, up_weight, ("row", "col"), made
        )
        gate_grad, up_grad = (x.reshape(tokens, wide) for x in made)
        keep, send, halves = hold(keep, send, halves)
        parts = [scatter_sum(half, "col", n_col) for half in halves]
        last = scatter_halves(keep, send, "col", n_col)
        gate_weight_grad = projection_grad(inputs, gate_grad, scale, "gate_weight_grads")
        last, gate_weight_grad, inputs, parts = hold(last, gate_weight_grad, inputs, parts)
        parts.append(scatter_sum(last, "col", n_col))
        up_weight_grad = projection_grad(inputs, up_grad, scale, "up_weight_grads")
        input_grad = jnp.concatenate(parts, axis=0)
        return input_grad, gate_weight_grad, up_weight_grad, down_weight_grad

    by_token, by_unit = P("col", "row"), P("row", "col")
    return jax.shard_map(
        shards,
        mesh=mesh,
        in_specs=(by_token, by_token, by_unit, by_unit, by_unit, by_unit, by_token),
        out_specs=(by_token, by_unit, by_unit, by_token),
        check_vma=False,
    )
```

```python
import jax
import jax.numpy as jnp
from jax import lax
from jax.experimental import pallas as pl
from jax.experimental.pallas import tpu as pltpu
from jax.sharding import PartitionSpec as P

CHUNKS = 2
VMEM = 56 * 1024 * 1024


def tile_of(size, limit):
    return max(t for t in range(128, limit + 1, 128) if size % t == 0)


def params():
    return pltpu.CompilerParams(vmem_limit_bytes=VMEM)


def cost(flops, moved):
    return pl.CostEstimate(flops=flops, bytes_accessed=moved, transcendentals=0)


def dot(left, right, dims):
    return lax.dot_general(left, right, (dims, ((), ())), preferred_element_type=jnp.float32)


def halves_of(size):
    cut = max(size // 2 // 256 * 256, 128)
    return slice(0, size - cut), slice(size - cut, size)


def sigmoid(gate):
    return 1.0 / (1.0 + jnp.exp(-gate))


def hidden_grad_terms(grad, down):
    cols, chunks, rows, depth = grad.shape
    tokens = cols * chunks * rows
    wide = down.shape[0]
    tile = tile_of(wide, 256)

    def body(grad_ref, down_ref, *refs):
        out_refs, turned = refs[:-1], refs[-1]

        @pl.when(pl.program_id(0) == 0)
        def _():
            turned[...] = grad_ref[...].reshape(tokens, depth).T

        half = cols // 2
        for part in range(2):
            right = turned[:, part * tokens // 2 : (part + 1) * tokens // 2]
            res = dot(down_ref[...], right, ((1,), (0,)))
            res = res.astype(jnp.bfloat16).T.reshape(half, chunks, rows, tile)
            for q in range(chunks):
                out_refs[q][pl.ds(part * half * rows, half * rows)] = res[:, q].reshape(half * rows, tile)

    return pl.pallas_call(
        body,
        grid=(wide // tile,),
        in_specs=[
            pl.BlockSpec((cols, chunks, rows, depth), lambda i: (0, 0, 0, 0)),
            pl.BlockSpec((tile, depth), lambda i: (i, 0)),
        ],
        out_specs=[pl.BlockSpec((cols * rows, tile), lambda i: (0, i))] * chunks,
        out_shape=[jax.ShapeDtypeStruct((cols * rows, wide), jnp.bfloat16)] * chunks,
        scratch_shapes=[pltpu.VMEM((depth, tokens), jnp.bfloat16)],
        compiler_params=params(),
        cost_estimate=cost(2 * tokens * depth * wide, 2 * (down.size + grad.size)),
        name="hidden_grad_terms",
    )(grad, down)


def down_weight_grads(saved, places, grad, axis, scale):
    _, blocks, _, _, wide = saved[0].shape
    cols, chunks, rows, depth = grad.shape
    tokens = chunks * cols * rows
    tile = tile_of(wide, 256)
    n = len(saved)

    def body(*refs):
        saved_refs = refs[:n]
        grad_ref, out_ref, by_gate_ref, by_up_ref, hidden_ref = refs[n:]
        for k, (shard, there) in enumerate(places(lax.axis_index(axis))):

            @pl.when(there)
            def _():
                gate_val = saved_refs[k][0].astype(jnp.float32)
                up_val = saved_refs[k][1].astype(jnp.float32)
                sigma = sigmoid(gate_val)
                silu = gate_val * sigma
                slope = sigma * (1.0 + gate_val * (1.0 - sigma))
                to = pl.ds(shard * blocks, blocks)
                hidden_ref[to] = (silu * up_val).astype(jnp.bfloat16)
                by_gate_ref[to] = (up_val * slope).astype(jnp.bfloat16)
                by_up_ref[to] = silu.astype(jnp.bfloat16)

        left = hidden_ref[...].reshape(tokens, tile)
        for part in halves_of(depth):
            right = grad_ref[:, :, :, part].reshape(tokens, part.stop - part.start)
            out_ref[:, part] = scale * dot(left, right, ((0,), (0,)))

    shard = pl.BlockSpec((2, blocks, chunks, rows, tile), lambda i: (0, 0, 0, 0, i))
    factor = pl.BlockSpec((cols, chunks, rows, tile), lambda i: (0, 0, 0, i))
    factors = jax.ShapeDtypeStruct((cols, chunks, rows, wide), jnp.bfloat16)
    return pl.pallas_call(
        body,
        grid=(wide // tile,),
        in_specs=[shard] * n
        + [pl.BlockSpec((cols, chunks, rows, depth), lambda i: (0, 0, 0, 0))],
        out_specs=[pl.BlockSpec((tile, depth), lambda i: (i, 0)), factor, factor],
        out_shape=[jax.ShapeDtypeStruct((wide, depth), jnp.float32), factors, factors],
        scratch_shapes=[pltpu.VMEM((cols, chunks, rows, tile), jnp.bfloat16)],
        compiler_params=params(),
        cost_estimate=cost(2 * tokens * wide * depth, 4 * wide * depth),
        name="down_weight_grads",
    )(*saved, grad)


def input_grad_terms(q, sums, by_gate, by_up, gate_weight, up_weight, axes, made):
    cols, chunks, rows, wide = by_gate.shape
    depth = gate_weight.shape[0]
    tokens = cols * rows
    levels = len(sums)
    tile = tile_of(depth, 512)
    steps = depth // tile

    def body(*refs):
        sums_refs, refs = refs[:levels], refs[levels:]
        by_refs, weight_refs = refs[:2], refs[2:4]
        grad_outs, keep_ref, send_ref = refs[-12:-10], refs[-10], refs[-9]
        sums_in, by_in, weights_in, grads, turned, in_sems, weight_sems, out_sems = refs[-8:]

        first = [
            pltpu.make_async_copy(sums_refs[k], sums_in.at[k], in_sems.at[k]) for k in range(levels)
        ]
        first += [
            pltpu.make_async_copy(by_refs[k].at[:, q], by_in.at[k], in_sems.at[levels + k])
            for k in range(2)
        ]
        for copy in first:
            copy.start()
        weights = [
            [
                pltpu.make_async_copy(
                    weight_refs[k].at[pl.ds(i * tile, tile)],
                    weights_in.at[k, pl.ds(i * tile, tile)],
                    weight_sems.at[k, i],
                )
                for k in range(2)
            ]
            for i in range(steps)
        ]
        for pair in weights:
            for copy in pair:
                copy.start()
        for copy in first:
            copy.wait()

        here = lax.axis_index(axes[0])
        hidden_grad = sums_in[0].astype(jnp.float32)
        for level in range(1, levels):
            at_level = (here == levels - 1 - level) | (here == levels + level)
            hidden_grad = jnp.where(at_level, sums_in[level].astype(jnp.float32), hidden_grad)
        out_copies = []
        for k in range(2):
            by = by_in[k].reshape(tokens, wide).astype(jnp.float32)
            value = (hidden_grad * by).astype(jnp.bfloat16)
            grads[k] = value.reshape(cols, rows, wide)
            turned[k] = value.T
            copy = pltpu.make_async_copy(grads.at[k], grad_outs[k].at[:, q], out_sems.at[k])
            copy.start()
            out_copies.append(copy)

        odd = lax.axis_index(axes[1]) % 2 == 1
        for i in range(steps):
            for copy in weights[i]:
                copy.wait()
            part = slice(i * tile, (i + 1) * tile)
            res = dot(weights_in[0, part], turned[0], ((1,), (0,)))
            res += dot(weights_in[1, part], turned[1], ((1,), (0,)))
            res = res.astype(jnp.bfloat16).T.reshape(cols // 2, 2, rows, tile)
            keep_ref[:, :, part] = jnp.where(odd, res[:, 1], res[:, 0])
            send_ref[:, :, part] = jnp.where(odd, res[:, 0], res[:, 1])
        for copy in out_copies:
            copy.wait()

    anywhere = pl.BlockSpec(memory_space=pl.ANY)
    in_vmem = pl.BlockSpec(memory_space=pltpu.VMEM)
    halves = jax.ShapeDtypeStruct((cols // 2, rows, depth), jnp.bfloat16)
    whole = jax.ShapeDtypeStruct((cols, chunks, rows, wide), jnp.bfloat16)
    return pl.pallas_call(
        body,
        in_specs=[anywhere] * (levels + 4 + len(made)),
        out_specs=[anywhere, anywhere, in_vmem, in_vmem],
        out_shape=[whole, whole, halves, halves],
        input_output_aliases={levels + 4 + j: j for j in range(len(made))},
        scratch_shapes=[
            pltpu.VMEM((levels, tokens, wide), jnp.bfloat16),
            pltpu.VMEM((2, cols, rows, wide), jnp.bfloat16),
            pltpu.VMEM((2, depth, wide), jnp.bfloat16),
            pltpu.VMEM((2, cols, rows, wide), jnp.bfloat16),
            pltpu.VMEM((2, wide, tokens), jnp.bfloat16),
            pltpu.SemaphoreType.DMA((levels + 2,)),
            pltpu.SemaphoreType.DMA((2, steps)),
            pltpu.SemaphoreType.DMA((2,)),
        ],
        compiler_params=params(),
        cost_estimate=cost(4 * tokens * wide * depth, 4 * wide * depth),
        name="input_grad_terms",
    )(*sums, by_gate, by_up, gate_weight, up_weight, *made)


def projection_grad(inputs, grads, scale, name):
    depth, tokens = inputs.shape
    wide = grads.shape[1]
    tile = tile_of(depth, 256)
    steps = depth // tile
    slots = min(4, steps)

    def body(inputs_ref, grads_ref, out_ref, inputs_in, grads_in, made, in_sems, grads_sems, out_sems):
        piece = tokens // 4
        firsts = [
            pltpu.make_async_copy(
                grads_ref.at[pl.ds(k * piece, piece)],
                grads_in.at[pl.ds(k * piece, piece)],
                grads_sems.at[k],
            )
            for k in range(4)
        ]
        tiles = [
            pltpu.make_async_copy(
                inputs_ref.at[pl.ds(i * tile, tile)], inputs_in.at[pl.ds(i * tile, tile)], in_sems.at[i]
            )
            for i in range(steps)
        ]
        for copy in firsts + tiles:
            copy.start()
        for copy in firsts:
            copy.wait()
        outs = []
        for i in range(steps):
            tiles[i].wait()
            if i >= slots:
                outs[i - slots].wait()
            left = inputs_in[i * tile : (i + 1) * tile]
            made[i % slots] = scale * dot(left, grads_in[...], ((1,), (0,)))
            outs.append(
                pltpu.make_async_copy(
                    made.at[i % slots], out_ref.at[pl.ds(i * tile, tile)], out_sems.at[i % slots]
                )
            )
            outs[i].start()
        for copy in outs[-slots:]:
            copy.wait()

    return pl.pallas_call(
        body,
        in_specs=[pl.BlockSpec(memory_space=pl.ANY)] * 2,
        out_specs=pl.BlockSpec(memory_space=pl.ANY),
        out_shape=jax.ShapeDtypeStruct((depth, wide), jnp.float32),
        scratch_shapes=[
            pltpu.VMEM((depth, tokens), jnp.bfloat16),
            pltpu.VMEM((tokens, wide), jnp.bfloat16),
            pltpu.VMEM((slots, tile, wide), jnp.float32),
            pltpu.SemaphoreType.DMA((steps,)),
            pltpu.SemaphoreType.DMA((4,)),
            pltpu.SemaphoreType.DMA((slots,)),
        ],
        compiler_params=params(),
        cost_estimate=cost(2 * tokens * wide * depth, 4 * wide * depth),
        name=name,
    )(inputs, grads)


def gather_first(shard, axis, size):
    near = range(1, 3 if size == 4 else size)
    return [shard] + [lax.ppermute(shard, axis, [(i, i ^ k) for i in range(size)]) for k in near]


def gather_rest(found, axis, size):
    if size != 4:
        return found
    middle = lax.ppermute(found[0], axis, [(1, 2), (2, 1)])
    far = lax.ppermute(found[2], axis, [(2, 3), (1, 0)])
    return found + [far, middle]


def gather_places(size):
    def places(here):
        if size != 4:
            return [(here ^ k, True) for k in range(size)]
        outer = (here == 0) | (here == 3)
        inner = jnp.logical_not(outer)
        return [(here, True), (here ^ 1, True), (here ^ 2, True), (here ^ 3, outer), (here ^ 3, inner)]

    return places


def both(left, right):
    return (left.astype(jnp.float32) + right.astype(jnp.float32)).astype(jnp.bfloat16)


def sum_in(term, axis, size):
    total = term
    for k in range(size // 2 - 1):
        got = lax.ppermute(total, axis, [(k, k + 1), (size - 1 - k, size - 2 - k)])
        total = both(term, got)
    return total


def sum_swap(total, axis, size):
    half = size // 2
    return both(total, lax.ppermute(total, axis, [(half - 1, half), (half, half - 1)]))


def sum_out(total, axis, size):
    found = [total]
    for k in reversed(range(size // 2 - 1)):
        found.append(lax.ppermute(found[-1], axis, [(k + 1, k), (size - 2 - k, size - 1 - k)]))
    return found


def scatter_halves(keep, send, axis, size):
    return both(keep, lax.ppermute(send, axis, [(i, i ^ 1) for i in range(size)]))


def scatter_sum(half, axis, size):
    here = lax.axis_index(axis)

    def block(k):
        return lax.dynamic_index_in_dim(half, (here // 2) ^ k, 0, keepdims=False)

    total = block(0).astype(jnp.float32)
    for k in range(1, size // 2):
        got = lax.ppermute(block(k), axis, [(i, i ^ (2 * k)) for i in range(size)])
        total += got.astype(jnp.float32)
    return total.astype(jnp.bfloat16)


def hold(*values):
    return lax.optimization_barrier(values)


def solution(mesh):
    n_row, n_col = mesh.shape["row"], mesh.shape["col"]

    def shards(layer_input, out_grad, gate_saved, up_saved, gate_weight, up_weight, down_weight):
        block, depth = layer_input.shape
        row_tokens, wide = gate_saved.shape
        tokens = block * n_col
        rows = block // CHUNKS
        scale = float(tokens) ** (-0.5)

        grad = lax.all_gather(out_grad, "col", axis=0, tiled=True)
        grad = grad.reshape(n_col, CHUNKS, rows, depth)
        saved = jnp.stack([gate_saved, up_saved])
        saved = saved.reshape(2, row_tokens // block, CHUNKS, rows, wide)
        saved = gather_first(saved, "row", n_row)
        terms = hidden_grad_terms(grad, down_weight)
        saved, _ = hold(saved, terms)

        terms = list(terms)
        swapped, sums = [None] * CHUNKS, [None] * CHUNKS
        made, halves = (), [None] * CHUNKS
        for step in range(CHUNKS + 2):
            if step < CHUNKS:
                terms[step] = sum_in(terms[step], "row", n_row)
            if 0 <= step - 1 < CHUNKS:
                swapped[step - 1] = sum_swap(terms[step - 1], "row", n_row)
            if 0 <= step - 2:
                sums[step - 2] = sum_out(swapped[step - 2], "row", n_row)
            held = (terms, swapped, sums)
            if step == 0:
                saved = gather_rest(saved, "row", n_row)
                inputs = lax.all_gather(layer_input, "col", axis=0, tiled=True)
                inputs = lax.all_gather(layer_input, "col", axis=0, tiled=True)
                (terms,) = hold(terms)
            elif step == 1:
                saved, inputs = hold(saved, inputs)
                down_weight_grad, by_gate, by_up = down_weight_grads(
                    saved, gather_places(n_row), grad, "row", scale
                )
                (terms, swapped, sums), down_weight_grad, by_gate, by_up, inputs = hold(
                    held, down_weight_grad, by_gate, by_up, inputs
                )
            elif step == 2:
                inputs = inputs.T
                (terms, swapped, sums), inputs = hold(held, inputs)
            else:
                q = step - 3
                *made, keep, send = input_grad_terms(
                    q, sums[q], by_gate, by_up, gate_weight, up_weight, ("row", "col"), made
                )
                (terms, swapped, sums), *halves[q] = hold(held, keep, send)

        halves = [scatter_halves(*half, "col", n_col) for half in halves[:-1]]
        q = CHUNKS - 1
        *made, keep, send = input_grad_terms(
            q, sums[q], by_gate, by_up, gate_weight, up_weight, ("row", "col"), made
        )
        gate_grad, up_grad = (x.reshape(tokens, wide) for x in made)
        keep, send, halves = hold(keep, send, halves)
        parts = [scatter_sum(half, "col", n_col) for half in halves]
        last = scatter_halves(keep, send, "col", n_col)
        gate_weight_grad = projection_grad(inputs, gate_grad, scale, "gate_weight_grads")
        last, gate_weight_grad, inputs, parts = hold(last, gate_weight_grad, inputs, parts)
        parts.append(scatter_sum(last, "col", n_col))
        up_weight_grad = projection_grad(inputs, up_grad, scale, "up_weight_grads")
        input_grad = jnp.concatenate(parts, axis=0)
        return input_grad, gate_weight_grad, up_weight_grad, down_weight_grad

    by_token, by_unit = P("col", "row"), P("row", "col")
    return jax.shard_map(
        shards,
        mesh=mesh,
        in_specs=(by_token, by_token, by_unit, by_unit, by_unit, by_unit, by_token),
        out_specs=(by_token, by_unit, by_unit, by_token),
        check_vma=False,
    )
```

```python
import jax
import jax.numpy as jnp
from jax import lax
from jax.experimental import pallas as pl
from jax.experimental.pallas import tpu as pltpu
from jax.sharding import PartitionSpec as P

CHUNKS = 2
VMEM = 60 * 1024 * 1024


def tile_of(size, limit):
    return max(t for t in range(128, limit + 1, 128) if size % t == 0)


def params():
    return pltpu.CompilerParams(vmem_limit_bytes=VMEM)


def cost(flops, moved):
    return pl.CostEstimate(flops=flops, bytes_accessed=moved, transcendentals=0)


def dot(left, right, dims):
    return lax.dot_general(left, right, (dims, ((), ())), preferred_element_type=jnp.float32)


def halves_of(size):
    cut = max(size // 2 // 256 * 256, 128)
    return slice(0, size - cut), slice(size - cut, size)


def sigmoid(gate):
    return 1.0 / (1.0 + jnp.exp(-gate))


def hidden_grad_terms(grad, down):
    tokens, depth = grad.shape
    wide = down.shape[0]
    tile = tile_of(wide, 256)

    def body(grad_ref, down_ref, out_ref):
        res = dot(grad_ref[...], down_ref[...], ((1,), (1,)))
        out_ref[...] = res.astype(jnp.bfloat16)

    return pl.pallas_call(
        body,
        grid=(wide // tile,),
        in_specs=[
            pl.BlockSpec((tokens, depth), lambda i: (0, 0)),
            pl.BlockSpec((tile, depth), lambda i: (i, 0)),
        ],
        out_specs=pl.BlockSpec((tokens, tile), lambda i: (0, i)),
        out_shape=jax.ShapeDtypeStruct((tokens, wide), jnp.bfloat16),
        compiler_params=params(),
        cost_estimate=cost(2 * tokens * depth * wide, 2 * (down.size + grad.size)),
        name="hidden_grad_terms",
    )(grad, down)


def down_weight_grads(saved, places, grads, axis, scale):
    _, blocks, chunks, rows, wide = saved[0].shape
    part, depth = grads[0].shape
    cols = part // rows
    tile = tile_of(wide, 256)
    n = len(saved)

    def body(*refs):
        saved_refs = refs[:n]
        grad_refs, refs = refs[n : n + chunks], refs[n + chunks :]
        out_ref, by_gate_ref, by_up_ref, hidden_ref = refs
        for k, (shard, there) in enumerate(places(lax.axis_index(axis))):

            @pl.when(there)
            def _():
                gate_val = saved_refs[k][0].astype(jnp.float32)
                up_val = saved_refs[k][1].astype(jnp.float32)
                sigma = sigmoid(gate_val)
                silu = gate_val * sigma
                slope = sigma * (1.0 + gate_val * (1.0 - sigma))
                to = pl.ds(shard * blocks, blocks)
                hidden_ref[to] = (silu * up_val).astype(jnp.bfloat16)
                by_gate_ref[to] = (up_val * slope).astype(jnp.bfloat16)
                by_up_ref[to] = silu.astype(jnp.bfloat16)

        res = 0.0
        for q in range(chunks):
            left = hidden_ref[:, q].reshape(part, tile)
            res += dot(left, grad_refs[q][...], ((0,), (0,)))
        out_ref[...] = scale * res

    shard = pl.BlockSpec((2, blocks, chunks, rows, tile), lambda i: (0, 0, 0, 0, i))
    factor = pl.BlockSpec((cols, chunks, rows, tile), lambda i: (0, 0, 0, i))
    factors = jax.ShapeDtypeStruct((cols, chunks, rows, wide), jnp.bfloat16)
    return pl.pallas_call(
        body,
        grid=(wide // tile,),
        in_specs=[shard] * n
        + [pl.BlockSpec((part, depth), lambda i: (0, 0))] * chunks,
        out_specs=[pl.BlockSpec((tile, depth), lambda i: (i, 0)), factor, factor],
        out_shape=[jax.ShapeDtypeStruct((wide, depth), jnp.float32), factors, factors],
        scratch_shapes=[pltpu.VMEM((cols, chunks, rows, tile), jnp.bfloat16)],
        compiler_params=params(),
        cost_estimate=cost(2 * chunks * part * wide * depth, 4 * wide * depth),
        name="down_weight_grads",
    )(*saved, *grads)


def input_grad_terms(q, sums, by_gate, by_up, gate_weight, up_weight, axes, made):
    cols, chunks, rows, wide = by_gate.shape
    depth = gate_weight.shape[0]
    tokens = cols * rows
    levels = len(sums)
    tile = tile_of(depth, 512)

    def body(*refs):
        sums_refs, refs = refs[:levels], refs[levels:]
        by_gate_ref, by_up_ref, gate_w_ref, up_w_ref = refs[:4]
        gate_out, up_out, keep_ref, send_ref = refs[-4:]

        @pl.when(pl.program_id(0) == 0)
        def _():
            here = lax.axis_index(axes[0])
            hidden_grad = sums_refs[0][...].astype(jnp.float32)
            for level in range(1, levels):
                at_level = (here == levels - 1 - level) | (here == levels + level)
                other = sums_refs[level][...].astype(jnp.float32)
                hidden_grad = jnp.where(at_level, other, hidden_grad)
            for by_ref, out in ((by_gate_ref, gate_out), (by_up_ref, up_out)):
                by = by_ref[...].reshape(tokens, wide).astype(jnp.float32)
                out[...] = (hidden_grad * by).astype(jnp.bfloat16).reshape(cols, rows, wide)

        odd = lax.axis_index(axes[1]) % 2 == 1
        gate_grad = gate_out[...].reshape(tokens, wide)
        up_grad = up_out[...].reshape(tokens, wide)
        for part in halves_of(tile):
            res = dot(gate_grad, gate_w_ref[part], ((1,), (1,)))
            res += dot(up_grad, up_w_ref[part], ((1,), (1,)))
            res = res.astype(jnp.bfloat16).reshape(cols // 2, 2, rows, part.stop - part.start)
            keep_ref[:, :, part] = jnp.where(odd, res[:, 1], res[:, 0])
            send_ref[:, :, part] = jnp.where(odd, res[:, 0], res[:, 1])

    into = pl.BlockSpec((cols, None, rows, wide), lambda i: (0, q, 0, 0))
    weight = pl.BlockSpec((tile, wide), lambda i: (i, 0))
    half = pl.BlockSpec((cols // 2, rows, tile), lambda i: (0, 0, i))
    halves = jax.ShapeDtypeStruct((cols // 2, rows, depth), jnp.bfloat16)
    whole = jax.ShapeDtypeStruct((cols, chunks, rows, wide), jnp.bfloat16)
    return pl.pallas_call(
        body,
        grid=(depth // tile,),
        in_specs=[pl.BlockSpec((tokens, wide), lambda i: (0, 0))] * levels
        + [into, into, weight, weight]
        + [pl.BlockSpec(memory_space=pl.ANY)] * len(made),
        out_specs=[into, into, half, half],
        out_shape=[whole, whole, halves, halves],
        input_output_aliases={levels + 4 + j: j for j in range(len(made))},
        compiler_params=params(),
        cost_estimate=cost(4 * tokens * wide * depth, 4 * wide * depth),
        name="input_grad_terms",
    )(*sums, by_gate, by_up, gate_weight, up_weight, *made)


def projection_grads(inputs, gate_grad, up_grad, scale):
    depth, tokens = inputs.shape
    wide = gate_grad.shape[1]
    tile = tile_of(depth, 256)

    def body(inputs_ref, gate_ref, up_ref, gate_out, up_out):
        left = inputs_ref[...]
        gate_out[...] = scale * dot(left, gate_ref[...], ((1,), (0,)))
        up_out[...] = scale * dot(left, up_ref[...], ((1,), (0,)))

    once = pl.BlockSpec((tokens, wide), lambda i: (0, 0))
    out = pl.BlockSpec((tile, wide), lambda i: (i, 0))
    return pl.pallas_call(
        body,
        grid=(depth // tile,),
        in_specs=[pl.BlockSpec((tile, tokens), lambda i: (i, 0)), once, once],
        out_specs=[out, out],
        out_shape=[jax.ShapeDtypeStruct((depth, wide), jnp.float32)] * 2,
        compiler_params=params(),
        cost_estimate=cost(4 * tokens * wide * depth, 8 * wide * depth),
        name="projection_grads",
    )(inputs, gate_grad, up_grad)


def gather_places(size):
    def places(here):
        if size != 4:
            return [(here ^ k, True) for k in range(size)]
        outer = (here == 0) | (here == 3)
        inner = jnp.logical_not(outer)
        return [
            (here, True),
            (here ^ 1, True),
            (here ^ 3, inner),
            (here ^ 2, inner),
            (here ^ 2, outer),
            (here ^ 3, outer),
        ]

    return places


def gather_step(found, step, axis, size):
    inner, outward = [(1, 2), (2, 1)], [(2, 3), (1, 0)]
    if size != 4:
        near = range(1, size) if step == 0 else ()
        new = [(0, [(i, i ^ k) for i in range(size)]) for k in near]
    else:
        swap = [(i, i ^ 1) for i in range(size)]
        new = [[(0, swap), (0, inner)], [(1, inner), (2, outward)], [(3, outward)]][step]
    return found + [lax.ppermute(found[k], axis, pairs) for k, pairs in new]


def both(left, right):
    return (left.astype(jnp.float32) + right.astype(jnp.float32)).astype(jnp.bfloat16)


def sum_in(term, axis, size):
    total = term
    for k in range(size // 2 - 1):
        got = lax.ppermute(total, axis, [(k, k + 1), (size - 1 - k, size - 2 - k)])
        total = both(term, got)
    return total


def sum_swap(total, axis, size):
    half = size // 2
    return both(total, lax.ppermute(total, axis, [(half - 1, half), (half, half - 1)]))


def sum_out(total, axis, size):
    found = [total]
    for k in reversed(range(size // 2 - 1)):
        found.append(lax.ppermute(found[-1], axis, [(k + 1, k), (size - 2 - k, size - 1 - k)]))
    return found


def scatter_halves(keep, send, axis, size):
    return both(keep, lax.ppermute(send, axis, [(i, i ^ 1) for i in range(size)]))


def scatter_send(half, axis, size):
    here = lax.axis_index(axis)

    def block(k):
        return lax.dynamic_index_in_dim(half, (here // 2) ^ k, 0, keepdims=False)

    return [block(0)] + [
        lax.ppermute(block(k), axis, [(i, i ^ (2 * k)) for i in range(size)])
        for k in range(1, size // 2)
    ]


def add_up(terms):
    return sum(x.astype(jnp.float32) for x in terms).astype(jnp.bfloat16)


def hold(*values):
    return lax.optimization_barrier(values)


def solution(mesh):
    n_row, n_col = mesh.shape["row"], mesh.shape["col"]

    def shards(layer_input, out_grad, gate_saved, up_saved, gate_weight, up_weight, down_weight):
        block, depth = layer_input.shape
        row_tokens, wide = gate_saved.shape
        tokens = block * n_col
        rows = block // CHUNKS
        scale = float(tokens) ** (-0.5)
        weights = (gate_weight, up_weight, ("row", "col"))

        grads = [
            lax.all_gather(out_grad[q * rows : (q + 1) * rows], "col", axis=0, tiled=True)
            for q in range(CHUNKS)
        ]
        saved = jnp.stack([gate_saved, up_saved])
        saved = [saved.reshape(2, row_tokens // block, CHUNKS, rows, wide)]
        saved = gather_step(saved, 0, "row", n_row)
        first, saved = hold(hidden_grad_terms(grads[0], down_weight), saved)

        first = sum_in(first, "row", n_row)
        saved = gather_step(saved, 1, "row", n_row)
        second = hidden_grad_terms(grads[1], down_weight)
        first, second, saved = hold(first, second, saved)

        second = sum_in(second, "row", n_row)
        first = sum_swap(first, "row", n_row)
        saved = gather_step(saved, 2, "row", n_row)
        inputs = lax.all_gather(layer_input, "col", axis=0, tiled=True)
        first, second, saved, inputs = hold(first, second, saved, inputs)

        first = sum_out(first, "row", n_row)
        second = sum_swap(second, "row", n_row)
        down_weight_grad, *factors = down_weight_grads(
            saved, gather_places(n_row), grads, "row", scale
        )
        first, second, down_weight_grad, factors = hold(first, second, down_weight_grad, factors)

        second = sum_out(second, "row", n_row)
        *made, keep, send = input_grad_terms(0, first, *factors, *weights, ())
        inputs = inputs.T
        second, made, keep, send, inputs = hold(second, made, keep, send, inputs)

        early = scatter_halves(keep, send, "col", n_col)
        *made, keep, send = input_grad_terms(1, second, *factors, *weights, made)
        early, made, keep, send = hold(early, made, keep, send)
        late = scatter_halves(keep, send, "col", n_col)
        early = scatter_send(early, "col", n_col)
        late, made = hold(late, made)
        late = scatter_send(late, "col", n_col)
        made = [x.reshape(tokens, wide) for x in made]
        gate_weight_grad, up_weight_grad = projection_grads(inputs, *made, scale)
        early, late, gate_weight_grad, up_weight_grad = hold(
            early, late, gate_weight_grad, up_weight_grad
        )
        input_grad = jnp.concatenate([add_up(early), add_up(late)], axis=0)
        return input_grad, gate_weight_grad, up_weight_grad, down_weight_grad

    by_token, by_unit = P("col", "row"), P("row", "col")
    return jax.shard_map(
        shards,
        mesh=mesh,
        in_specs=(by_token, by_token, by_unit, by_unit, by_unit, by_unit, by_token),
        out_specs=(by_token, by_unit, by_unit, by_token),
        check_vma=False,
    )
```

```python
import jax
import jax.numpy as jnp
from jax import lax
from jax.experimental import pallas as pl
from jax.experimental.pallas import tpu as pltpu
from jax.sharding import PartitionSpec as P

CHUNKS = 2
VMEM = 60 * 1024 * 1024


def tile_of(size, limit):
    return max(t for t in range(128, limit + 1, 128) if size % t == 0)


def params():
    return pltpu.CompilerParams(vmem_limit_bytes=VMEM)


def cost(flops, moved):
    return pl.CostEstimate(flops=flops, bytes_accessed=moved, transcendentals=0)


def dot(left, right, dims):
    return lax.dot_general(left, right, (dims, ((), ())), preferred_element_type=jnp.float32)


def halves_of(size):
    cut = max(size // 2 // 256 * 256, 128)
    return slice(0, size - cut), slice(size - cut, size)


def sigmoid(gate):
    return 1.0 / (1.0 + jnp.exp(-gate))


def hidden_grad_terms(grad, q, down):
    cols, _, rows, depth = grad.shape

    def left_of(grad_ref):
        return grad_ref[...].reshape(cols * rows, depth)

    chunk = pl.BlockSpec((cols, None, rows, depth), lambda i: (0, q, 0, 0))
    return hidden_grad_call(left_of, [grad], [chunk], [], down)


def hidden_grad_terms_of(pieces, axis, down):
    cols = len(pieces)
    rows, depth = pieces[0].shape

    def left_of(*refs):
        whole_ref = refs[-1]

        @pl.when(pl.program_id(0) == 0)
        def _():
            here = lax.axis_index(axis)
            for k in range(cols):
                whole_ref[here ^ k] = refs[k][...]

        return whole_ref[...].reshape(cols * rows, depth)

    piece = pl.BlockSpec((rows, depth), lambda i: (0, 0))
    scratch = [pltpu.VMEM((cols, rows, depth), jnp.bfloat16)]
    return hidden_grad_call(left_of, pieces, [piece] * cols, scratch, down)


def hidden_grad_call(left_of, operands, specs, scratch, down):
    wide, depth = down.shape
    tokens = sum(x.size for x in operands) // depth
    if len(operands) == 1:
        tokens //= CHUNKS
    tile = tile_of(wide, 896)
    n = len(operands)

    def body(*refs):
        left = left_of(*refs[:n], *refs[n + 2 :])
        refs[n + 1][...] = dot(left, refs[n][...], ((1,), (1,))).astype(jnp.bfloat16)

    return pl.pallas_call(
        body,
        grid=(wide // tile,),
        in_specs=specs + [pl.BlockSpec((tile, depth), lambda i: (i, 0))],
        out_specs=pl.BlockSpec((tokens, tile), lambda i: (0, i)),
        out_shape=jax.ShapeDtypeStruct((tokens, wide), jnp.bfloat16),
        scratch_shapes=scratch,
        compiler_params=params(),
        cost_estimate=cost(2 * tokens * depth * wide, 2 * (down.size + tokens * depth)),
        name="hidden_grad_terms",
    )(*operands, down)


def down_weight_grads(saved, places, grad, axis, scale):
    _, blocks, _, _, wide = saved[0].shape
    cols, chunks, rows, depth = grad.shape
    tokens = chunks * cols * rows
    tile = tile_of(wide, 256)
    n = len(saved)

    def body(*refs):
        saved_refs = refs[:n]
        grad_ref, out_ref, by_gate_ref, by_up_ref, hidden_ref = refs[n:]
        for k, (shard, there) in enumerate(places(lax.axis_index(axis))):

            @pl.when(there)
            def _():
                gate_val = saved_refs[k][0].astype(jnp.float32)
                up_val = saved_refs[k][1].astype(jnp.float32)
                sigma = sigmoid(gate_val)
                silu = gate_val * sigma
                slope = sigma * (1.0 + gate_val * (1.0 - sigma))
                to = pl.ds(shard * blocks, blocks)
                hidden_ref[to] = (silu * up_val).astype(jnp.bfloat16)
                by_gate_ref[to] = (up_val * slope).astype(jnp.bfloat16)
                by_up_ref[to] = silu.astype(jnp.bfloat16)

        left = hidden_ref[...].reshape(tokens, tile)
        right = grad_ref[...].reshape(tokens, depth)
        out_ref[...] = scale * dot(left, right, ((0,), (0,)))

    shard = pl.BlockSpec((2, blocks, chunks, rows, tile), lambda i: (0, 0, 0, 0, i))
    factor = pl.BlockSpec((cols, chunks, rows, tile), lambda i: (0, 0, 0, i))
    factors = jax.ShapeDtypeStruct((cols, chunks, rows, wide), jnp.bfloat16)
    return pl.pallas_call(
        body,
        grid=(wide // tile,),
        in_specs=[shard] * n
        + [pl.BlockSpec((cols, chunks, rows, depth), lambda i: (0, 0, 0, 0))],
        out_specs=[pl.BlockSpec((tile, depth), lambda i: (i, 0)), factor, factor],
        out_shape=[jax.ShapeDtypeStruct((wide, depth), jnp.float32), factors, factors],
        scratch_shapes=[pltpu.VMEM((cols, chunks, rows, tile), jnp.bfloat16)],
        compiler_params=params(),
        cost_estimate=cost(2 * tokens * wide * depth, 4 * wide * depth),
        name="down_weight_grads",
    )(*saved, grad)


def input_grad_terms(q, sums, by_gate, by_up, gate_weight, up_weight, axes, made):
    cols, chunks, rows, wide = by_gate.shape
    depth = gate_weight.shape[0]
    tokens = cols * rows
    levels = len(sums)
    tile = tile_of(depth, 512)

    def body(*refs):
        sums_refs, refs = refs[:levels], refs[levels:]
        by_gate_ref, by_up_ref, gate_w_ref, up_w_ref = refs[:4]
        gate_out, up_out, keep_ref, send_ref = refs[-4:]

        @pl.when(pl.program_id(0) == 0)
        def _():
            here = lax.axis_index(axes[0])
            hidden_grad = sums_refs[0][...].astype(jnp.float32)
            for level in range(1, levels):
                at_level = (here == levels - 1 - level) | (here == levels + level)
                other = sums_refs[level][...].astype(jnp.float32)
                hidden_grad = jnp.where(at_level, other, hidden_grad)
            for by_ref, out in ((by_gate_ref, gate_out), (by_up_ref, up_out)):
                by = by_ref[...].reshape(tokens, wide).astype(jnp.float32)
                out[...] = (hidden_grad * by).astype(jnp.bfloat16).reshape(cols, rows, wide)

        odd = lax.axis_index(axes[1]) % 2 == 1
        gate_grad = gate_out[...].reshape(tokens, wide)
        up_grad = up_out[...].reshape(tokens, wide)
        for part in halves_of(tile):
            res = dot(gate_grad, gate_w_ref[part], ((1,), (1,)))
            res += dot(up_grad, up_w_ref[part], ((1,), (1,)))
            res = res.astype(jnp.bfloat16).reshape(cols // 2, 2, rows, part.stop - part.start)
            keep_ref[:, :, part] = jnp.where(odd, res[:, 1], res[:, 0])
            send_ref[:, :, part] = jnp.where(odd, res[:, 0], res[:, 1])

    into = pl.BlockSpec((cols, None, rows, wide), lambda i: (0, q, 0, 0))
    weight = pl.BlockSpec((tile, wide), lambda i: (i, 0))
    half = pl.BlockSpec((cols // 2, rows, tile), lambda i: (0, 0, i))
    halves = jax.ShapeDtypeStruct((cols // 2, rows, depth), jnp.bfloat16)
    whole = jax.ShapeDtypeStruct((cols, chunks, rows, wide), jnp.bfloat16)
    return pl.pallas_call(
        body,
        grid=(depth // tile,),
        in_specs=[pl.BlockSpec((tokens, wide), lambda i: (0, 0))] * levels
        + [into, into, weight, weight]
        + [pl.BlockSpec(memory_space=pl.ANY)] * len(made),
        out_specs=[into, into, half, half],
        out_shape=[whole, whole, halves, halves],
        input_output_aliases={levels + 4 + j: j for j in range(len(made))},
        compiler_params=params(),
        cost_estimate=cost(4 * tokens * wide * depth, 4 * wide * depth),
        name="input_grad_terms",
    )(*sums, by_gate, by_up, gate_weight, up_weight, *made)


def projection_grads(inputs, gate_grad, up_grad, scale):
    depth, tokens = inputs.shape
    wide = gate_grad.shape[1]
    tile = tile_of(depth, 256)

    def body(inputs_ref, gate_ref, up_ref, gate_out, up_out):
        left = inputs_ref[...]
        gate_out[...] = scale * dot(left, gate_ref[...], ((1,), (0,)))
        up_out[...] = scale * dot(left, up_ref[...], ((1,), (0,)))

    once = pl.BlockSpec((tokens, wide), lambda i: (0, 0))
    out = pl.BlockSpec((tile, wide), lambda i: (i, 0))
    return pl.pallas_call(
        body,
        grid=(depth // tile,),
        in_specs=[pl.BlockSpec((tile, tokens), lambda i: (i, 0)), once, once],
        out_specs=[out, out],
        out_shape=[jax.ShapeDtypeStruct((depth, wide), jnp.float32)] * 2,
        compiler_params=params(),
        cost_estimate=cost(4 * tokens * wide * depth, 8 * wide * depth),
        name="projection_grads",
    )(inputs, gate_grad, up_grad)


def gather_places(size):
    def places(here):
        if size != 4:
            return [(here ^ k, True) for k in range(size)]
        outer = (here == 0) | (here == 3)
        inner = jnp.logical_not(outer)
        return [
            (here, True),
            (here ^ 1, True),
            (here ^ 3, inner),
            (here ^ 2, inner),
            (here ^ 2, outer),
            (here ^ 3, outer),
        ]

    return places


def gather_step(found, step, axis, size):
    inner, outward = [(1, 2), (2, 1)], [(2, 3), (1, 0)]
    if size != 4:
        near = range(1, size) if step == 0 else ()
        new = [(0, [(i, i ^ k) for i in range(size)]) for k in near]
    else:
        swap = [(i, i ^ 1) for i in range(size)]
        new = [[(0, swap), (0, inner)], [(1, inner), (2, outward)], [(3, outward)]][step]
    return found + [lax.ppermute(found[k], axis, pairs) for k, pairs in new]


def both(left, right):
    return (left.astype(jnp.float32) + right.astype(jnp.float32)).astype(jnp.bfloat16)


def sum_in(term, axis, size):
    total = term
    for k in range(size // 2 - 1):
        got = lax.ppermute(total, axis, [(k, k + 1), (size - 1 - k, size - 2 - k)])
        total = both(term, got)
    return total


def sum_swap(total, axis, size):
    half = size // 2
    return both(total, lax.ppermute(total, axis, [(half - 1, half), (half, half - 1)]))


def sum_out(total, axis, size):
    found = [total]
    for k in reversed(range(size // 2 - 1)):
        found.append(lax.ppermute(found[-1], axis, [(k + 1, k), (size - 2 - k, size - 1 - k)]))
    return found


def scatter_halves(keep, send, axis, size):
    return both(keep, lax.ppermute(send, axis, [(i, i ^ 1) for i in range(size)]))


def scatter_sum(halves, axis, size):
    here = lax.axis_index(axis)

    def block(k):
        at = (here // 2) ^ k
        return jnp.concatenate(
            [lax.dynamic_index_in_dim(x, at, 0, keepdims=False) for x in halves], axis=0
        )

    total = block(0).astype(jnp.float32)
    for k in range(1, size // 2):
        got = lax.ppermute(block(k), axis, [(i, i ^ (2 * k)) for i in range(size)])
        total += got.astype(jnp.float32)
    return total.astype(jnp.bfloat16)


def hold(*values):
    return lax.optimization_barrier(values)


def solution(mesh):
    n_row, n_col = mesh.shape["row"], mesh.shape["col"]

    def shards(layer_input, out_grad, gate_saved, up_saved, gate_weight, up_weight, down_weight):
        block, depth = layer_input.shape
        row_tokens, wide = gate_saved.shape
        tokens = block * n_col
        rows = block // CHUNKS
        scale = float(tokens) ** (-0.5)
        weights = (gate_weight, up_weight, ("row", "col"))

        grad = lax.all_gather(out_grad, "col", axis=0, tiled=True)
        grad = grad.reshape(n_col, CHUNKS, rows, depth)
        saved = jnp.stack([gate_saved, up_saved])
        saved = [saved.reshape(2, row_tokens // block, CHUNKS, rows, wide)]
        saved = gather_step(saved, 0, "row", n_row)
        own = out_grad[:rows]
        pieces = [own] + [
            lax.ppermute(own, "col", [(i, i ^ k) for i in range(n_col)]) for k in range(1, n_col)
        ]
        first, saved = hold(hidden_grad_terms_of(pieces, "col", down_weight), saved)

        first = sum_in(first, "row", n_row)
        saved = gather_step(saved, 1, "row", n_row)
        second = hidden_grad_terms(grad, 1, down_weight)
        first, second, saved = hold(first, second, saved)

        second = sum_in(second, "row", n_row)
        first = sum_swap(first, "row", n_row)
        saved = gather_step(saved, 2, "row", n_row)
        inputs = lax.all_gather(layer_input, "col", axis=0, tiled=True)
        first, second, inputs = hold(first, second, inputs)

        first = sum_out(first, "row", n_row)
        second = sum_swap(second, "row", n_row)
        down_weight_grad, *factors = down_weight_grads(
            saved, gather_places(n_row), grad, "row", scale
        )
        inputs = inputs.T
        first, second, down_weight_grad, factors, inputs = hold(
            first, second, down_weight_grad, factors, inputs
        )

        second = sum_out(second, "row", n_row)
        *made, keep, send = input_grad_terms(0, first, *factors, *weights, ())
        second, made, keep, send = hold(second, made, keep, send)

        early = scatter_halves(keep, send, "col", n_col)
        *made, keep, send = input_grad_terms(1, second, *factors, *weights, made)
        early, made, keep, send = hold(early, made, keep, send)
        late = scatter_halves(keep, send, "col", n_col)
        late, made = hold(late, made)
        input_grad = scatter_sum([early, late], "col", n_col)
        made = [x.reshape(tokens, wide) for x in made]
        gate_weight_grad, up_weight_grad = projection_grads(inputs, *made, scale)
        return input_grad, gate_weight_grad, up_weight_grad, down_weight_grad

    by_token, by_unit = P("col", "row"), P("row", "col")
    return jax.shard_map(
        shards,
        mesh=mesh,
        in_specs=(by_token, by_token, by_unit, by_unit, by_unit, by_unit, by_token),
        out_specs=(by_token, by_unit, by_unit, by_token),
        check_vma=False,
    )
```

```python
import jax
import jax.numpy as jnp
from jax import lax
from jax.experimental import pallas as pl
from jax.experimental.pallas import tpu as pltpu
from jax.sharding import PartitionSpec as P

CHUNKS = 2
VMEM = 60 * 1024 * 1024


def tile_of(size, limit):
    return max(t for t in range(128, limit + 1, 128) if size % t == 0)


def params():
    return pltpu.CompilerParams(vmem_limit_bytes=VMEM)


def cost(flops, moved):
    return pl.CostEstimate(flops=flops, bytes_accessed=moved, transcendentals=0)


def dot(left, right, dims):
    return lax.dot_general(left, right, (dims, ((), ())), preferred_element_type=jnp.float32)


def halves_of(size):
    cut = max(size // 2 // 256 * 256, 128)
    return slice(0, size - cut), slice(size - cut, size)


def sigmoid(gate):
    return 1.0 / (1.0 + jnp.exp(-gate))


def hidden_grad_terms(q, pieces, others, axis, down):
    half = len(pieces)
    _, rows, depth = pieces[0].shape
    wide = down.shape[0]
    tokens = 2 * half * rows
    tile = tile_of(wide, 896)

    def body(*refs):
        down_ref, out_ref, grad_ref = refs[2 * half :]

        @pl.when(pl.program_id(0) == 0)
        def _():
            here = lax.axis_index(axis)
            for k in range(half):
                grad_ref[here ^ (2 * k)] = refs[k][...]
                grad_ref[here ^ (2 * k + 1)] = refs[half + k][...]

        left = grad_ref[...].reshape(tokens, depth)
        out_ref[...] = dot(left, down_ref[...], ((1,), (1,))).astype(jnp.bfloat16)

    return pl.pallas_call(
        body,
        grid=(wide // tile,),
        in_specs=[pl.BlockSpec((None, rows, depth), lambda i: (q, 0, 0))] * (2 * half)
        + [pl.BlockSpec((tile, depth), lambda i: (i, 0))],
        out_specs=pl.BlockSpec((tokens, tile), lambda i: (0, i)),
        out_shape=jax.ShapeDtypeStruct((tokens, wide), jnp.bfloat16),
        scratch_shapes=[pltpu.VMEM((2 * half, rows, depth), jnp.bfloat16)],
        compiler_params=params(),
        cost_estimate=cost(2 * tokens * depth * wide, 2 * (down.size + tokens * depth)),
        name="hidden_grad_terms",
    )(*pieces, *others, down)


def down_weight_grads(saved, places, grad, axis, scale):
    _, blocks, _, _, wide = saved[0].shape
    cols, chunks, rows, depth = grad.shape
    tokens = chunks * cols * rows
    tile = tile_of(wide, 256)
    n = len(saved)

    def body(*refs):
        saved_refs = refs[:n]
        grad_ref, out_ref, by_gate_ref, by_up_ref, hidden_ref = refs[n:]
        for k, (shard, there) in enumerate(places(lax.axis_index(axis))):

            @pl.when(there)
            def _():
                gate_val = saved_refs[k][0].astype(jnp.float32)
                up_val = saved_refs[k][1].astype(jnp.float32)
                sigma = sigmoid(gate_val)
                silu = gate_val * sigma
                slope = sigma * (1.0 + gate_val * (1.0 - sigma))
                to = pl.ds(shard * blocks, blocks)
                hidden_ref[to] = (silu * up_val).astype(jnp.bfloat16)
                by_gate_ref[to] = (up_val * slope).astype(jnp.bfloat16)
                by_up_ref[to] = silu.astype(jnp.bfloat16)

        left = hidden_ref[...].reshape(tokens, tile)
        right = grad_ref[...].reshape(tokens, depth)
        out_ref[...] = scale * dot(left, right, ((0,), (0,)))

    shard = pl.BlockSpec((2, blocks, chunks, rows, tile), lambda i: (0, 0, 0, 0, i))
    factor = pl.BlockSpec((cols, chunks, rows, tile), lambda i: (0, 0, 0, i))
    factors = jax.ShapeDtypeStruct((cols, chunks, rows, wide), jnp.bfloat16)
    return pl.pallas_call(
        body,
        grid=(wide // tile,),
        in_specs=[shard] * n
        + [pl.BlockSpec((cols, chunks, rows, depth), lambda i: (0, 0, 0, 0))],
        out_specs=[pl.BlockSpec((tile, depth), lambda i: (i, 0)), factor, factor],
        out_shape=[jax.ShapeDtypeStruct((wide, depth), jnp.float32), factors, factors],
        scratch_shapes=[pltpu.VMEM((cols, chunks, rows, tile), jnp.bfloat16)],
        compiler_params=params(),
        cost_estimate=cost(2 * tokens * wide * depth, 4 * wide * depth),
        name="down_weight_grads",
    )(*saved, grad)


def input_grad_terms(q, sums, by_gate, by_up, gate_weight, up_weight, axes, made):
    cols, chunks, rows, wide = by_gate.shape
    depth = gate_weight.shape[0]
    tokens = cols * rows
    levels = len(sums)
    tile = tile_of(depth, 512)

    def body(*refs):
        sums_refs, refs = refs[:levels], refs[levels:]
        by_gate_ref, by_up_ref, gate_w_ref, up_w_ref = refs[:4]
        gate_out, up_out, keep_ref, send_ref = refs[-4:]

        @pl.when(pl.program_id(0) == 0)
        def _():
            here = lax.axis_index(axes[0])
            hidden_grad = sums_refs[0][...].astype(jnp.float32)
            for level in range(1, levels):
                at_level = (here == levels - 1 - level) | (here == levels + level)
                other = sums_refs[level][...].astype(jnp.float32)
                hidden_grad = jnp.where(at_level, other, hidden_grad)
            for by_ref, out in ((by_gate_ref, gate_out), (by_up_ref, up_out)):
                by = by_ref[...].reshape(tokens, wide).astype(jnp.float32)
                out[...] = (hidden_grad * by).astype(jnp.bfloat16).reshape(cols, rows, wide)

        odd = lax.axis_index(axes[1]) % 2 == 1
        gate_grad = gate_out[...].reshape(tokens, wide)
        up_grad = up_out[...].reshape(tokens, wide)
        for part in halves_of(tile):
            res = dot(gate_grad, gate_w_ref[part], ((1,), (1,)))
            res += dot(up_grad, up_w_ref[part], ((1,), (1,)))
            res = res.astype(jnp.bfloat16).reshape(cols // 2, 2, rows, part.stop - part.start)
            keep_ref[:, :, part] = jnp.where(odd, res[:, 1], res[:, 0])
            send_ref[:, :, part] = jnp.where(odd, res[:, 0], res[:, 1])

    into = pl.BlockSpec((cols, None, rows, wide), lambda i: (0, q, 0, 0))
    weight = pl.BlockSpec((tile, wide), lambda i: (i, 0))
    half = pl.BlockSpec((cols // 2, rows, tile), lambda i: (0, 0, i))
    halves = jax.ShapeDtypeStruct((cols // 2, rows, depth), jnp.bfloat16)
    whole = jax.ShapeDtypeStruct((cols, chunks, rows, wide), jnp.bfloat16)
    return pl.pallas_call(
        body,
        grid=(depth // tile,),
        in_specs=[pl.BlockSpec((tokens, wide), lambda i: (0, 0))] * levels
        + [into, into, weight, weight]
        + [pl.BlockSpec(memory_space=pl.ANY)] * len(made),
        out_specs=[into, into, half, half],
        out_shape=[whole, whole, halves, halves],
        input_output_aliases={levels + 4 + j: j for j in range(len(made))},
        compiler_params=params(),
        cost_estimate=cost(4 * tokens * wide * depth, 4 * wide * depth),
        name="input_grad_terms",
    )(*sums, by_gate, by_up, gate_weight, up_weight, *made)


def projection_grads(inputs, gate_grad, up_grad, scale):
    depth, tokens = inputs.shape
    wide = gate_grad.shape[1]
    tile = tile_of(depth, 256)

    def body(inputs_ref, gate_ref, up_ref, gate_out, up_out):
        left = inputs_ref[...]
        gate_out[...] = scale * dot(left, gate_ref[...], ((1,), (0,)))
        up_out[...] = scale * dot(left, up_ref[...], ((1,), (0,)))

    once = pl.BlockSpec((tokens, wide), lambda i: (0, 0))
    out = pl.BlockSpec((tile, wide), lambda i: (i, 0))
    return pl.pallas_call(
        body,
        grid=(depth // tile,),
        in_specs=[pl.BlockSpec((tile, tokens), lambda i: (i, 0)), once, once],
        out_specs=[out, out],
        out_shape=[jax.ShapeDtypeStruct((depth, wide), jnp.float32)] * 2,
        compiler_params=params(),
        cost_estimate=cost(4 * tokens * wide * depth, 8 * wide * depth),
        name="projection_grads",
    )(inputs, gate_grad, up_grad)


def gather_places(size):
    def places(here):
        if size != 4:
            return [(here ^ k, True) for k in range(size)]
        outer = (here == 0) | (here == 3)
        inner = jnp.logical_not(outer)
        return [
            (here, True),
            (here ^ 1, True),
            (here ^ 3, inner),
            (here ^ 2, inner),
            (here ^ 2, outer),
            (here ^ 3, outer),
        ]

    return places


def gather_step(found, step, axis, size):
    inner, outward = [(1, 2), (2, 1)], [(2, 3), (1, 0)]
    if size != 4:
        near = range(1, size) if step == 0 else ()
        new = [(0, [(i, i ^ k) for i in range(size)]) for k in near]
    else:
        swap = [(i, i ^ 1) for i in range(size)]
        new = [[(0, swap), (0, inner)], [(1, inner), (2, outward)], [(3, outward)]][step]
    return found + [lax.ppermute(found[k], axis, pairs) for k, pairs in new]


def both(left, right):
    return (left.astype(jnp.float32) + right.astype(jnp.float32)).astype(jnp.bfloat16)


def sum_in(term, axis, size):
    total = term
    for k in range(size // 2 - 1):
        got = lax.ppermute(total, axis, [(k, k + 1), (size - 1 - k, size - 2 - k)])
        total = both(term, got)
    return total


def sum_swap(total, axis, size):
    half = size // 2
    return both(total, lax.ppermute(total, axis, [(half - 1, half), (half, half - 1)]))


def sum_out(total, axis, size):
    found = [total]
    for k in reversed(range(size // 2 - 1)):
        found.append(lax.ppermute(found[-1], axis, [(k + 1, k), (size - 2 - k, size - 1 - k)]))
    return found


def scatter_halves(keep, send, axis, size):
    return both(keep, lax.ppermute(send, axis, [(i, i ^ 1) for i in range(size)]))


def scatter_sum(halves, axis, size):
    here = lax.axis_index(axis)

    def block(k):
        at = (here // 2) ^ k
        return jnp.concatenate(
            [lax.dynamic_index_in_dim(x, at, 0, keepdims=False) for x in halves], axis=0
        )

    total = block(0).astype(jnp.float32)
    for k in range(1, size // 2):
        got = lax.ppermute(block(k), axis, [(i, i ^ (2 * k)) for i in range(size)])
        total += got.astype(jnp.float32)
    return total.astype(jnp.bfloat16)


def hold(*values):
    return lax.optimization_barrier(values)


def solution(mesh):
    n_row, n_col = mesh.shape["row"], mesh.shape["col"]

    def shards(layer_input, out_grad, gate_saved, up_saved, gate_weight, up_weight, down_weight):
        block, depth = layer_input.shape
        row_tokens, wide = gate_saved.shape
        tokens = block * n_col
        rows = block // CHUNKS
        scale = float(tokens) ** (-0.5)
        weights = (gate_weight, up_weight, ("row", "col"))

        saved = jnp.stack([gate_saved, up_saved])
        saved = [saved.reshape(2, row_tokens // block, CHUNKS, rows, wide)]
        saved = gather_step(saved, 0, "row", n_row)
        own = out_grad.reshape(CHUNKS, rows, depth)
        pieces = [own] + [
            lax.ppermute(own, "col", [(i, i ^ (2 * k)) for i in range(n_col)])
            for k in range(1, n_col // 2)
        ]
        pieces, out_grad, layer_input = hold(pieces, out_grad, layer_input)
        others = [lax.ppermute(x, "col", [(i, i ^ 1) for i in range(n_col)]) for x in pieces]
        grad = lax.all_gather(out_grad, "col", axis=0, tiled=True)
        inputs = lax.all_gather(layer_input, "col", axis=0, tiled=True)
        first = hidden_grad_terms(0, pieces, others, "col", down_weight)
        first, saved, pieces, others = hold(first, saved, pieces, others)

        first = sum_in(first, "row", n_row)
        saved = gather_step(saved, 1, "row", n_row)
        second = hidden_grad_terms(1, pieces, others, "col", down_weight)
        first, second, saved = hold(first, second, saved)

        second = sum_in(second, "row", n_row)
        first = sum_swap(first, "row", n_row)
        saved = gather_step(saved, 2, "row", n_row)
        first, second, grad = hold(first, second, grad)

        first = sum_out(first, "row", n_row)
        second = sum_swap(second, "row", n_row)
        grad = grad.reshape(n_col, CHUNKS, rows, depth)
        down_weight_grad, *factors = down_weight_grads(
            saved, gather_places(n_row), grad, "row", scale
        )
        first, second, down_weight_grad, factors, inputs = hold(
            first, second, down_weight_grad, factors, inputs
        )

        second = sum_out(second, "row", n_row)
        *made, keep, send = input_grad_terms(0, first, *factors, *weights, ())
        inputs = inputs.T
        second, made, keep, send, inputs = hold(second, made, keep, send, inputs)

        early = scatter_halves(keep, send, "col", n_col)
        *made, keep, send = input_grad_terms(1, second, *factors, *weights, made)
        early, made, keep, send = hold(early, made, keep, send)
        late = scatter_halves(keep, send, "col", n_col)
        late, made = hold(late, made)
        input_grad = scatter_sum([early, late], "col", n_col)
        made = [x.reshape(tokens, wide) for x in made]
        gate_weight_grad, up_weight_grad = projection_grads(inputs, *made, scale)
        return input_grad, gate_weight_grad, up_weight_grad, down_weight_grad

    by_token, by_unit = P("col", "row"), P("row", "col")
    return jax.shard_map(
        shards,
        mesh=mesh,
        in_specs=(by_token, by_token, by_unit, by_unit, by_unit, by_unit, by_token),
        out_specs=(by_token, by_unit, by_unit, by_token),
        check_vma=False,
    )
```

```python
import jax
import jax.numpy as jnp
from jax import lax
from jax.experimental import pallas as pl
from jax.experimental.pallas import tpu as pltpu
from jax.sharding import PartitionSpec as P

CHUNKS = 2
VMEM = 32 * 1024 * 1024


def tile_of(size, limit):
    return max(t for t in range(128, limit + 1, 128) if size % t == 0)


def params():
    return pltpu.CompilerParams(vmem_limit_bytes=VMEM)


def cost(flops, moved):
    return pl.CostEstimate(flops=flops, bytes_accessed=moved, transcendentals=0)


def dot(left, right, dims):
    return lax.dot_general(left, right, (dims, ((), ())), preferred_element_type=jnp.float32)


def halves_of(size):
    cut = max(size // 2 // 256 * 256, 128)
    return slice(0, size - cut), slice(size - cut, size)


def sigmoid(gate):
    return 1.0 / (1.0 + jnp.exp(-gate))


def hidden_grad_terms(q, pieces, others, axis, down):
    half = len(pieces)
    _, rows, depth = pieces[0].shape
    wide = down.shape[0]
    tokens = 2 * half * rows
    tile = tile_of(wide, 896)

    def body(*refs):
        down_ref, out_ref, grad_ref = refs[2 * half :]

        @pl.when(pl.program_id(0) == 0)
        def _():
            here = lax.axis_index(axis)
            for k in range(half):
                grad_ref[here ^ (2 * k)] = refs[k][...]
                grad_ref[here ^ (2 * k + 1)] = refs[half + k][...]

        left = grad_ref[...].reshape(tokens, depth)
        out_ref[...] = dot(left, down_ref[...], ((1,), (1,))).astype(jnp.bfloat16)

    return pl.pallas_call(
        body,
        grid=(wide // tile,),
        in_specs=[pl.BlockSpec((None, rows, depth), lambda i: (q, 0, 0))] * (2 * half)
        + [pl.BlockSpec((tile, depth), lambda i: (i, 0))],
        out_specs=pl.BlockSpec((tokens, tile), lambda i: (0, i)),
        out_shape=jax.ShapeDtypeStruct((tokens, wide), jnp.bfloat16),
        scratch_shapes=[pltpu.VMEM((2 * half, rows, depth), jnp.bfloat16)],
        compiler_params=params(),
        cost_estimate=cost(1, 1),
        name="hidden_grad_terms",
    )(*pieces, *others, down)


def down_weight_grads(saved, places, grad, axis, scale):
    _, blocks, _, _, wide = saved[0].shape
    cols, chunks, rows, depth = grad.shape
    tokens = chunks * cols * rows
    tile = tile_of(wide, 256)
    n = len(saved)

    def body(*refs):
        saved_refs = refs[:n]
        grad_ref, out_ref, by_gate_ref, by_up_ref, hidden_ref = refs[n:]
        for k, (shard, there) in enumerate(places(lax.axis_index(axis))):

            @pl.when(there)
            def _():
                gate_val = saved_refs[k][0].astype(jnp.float32)
                up_val = saved_refs[k][1].astype(jnp.float32)
                sigma = sigmoid(gate_val)
                silu = gate_val * sigma
                slope = sigma * (1.0 + gate_val * (1.0 - sigma))
                to = pl.ds(shard * blocks, blocks)
                hidden_ref[to] = (silu * up_val).astype(jnp.bfloat16)
                by_gate_ref[to] = (up_val * slope).astype(jnp.bfloat16)
                by_up_ref[to] = silu.astype(jnp.bfloat16)

        left = hidden_ref[...].reshape(tokens, tile)
        right = grad_ref[...].reshape(tokens, depth)
        out_ref[...] = scale * dot(left, right, ((0,), (0,)))

    shard = pl.BlockSpec((2, blocks, chunks, rows, tile), lambda i: (0, 0, 0, 0, i))
    factor = pl.BlockSpec((cols, chunks, rows, tile), lambda i: (0, 0, 0, i))
    factors = jax.ShapeDtypeStruct((cols, chunks, rows, wide), jnp.bfloat16)
    return pl.pallas_call(
        body,
        grid=(wide // tile,),
        in_specs=[shard] * n
        + [pl.BlockSpec((cols, chunks, rows, depth), lambda i: (0, 0, 0, 0))],
        out_specs=[pl.BlockSpec((tile, depth), lambda i: (i, 0)), factor, factor],
        out_shape=[jax.ShapeDtypeStruct((wide, depth), jnp.float32), factors, factors],
        scratch_shapes=[pltpu.VMEM((cols, chunks, rows, tile), jnp.bfloat16)],
        compiler_params=params(),
        cost_estimate=cost(2 * tokens * wide * depth, 4 * wide * depth),
        name="down_weight_grads",
    )(*saved, grad)


def input_grad_terms(q, sums, by_gate, by_up, gate_weight, up_weight, axes, made):
    cols, chunks, rows, wide = by_gate.shape
    depth = gate_weight.shape[0]
    tokens = cols * rows
    levels = len(sums)
    tile = tile_of(depth, 512)

    def body(*refs):
        sums_refs, refs = refs[:levels], refs[levels:]
        by_gate_ref, by_up_ref, gate_w_ref, up_w_ref = refs[:4]
        gate_out, up_out, keep_ref, send_ref = refs[-4:]

        @pl.when(pl.program_id(0) == 0)
        def _():
            here = lax.axis_index(axes[0])
            hidden_grad = sums_refs[0][...].astype(jnp.float32)
            for level in range(1, levels):
                at_level = (here == levels - 1 - level) | (here == levels + level)
                other = sums_refs[level][...].astype(jnp.float32)
                hidden_grad = jnp.where(at_level, other, hidden_grad)
            for by_ref, out in ((by_gate_ref, gate_out), (by_up_ref, up_out)):
                by = by_ref[...].reshape(tokens, wide).astype(jnp.float32)
                out[...] = (hidden_grad * by).astype(jnp.bfloat16).reshape(cols, rows, wide)

        odd = lax.axis_index(axes[1]) % 2 == 1
        gate_grad = gate_out[...].reshape(tokens, wide)
        up_grad = up_out[...].reshape(tokens, wide)
        for part in halves_of(tile):
            res = dot(gate_grad, gate_w_ref[part], ((1,), (1,)))
            res += dot(up_grad, up_w_ref[part], ((1,), (1,)))
            res = res.astype(jnp.bfloat16).reshape(cols // 2, 2, rows, part.stop - part.start)
            keep_ref[:, :, part] = jnp.where(odd, res[:, 1], res[:, 0])
            send_ref[:, :, part] = jnp.where(odd, res[:, 0], res[:, 1])

    into = pl.BlockSpec((cols, None, rows, wide), lambda i: (0, q, 0, 0))
    weight = pl.BlockSpec((tile, wide), lambda i: (i, 0))
    half = pl.BlockSpec((cols // 2, rows, tile), lambda i: (0, 0, i))
    halves = jax.ShapeDtypeStruct((cols // 2, rows, depth), jnp.bfloat16)
    whole = jax.ShapeDtypeStruct((cols, chunks, rows, wide), jnp.bfloat16)
    return pl.pallas_call(
        body,
        grid=(depth // tile,),
        in_specs=[pl.BlockSpec((tokens, wide), lambda i: (0, 0))] * levels
        + [into, into, weight, weight]
        + [pl.BlockSpec(memory_space=pl.ANY)] * len(made),
        out_specs=[into, into, half, half],
        out_shape=[whole, whole, halves, halves],
        input_output_aliases={levels + 4 + j: j for j in range(len(made))},
        compiler_params=params(),
        cost_estimate=cost(4 * tokens * wide * depth, 4 * wide * depth),
        name="input_grad_terms",
    )(*sums, by_gate, by_up, gate_weight, up_weight, *made)


def projection_grads(inputs, gate_grad, up_grad, scale):
    depth, tokens = inputs.shape
    wide = gate_grad.shape[1]
    tile = tile_of(depth, 256)

    def body(inputs_ref, gate_ref, up_ref, gate_out, up_out):
        left = inputs_ref[...]
        gate_out[...] = scale * dot(left, gate_ref[...], ((1,), (0,)))
        up_out[...] = scale * dot(left, up_ref[...], ((1,), (0,)))

    once = pl.BlockSpec((tokens, wide), lambda i: (0, 0))
    out = pl.BlockSpec((tile, wide), lambda i: (i, 0))
    return pl.pallas_call(
        body,
        grid=(depth // tile,),
        in_specs=[pl.BlockSpec((tile, tokens), lambda i: (i, 0)), once, once],
        out_specs=[out, out],
        out_shape=[jax.ShapeDtypeStruct((depth, wide), jnp.float32)] * 2,
        compiler_params=params(),
        cost_estimate=cost(4 * tokens * wide * depth, 8 * wide * depth),
        name="projection_grads",
    )(inputs, gate_grad, up_grad)


def gather_places(size):
    def places(here):
        if size != 4:
            return [(here ^ k, True) for k in range(size)]
        outer = (here == 0) | (here == 3)
        inner = jnp.logical_not(outer)
        return [
            (here, True),
            (here ^ 1, True),
            (here ^ 3, inner),
            (here ^ 2, inner),
            (here ^ 2, outer),
            (here ^ 3, outer),
        ]

    return places


def gather_step(found, step, axis, size):
    inner, outward = [(1, 2), (2, 1)], [(2, 3), (1, 0)]
    if size != 4:
        near = range(1, size) if step == 0 else ()
        new = [(0, [(i, i ^ k) for i in range(size)]) for k in near]
    else:
        swap = [(i, i ^ 1) for i in range(size)]
        new = [[(0, swap), (0, inner)], [(1, inner), (2, outward)], [(3, outward)]][step]
    return found + [lax.ppermute(found[k], axis, pairs) for k, pairs in new]


def both(left, right):
    return (left.astype(jnp.float32) + right.astype(jnp.float32)).astype(jnp.bfloat16)


def sum_in(term, axis, size):
    total = term
    for k in range(size // 2 - 1):
        got = lax.ppermute(total, axis, [(k, k + 1), (size - 1 - k, size - 2 - k)])
        total = both(term, got)
    return total


def sum_swap(total, axis, size):
    half = size // 2
    return both(total, lax.ppermute(total, axis, [(half - 1, half), (half, half - 1)]))


def sum_out(total, axis, size):
    found = [total]
    for k in reversed(range(size // 2 - 1)):
        found.append(lax.ppermute(found[-1], axis, [(k + 1, k), (size - 2 - k, size - 1 - k)]))
    return found


def scatter_halves(keep, send, axis, size):
    return both(keep, lax.ppermute(send, axis, [(i, i ^ 1) for i in range(size)]))


def scatter_sum(halves, axis, size):
    here = lax.axis_index(axis)

    def block(k):
        at = (here // 2) ^ k
        return jnp.concatenate(
            [lax.dynamic_index_in_dim(x, at, 0, keepdims=False) for x in halves], axis=0
        )

    total = block(0).astype(jnp.float32)
    for k in range(1, size // 2):
        got = lax.ppermute(block(k), axis, [(i, i ^ (2 * k)) for i in range(size)])
        total += got.astype(jnp.float32)
    return total.astype(jnp.bfloat16)


def hold(*values):
    return lax.optimization_barrier(values)


def solution(mesh):
    n_row, n_col = mesh.shape["row"], mesh.shape["col"]

    def shards(layer_input, out_grad, gate_saved, up_saved, gate_weight, up_weight, down_weight):
        block, depth = layer_input.shape
        row_tokens, wide = gate_saved.shape
        tokens = block * n_col
        rows = block // CHUNKS
        scale = float(tokens) ** (-0.5)
        weights = (gate_weight, up_weight, ("row", "col"))

        saved = jnp.stack([gate_saved, up_saved])
        saved = [saved.reshape(2, row_tokens // block, CHUNKS, rows, wide)]
        saved = gather_step(saved, 0, "row", n_row)
        own = out_grad.reshape(CHUNKS, rows, depth)
        pieces = [own] + [
            lax.ppermute(own, "col", [(i, i ^ (2 * k)) for i in range(n_col)])
            for k in range(1, n_col // 2)
        ]
        pieces, out_grad, layer_input = hold(pieces, out_grad, layer_input)
        others = [lax.ppermute(x, "col", [(i, i ^ 1) for i in range(n_col)]) for x in pieces]
        grad = lax.all_gather(out_grad, "col", axis=0, tiled=True)
        inputs = lax.all_gather(layer_input, "col", axis=0, tiled=True)
        first = hidden_grad_terms(0, pieces, others, "col", down_weight)
        first, saved, pieces, others = hold(first, saved, pieces, others)

        first = sum_in(first, "row", n_row)
        saved = gather_step(saved, 1, "row", n_row)
        second = hidden_grad_terms(1, pieces, others, "col", down_weight)
        first, second, saved = hold(first, second, saved)

        second = sum_in(second, "row", n_row)
        first = sum_swap(first, "row", n_row)
        saved = gather_step(saved, 2, "row", n_row)
        first, second, grad = hold(first, second, grad)

        first = sum_out(first, "row", n_row)
        second = sum_swap(second, "row", n_row)
        grad = grad.reshape(n_col, CHUNKS, rows, depth)
        down_weight_grad, *factors = down_weight_grads(
            saved, gather_places(n_row), grad, "row", scale
        )
        first, second, down_weight_grad, factors, inputs = hold(
            first, second, down_weight_grad, factors, inputs
        )

        second = sum_out(second, "row", n_row)
        *made, keep, send = input_grad_terms(0, first, *factors, *weights, ())
        inputs = inputs.T
        second, made, keep, send, inputs = hold(second, made, keep, send, inputs)

        early = scatter_halves(keep, send, "col", n_col)
        *made, keep, send = input_grad_terms(1, second, *factors, *weights, made)
        early, made, keep, send = hold(early, made, keep, send)
        late = scatter_halves(keep, send, "col", n_col)
        late, made = hold(late, made)
        input_grad = scatter_sum([early, late], "col", n_col)
        made = [x.reshape(tokens, wide) for x in made]
        gate_weight_grad, up_weight_grad = projection_grads(inputs, *made, scale)
        return input_grad, gate_weight_grad, up_weight_grad, down_weight_grad

    by_token, by_unit = P("col", "row"), P("row", "col")
    return jax.shard_map(
        shards,
        mesh=mesh,
        in_specs=(by_token, by_token, by_unit, by_unit, by_unit, by_unit, by_token),
        out_specs=(by_token, by_unit, by_unit, by_token),
        check_vma=False,
    )
```

```python
import jax
import jax.numpy as jnp
from jax import lax
from jax.experimental import pallas as pl
from jax.experimental.pallas import tpu as pltpu
from jax.sharding import PartitionSpec as P

CHUNKS = 2
VMEM = 60 * 1024 * 1024


def tile_of(size, limit):
    return max(t for t in range(128, limit + 1, 128) if size % t == 0)


def params():
    return pltpu.CompilerParams(vmem_limit_bytes=VMEM)


def cost(flops, moved):
    return pl.CostEstimate(flops=flops, bytes_accessed=moved, transcendentals=0)


def dot(left, right, dims):
    return lax.dot_general(left, right, (dims, ((), ())), preferred_element_type=jnp.float32)


def halves_of(size):
    cut = max(size // 2 // 256 * 256, 128)
    return slice(0, size - cut), slice(size - cut, size)


def sigmoid(gate):
    return 1.0 / (1.0 + jnp.exp(-gate))


def hidden_grad_terms(q, pieces, others, axis, down):
    half = len(pieces)
    _, rows, depth = pieces[0].shape
    wide = down.shape[0]
    tokens = 2 * half * rows
    tile = tile_of(wide, 896)

    def body(*refs):
        down_ref, out_ref, grad_ref = refs[2 * half :]

        @pl.when(pl.program_id(0) == 0)
        def _():
            here = lax.axis_index(axis)
            for k in range(half):
                grad_ref[here ^ (2 * k)] = refs[k][...]
                grad_ref[here ^ (2 * k + 1)] = refs[half + k][...]

        left = grad_ref[...].reshape(tokens, depth)
        out_ref[...] = dot(left, down_ref[...], ((1,), (1,))).astype(jnp.bfloat16)

    return pl.pallas_call(
        body,
        grid=(wide // tile,),
        in_specs=[pl.BlockSpec((None, rows, depth), lambda i: (q, 0, 0))] * (2 * half)
        + [pl.BlockSpec((tile, depth), lambda i: (i, 0))],
        out_specs=pl.BlockSpec((tokens, tile), lambda i: (0, i)),
        out_shape=jax.ShapeDtypeStruct((tokens, wide), jnp.bfloat16),
        scratch_shapes=[pltpu.VMEM((2 * half, rows, depth), jnp.bfloat16)],
        compiler_params=params(),
        cost_estimate=cost(2 * tokens * depth * wide, 2 * (down.size + tokens * depth)),
        name="hidden_grad_terms",
    )(*pieces, *others, down)


def down_weight_grads(gates, ups, places, grad, axis, scale):
    blocks, _, _, wide = gates[0].shape
    cols, chunks, rows, depth = grad.shape
    tokens = chunks * cols * rows
    tile = tile_of(wide, 256)
    n = len(gates)

    def body(*refs):
        gate_refs, up_refs = refs[:n], refs[n : 2 * n]
        grad_ref, out_ref, by_gate_ref, by_up_ref, hidden_ref = refs[2 * n :]
        for k, (shard, there) in enumerate(places(lax.axis_index(axis))):

            @pl.when(there)
            def _():
                gate_val = gate_refs[k][...].astype(jnp.float32)
                up_val = up_refs[k][...].astype(jnp.float32)
                sigma = sigmoid(gate_val)
                silu = gate_val * sigma
                slope = sigma * (1.0 + gate_val * (1.0 - sigma))
                to = pl.ds(shard * blocks, blocks)
                hidden_ref[to] = (silu * up_val).astype(jnp.bfloat16)
                by_gate_ref[to] = (up_val * slope).astype(jnp.bfloat16)
                by_up_ref[to] = silu.astype(jnp.bfloat16)

        left = hidden_ref[...].reshape(tokens, tile)
        right = grad_ref[...].reshape(tokens, depth)
        out_ref[...] = scale * dot(left, right, ((0,), (0,)))

    shard = pl.BlockSpec((blocks, chunks, rows, tile), lambda i: (0, 0, 0, i))
    factor = pl.BlockSpec((cols, chunks, rows, tile), lambda i: (0, 0, 0, i))
    factors = jax.ShapeDtypeStruct((cols, chunks, rows, wide), jnp.bfloat16)
    return pl.pallas_call(
        body,
        grid=(wide // tile,),
        in_specs=[shard] * (2 * n)
        + [pl.BlockSpec((cols, chunks, rows, depth), lambda i: (0, 0, 0, 0))],
        out_specs=[pl.BlockSpec((tile, depth), lambda i: (i, 0)), factor, factor],
        out_shape=[jax.ShapeDtypeStruct((wide, depth), jnp.float32), factors, factors],
        scratch_shapes=[pltpu.VMEM((cols, chunks, rows, tile), jnp.bfloat16)],
        compiler_params=params(),
        cost_estimate=cost(2 * tokens * wide * depth, 4 * wide * depth),
        name="down_weight_grads",
    )(*gates, *ups, grad)


def input_grad_terms(q, sums, by_gate, by_up, gate_weight, up_weight, axes, made):
    cols, chunks, rows, wide = by_gate.shape
    depth = gate_weight.shape[0]
    tokens = cols * rows
    levels = len(sums)
    tile = tile_of(depth, 512)

    def body(*refs):
        sums_refs, refs = refs[:levels], refs[levels:]
        by_gate_ref, by_up_ref, gate_w_ref, up_w_ref = refs[:4]
        gate_out, up_out, keep_ref, send_ref = refs[-4:]

        @pl.when(pl.program_id(0) == 0)
        def _():
            here = lax.axis_index(axes[0])
            hidden_grad = sums_refs[0][...].astype(jnp.float32)
            for level in range(1, levels):
                at_level = (here == levels - 1 - level) | (here == levels + level)
                other = sums_refs[level][...].astype(jnp.float32)
                hidden_grad = jnp.where(at_level, other, hidden_grad)
            for by_ref, out in ((by_gate_ref, gate_out), (by_up_ref, up_out)):
                by = by_ref[...].reshape(tokens, wide).astype(jnp.float32)
                out[...] = (hidden_grad * by).astype(jnp.bfloat16).reshape(cols, rows, wide)

        odd = lax.axis_index(axes[1]) % 2 == 1
        gate_grad = gate_out[...].reshape(tokens, wide)
        up_grad = up_out[...].reshape(tokens, wide)
        for part in halves_of(tile):
            res = dot(gate_grad, gate_w_ref[part], ((1,), (1,)))
            res += dot(up_grad, up_w_ref[part], ((1,), (1,)))
            res = res.astype(jnp.bfloat16).reshape(cols // 2, 2, rows, part.stop - part.start)
            keep_ref[:, :, part] = jnp.where(odd, res[:, 1], res[:, 0])
            send_ref[:, :, part] = jnp.where(odd, res[:, 0], res[:, 1])

    into = pl.BlockSpec((cols, None, rows, wide), lambda i: (0, q, 0, 0))
    weight = pl.BlockSpec((tile, wide), lambda i: (i, 0))
    half = pl.BlockSpec((cols // 2, rows, tile), lambda i: (0, 0, i))
    halves = jax.ShapeDtypeStruct((cols // 2, rows, depth), jnp.bfloat16)
    whole = jax.ShapeDtypeStruct((cols, chunks, rows, wide), jnp.bfloat16)
    return pl.pallas_call(
        body,
        grid=(depth // tile,),
        in_specs=[pl.BlockSpec((tokens, wide), lambda i: (0, 0))] * levels
        + [into, into, weight, weight]
        + [pl.BlockSpec(memory_space=pl.ANY)] * len(made),
        out_specs=[into, into, half, half],
        out_shape=[whole, whole, halves, halves],
        input_output_aliases={levels + 4 + j: j for j in range(len(made))},
        compiler_params=params(),
        cost_estimate=cost(4 * tokens * wide * depth, 4 * wide * depth),
        name="input_grad_terms",
    )(*sums, by_gate, by_up, gate_weight, up_weight, *made)


def projection_grads(inputs, gate_grad, up_grad, scale):
    depth, tokens = inputs.shape
    wide = gate_grad.shape[1]
    tile = tile_of(depth, 256)

    def body(inputs_ref, gate_ref, up_ref, gate_out, up_out):
        left = inputs_ref[...]
        gate_out[...] = scale * dot(left, gate_ref[...], ((1,), (0,)))
        up_out[...] = scale * dot(left, up_ref[...], ((1,), (0,)))

    once = pl.BlockSpec((tokens, wide), lambda i: (0, 0))
    out = pl.BlockSpec((tile, wide), lambda i: (i, 0))
    return pl.pallas_call(
        body,
        grid=(depth // tile,),
        in_specs=[pl.BlockSpec((tile, tokens), lambda i: (i, 0)), once, once],
        out_specs=[out, out],
        out_shape=[jax.ShapeDtypeStruct((depth, wide), jnp.float32)] * 2,
        compiler_params=params(),
        cost_estimate=cost(4 * tokens * wide * depth, 8 * wide * depth),
        name="projection_grads",
    )(inputs, gate_grad, up_grad)


def gather_places(size):
    def places(here):
        if size != 4:
            return [(here ^ k, True) for k in range(size)]
        outer = (here == 0) | (here == 3)
        inner = jnp.logical_not(outer)
        return [
            (here, True),
            (here ^ 1, True),
            (here ^ 3, inner),
            (here ^ 2, inner),
            (here ^ 2, outer),
            (here ^ 3, outer),
        ]

    return places


def gather_step(found, step, axis, size):
    inner, outward = [(1, 2), (2, 1)], [(2, 3), (1, 0)]
    if size != 4:
        near = range(1, size) if step == 0 else ()
        new = [(0, [(i, i ^ k) for i in range(size)]) for k in near]
    else:
        swap = [(i, i ^ 1) for i in range(size)]
        new = [[(0, swap), (0, inner)], [(1, inner), (2, outward)], [(3, outward)]][step]
    return found + [lax.ppermute(found[k], axis, pairs) for k, pairs in new]


def both(left, right):
    return (left.astype(jnp.float32) + right.astype(jnp.float32)).astype(jnp.bfloat16)


def sum_in(term, axis, size):
    total = term
    for k in range(size // 2 - 1):
        got = lax.ppermute(total, axis, [(k, k + 1), (size - 1 - k, size - 2 - k)])
        total = both(term, got)
    return total


def sum_swap(total, axis, size):
    half = size // 2
    return both(total, lax.ppermute(total, axis, [(half - 1, half), (half, half - 1)]))


def sum_out(total, axis, size):
    found = [total]
    for k in reversed(range(size // 2 - 1)):
        found.append(lax.ppermute(found[-1], axis, [(k + 1, k), (size - 2 - k, size - 1 - k)]))
    return found


def scatter_halves(keep, send, axis, size):
    return both(keep, lax.ppermute(send, axis, [(i, i ^ 1) for i in range(size)]))


def scatter_sum(halves, axis, size):
    here = lax.axis_index(axis)

    def block(k):
        at = (here // 2) ^ k
        return jnp.concatenate(
            [lax.dynamic_index_in_dim(x, at, 0, keepdims=False) for x in halves], axis=0
        )

    total = block(0).astype(jnp.float32)
    for k in range(1, size // 2):
        got = lax.ppermute(block(k), axis, [(i, i ^ (2 * k)) for i in range(size)])
        total += got.astype(jnp.float32)
    return total.astype(jnp.bfloat16)


def hold(*values):
    return lax.optimization_barrier(values)


def solution(mesh):
    n_row, n_col = mesh.shape["row"], mesh.shape["col"]

    def shards(layer_input, out_grad, gate_saved, up_saved, gate_weight, up_weight, down_weight):
        block, depth = layer_input.shape
        row_tokens, wide = gate_saved.shape
        tokens = block * n_col
        rows = block // CHUNKS
        scale = float(tokens) ** (-0.5)
        weights = (gate_weight, up_weight, ("row", "col"))

        view = (row_tokens // block, CHUNKS, rows, wide)
        gates = gather_step([gate_saved.reshape(view)], 0, "row", n_row)
        ups = [up_saved.reshape(view)]
        own = out_grad.reshape(CHUNKS, rows, depth)
        pieces = [own] + [
            lax.ppermute(own, "col", [(i, i ^ (2 * k)) for i in range(n_col)])
            for k in range(1, n_col // 2)
        ]
        pieces, gates, ups, out_grad, layer_input = hold(pieces, gates, ups, out_grad, layer_input)
        ups = gather_step(ups, 0, "row", n_row)
        others = [lax.ppermute(x, "col", [(i, i ^ 1) for i in range(n_col)]) for x in pieces]
        grad = lax.all_gather(out_grad, "col", axis=0, tiled=True)
        inputs = lax.all_gather(layer_input, "col", axis=0, tiled=True)
        first = hidden_grad_terms(0, pieces, others, "col", down_weight)
        first, gates, ups, pieces, others = hold(first, gates, ups, pieces, others)

        first = sum_in(first, "row", n_row)
        gates = gather_step(gates, 1, "row", n_row)
        ups = gather_step(ups, 1, "row", n_row)
        second = hidden_grad_terms(1, pieces, others, "col", down_weight)
        first, second, gates, ups = hold(first, second, gates, ups)

        second = sum_in(second, "row", n_row)
        first = sum_swap(first, "row", n_row)
        gates = gather_step(gates, 2, "row", n_row)
        ups = gather_step(ups, 2, "row", n_row)
        first, second, grad, gates, ups = hold(first, second, grad, gates, ups)

        first = sum_out(first, "row", n_row)
        second = sum_swap(second, "row", n_row)
        grad = grad.reshape(n_col, CHUNKS, rows, depth)
        down_weight_grad, *factors = down_weight_grads(
            gates, ups, gather_places(n_row), grad, "row", scale
        )
        first, second, down_weight_grad, factors, inputs = hold(
            first, second, down_weight_grad, factors, inputs
        )

        second = sum_out(second, "row", n_row)
        *made, keep, send = input_grad_terms(0, first, *factors, *weights, ())
        inputs = inputs.T
        second, made, keep, send, inputs = hold(second, made, keep, send, inputs)

        early = scatter_halves(keep, send, "col", n_col)
        *made, keep, send = input_grad_terms(1, second, *factors, *weights, made)
        early, made, keep, send = hold(early, made, keep, send)
        late = scatter_halves(keep, send, "col", n_col)
        late, made = hold(late, made)
        input_grad = scatter_sum([early, late], "col", n_col)
        made = [x.reshape(tokens, wide) for x in made]
        gate_weight_grad, up_weight_grad = projection_grads(inputs, *made, scale)
        return input_grad, gate_weight_grad, up_weight_grad, down_weight_grad

    by_token, by_unit = P("col", "row"), P("row", "col")
    return jax.shard_map(
        shards,
        mesh=mesh,
        in_specs=(by_token, by_token, by_unit, by_unit, by_unit, by_unit, by_token),
        out_specs=(by_token, by_unit, by_unit, by_token),
        check_vma=False,
    )
```

```python
import jax
import jax.numpy as jnp
from jax import lax
from jax.experimental import pallas as pl
from jax.experimental.pallas import tpu as pltpu
from jax.sharding import PartitionSpec as P

CHUNKS = 2
VMEM = 60 * 1024 * 1024


def tile_of(size, limit):
    return max(t for t in range(128, limit + 1, 128) if size % t == 0)


def params():
    return pltpu.CompilerParams(vmem_limit_bytes=VMEM)


def cost(flops, moved):
    return pl.CostEstimate(flops=flops, bytes_accessed=moved, transcendentals=0)


def dot(left, right, dims):
    return lax.dot_general(left, right, (dims, ((), ())), preferred_element_type=jnp.float32)


def halves_of(size):
    cut = max(size // 2 // 256 * 256, 128)
    return slice(0, size - cut), slice(size - cut, size)


def sigmoid(gate):
    return 1.0 / (1.0 + jnp.exp(-gate))


def hidden_grad_terms(q, pieces, others, axis, down):
    half = len(pieces)
    _, rows, depth = pieces[0].shape
    wide = down.shape[0]
    tokens = 2 * half * rows
    tile = tile_of(wide, 896)

    def body(*refs):
        down_ref, out_ref, grad_ref = refs[2 * half :]

        @pl.when(pl.program_id(0) == 0)
        def _():
            here = lax.axis_index(axis)
            for k in range(half):
                grad_ref[here ^ (2 * k)] = refs[k][...]
                grad_ref[here ^ (2 * k + 1)] = refs[half + k][...]

        left = grad_ref[...].reshape(tokens, depth)
        out_ref[...] = dot(left, down_ref[...], ((1,), (1,))).astype(jnp.bfloat16)

    return pl.pallas_call(
        body,
        grid=(wide // tile,),
        in_specs=[pl.BlockSpec((None, rows, depth), lambda i: (q, 0, 0))] * (2 * half)
        + [pl.BlockSpec((tile, depth), lambda i: (i, 0))],
        out_specs=pl.BlockSpec((tokens, tile), lambda i: (0, i)),
        out_shape=jax.ShapeDtypeStruct((tokens, wide), jnp.bfloat16),
        scratch_shapes=[pltpu.VMEM((2 * half, rows, depth), jnp.bfloat16)],
        compiler_params=params(),
        cost_estimate=cost(2 * tokens * depth * wide, 2 * (down.size + tokens * depth)),
        name="hidden_grad_terms",
    )(*pieces, *others, down)


def down_weight_grads(saved, places, grad, axis, scale):
    blocks, _, _, wide = saved[0][0].shape
    cols, chunks, rows, depth = grad.shape
    tokens = chunks * cols * rows
    tile = tile_of(wide, 256)
    flat = [x for shard in saved for x in shard]
    n = len(flat)

    def body(*refs):
        saved_refs = list(refs[:n])
        grad_ref, out_ref, by_gate_ref, by_up_ref, hidden_ref = refs[n:]
        for k, (shard, there) in enumerate(places(lax.axis_index(axis))):
            pair = [saved_refs.pop(0) for _ in saved[k]]
            gate_ref, up_ref = pair if len(pair) == 2 else (pair[0].at[0], pair[0].at[1])

            @pl.when(there)
            def _():
                gate_val = gate_ref[...].astype(jnp.float32)
                up_val = up_ref[...].astype(jnp.float32)
                sigma = sigmoid(gate_val)
                silu = gate_val * sigma
                slope = sigma * (1.0 + gate_val * (1.0 - sigma))
                to = pl.ds(shard * blocks, blocks)
                hidden_ref[to] = (silu * up_val).astype(jnp.bfloat16)
                by_gate_ref[to] = (up_val * slope).astype(jnp.bfloat16)
                by_up_ref[to] = silu.astype(jnp.bfloat16)

        left = hidden_ref[...].reshape(tokens, tile)
        right = grad_ref[...].reshape(tokens, depth)
        out_ref[...] = scale * dot(left, right, ((0,), (0,)))

    one = pl.BlockSpec((blocks, chunks, rows, tile), lambda i: (0, 0, 0, i))
    two = pl.BlockSpec((2, blocks, chunks, rows, tile), lambda i: (0, 0, 0, 0, i))
    factor = pl.BlockSpec((cols, chunks, rows, tile), lambda i: (0, 0, 0, i))
    factors = jax.ShapeDtypeStruct((cols, chunks, rows, wide), jnp.bfloat16)
    return pl.pallas_call(
        body,
        grid=(wide // tile,),
        in_specs=[one if x.ndim == 4 else two for x in flat]
        + [pl.BlockSpec((cols, chunks, rows, depth), lambda i: (0, 0, 0, 0))],
        out_specs=[pl.BlockSpec((tile, depth), lambda i: (i, 0)), factor, factor],
        out_shape=[jax.ShapeDtypeStruct((wide, depth), jnp.float32), factors, factors],
        scratch_shapes=[pltpu.VMEM((cols, chunks, rows, tile), jnp.bfloat16)],
        compiler_params=params(),
        cost_estimate=cost(2 * tokens * wide * depth, 4 * wide * depth),
        name="down_weight_grads",
    )(*flat, grad)


def input_grad_terms(q, sums, by_gate, by_up, gate_weight, up_weight, axes, made):
    cols, chunks, rows, wide = by_gate.shape
    depth = gate_weight.shape[0]
    tokens = cols * rows
    levels = len(sums)
    tile = tile_of(depth, 512)

    def body(*refs):
        sums_refs, refs = refs[:levels], refs[levels:]
        by_gate_ref, by_up_ref, gate_w_ref, up_w_ref = refs[:4]
        gate_out, up_out, keep_ref, send_ref = refs[-4:]

        @pl.when(pl.program_id(0) == 0)
        def _():
            here = lax.axis_index(axes[0])
            hidden_grad = sums_refs[0][...].astype(jnp.float32)
            for level in range(1, levels):
                at_level = (here == levels - 1 - level) | (here == levels + level)
                other = sums_refs[level][...].astype(jnp.float32)
                hidden_grad = jnp.where(at_level, other, hidden_grad)
            for by_ref, out in ((by_gate_ref, gate_out), (by_up_ref, up_out)):
                by = by_ref[...].reshape(tokens, wide).astype(jnp.float32)
                out[...] = (hidden_grad * by).astype(jnp.bfloat16).reshape(cols, rows, wide)

        odd = lax.axis_index(axes[1]) % 2 == 1
        gate_grad = gate_out[...].reshape(tokens, wide)
        up_grad = up_out[...].reshape(tokens, wide)
        for part in halves_of(tile):
            res = dot(gate_grad, gate_w_ref[part], ((1,), (1,)))
            res += dot(up_grad, up_w_ref[part], ((1,), (1,)))
            res = res.astype(jnp.bfloat16).reshape(cols // 2, 2, rows, part.stop - part.start)
            keep_ref[:, :, part] = jnp.where(odd, res[:, 1], res[:, 0])
            send_ref[:, :, part] = jnp.where(odd, res[:, 0], res[:, 1])

    into = pl.BlockSpec((cols, None, rows, wide), lambda i: (0, q, 0, 0))
    weight = pl.BlockSpec((tile, wide), lambda i: (i, 0))
    half = pl.BlockSpec((cols // 2, rows, tile), lambda i: (0, 0, i))
    halves = jax.ShapeDtypeStruct((cols // 2, rows, depth), jnp.bfloat16)
    whole = jax.ShapeDtypeStruct((cols, chunks, rows, wide), jnp.bfloat16)
    return pl.pallas_call(
        body,
        grid=(depth // tile,),
        in_specs=[pl.BlockSpec((tokens, wide), lambda i: (0, 0))] * levels
        + [into, into, weight, weight]
        + [pl.BlockSpec(memory_space=pl.ANY)] * len(made),
        out_specs=[into, into, half, half],
        out_shape=[whole, whole, halves, halves],
        input_output_aliases={levels + 4 + j: j for j in range(len(made))},
        compiler_params=params(),
        cost_estimate=cost(4 * tokens * wide * depth, 4 * wide * depth),
        name="input_grad_terms",
    )(*sums, by_gate, by_up, gate_weight, up_weight, *made)


def projection_grads(inputs, gate_grad, up_grad, scale):
    depth, tokens = inputs.shape
    wide = gate_grad.shape[1]
    tile = tile_of(depth, 256)

    def body(inputs_ref, gate_ref, up_ref, gate_out, up_out):
        left = inputs_ref[...]
        gate_out[...] = scale * dot(left, gate_ref[...], ((1,), (0,)))
        up_out[...] = scale * dot(left, up_ref[...], ((1,), (0,)))

    once = pl.BlockSpec((tokens, wide), lambda i: (0, 0))
    out = pl.BlockSpec((tile, wide), lambda i: (i, 0))
    return pl.pallas_call(
        body,
        grid=(depth // tile,),
        in_specs=[pl.BlockSpec((tile, tokens), lambda i: (i, 0)), once, once],
        out_specs=[out, out],
        out_shape=[jax.ShapeDtypeStruct((depth, wide), jnp.float32)] * 2,
        compiler_params=params(),
        cost_estimate=cost(4 * tokens * wide * depth, 8 * wide * depth),
        name="projection_grads",
    )(inputs, gate_grad, up_grad)


def gather_places(size):
    def places(here):
        if size != 4:
            return [(here ^ k, True) for k in range(size)]
        outer = (here == 0) | (here == 3)
        inner = jnp.logical_not(outer)
        return [
            (here, True),
            (here ^ 1, True),
            (here ^ 3, inner),
            (here ^ 2, inner),
            (here ^ 2, outer),
            (here ^ 3, outer),
        ]

    return places


def gather_near(shard, axis, size):
    if size == 4:
        swaps = [[(i, i ^ 1) for i in range(size)], [(1, 2), (2, 1)]]
    else:
        swaps = [[(i, i ^ k) for i in range(size)] for k in range(1, size)]
    return [shard] + [lax.ppermute(shard, axis, pairs) for pairs in swaps]


def trade(term, shards, axis):
    here = lax.axis_index(axis)
    outer = (here == 0) | (here == 3)
    given = jnp.where(outer, term, shards.reshape(term.shape))
    return lax.ppermute(given, axis, [(i, i ^ 1) for i in range(4)])


def both(left, right):
    return (left.astype(jnp.float32) + right.astype(jnp.float32)).astype(jnp.bfloat16)


def sum_in(term, axis, size):
    total = term
    for k in range(size // 2 - 1):
        got = lax.ppermute(total, axis, [(k, k + 1), (size - 1 - k, size - 2 - k)])
        total = both(term, got)
    return total


def sum_swap(total, axis, size):
    half = size // 2
    return both(total, lax.ppermute(total, axis, [(half - 1, half), (half, half - 1)]))


def sum_out(total, axis, size):
    found = [total]
    for k in reversed(range(size // 2 - 1)):
        found.append(lax.ppermute(found[-1], axis, [(k + 1, k), (size - 2 - k, size - 1 - k)]))
    return found


def scatter_halves(keep, send, axis, size):
    return both(keep, lax.ppermute(send, axis, [(i, i ^ 1) for i in range(size)]))


def scatter_sum(halves, axis, size):
    here = lax.axis_index(axis)

    def block(k):
        at = (here // 2) ^ k
        return jnp.concatenate(
            [lax.dynamic_index_in_dim(x, at, 0, keepdims=False) for x in halves], axis=0
        )

    total = block(0).astype(jnp.float32)
    for k in range(1, size // 2):
        got = lax.ppermute(block(k), axis, [(i, i ^ (2 * k)) for i in range(size)])
        total += got.astype(jnp.float32)
    return total.astype(jnp.bfloat16)


def hold(*values):
    return lax.optimization_barrier(values)


def solution(mesh):
    n_row, n_col = mesh.shape["row"], mesh.shape["col"]

    def shards(layer_input, out_grad, gate_saved, up_saved, gate_weight, up_weight, down_weight):
        block, depth = layer_input.shape
        row_tokens, wide = gate_saved.shape
        tokens = block * n_col
        rows = block // CHUNKS
        scale = float(tokens) ** (-0.5)
        weights = (gate_weight, up_weight, ("row", "col"))

        view = (row_tokens // block, CHUNKS, rows, wide)
        gates = gather_near(gate_saved.reshape(view), "row", n_row)
        up_saved = up_saved.reshape(view)
        own = out_grad.reshape(CHUNKS, rows, depth)
        pieces = [own] + [
            lax.ppermute(own, "col", [(i, i ^ (2 * k)) for i in range(n_col)])
            for k in range(1, n_col // 2)
        ]
        pieces, gates, up_saved, out_grad, layer_input = hold(
            pieces, gates, up_saved, out_grad, layer_input
        )
        ups = gather_near(up_saved, "row", n_row)
        others = [lax.ppermute(x, "col", [(i, i ^ 1) for i in range(n_col)]) for x in pieces]
        grad = lax.all_gather(out_grad, "col", axis=0, tiled=True)
        inputs = lax.all_gather(layer_input, "col", axis=0, tiled=True)
        first = hidden_grad_terms(0, pieces, others, "col", down_weight)
        first, gates, ups, pieces, others = hold(first, gates, ups, pieces, others)

        line = n_row == 4 and 2 * row_tokens * CHUNKS == tokens
        saved = [list(pair) for pair in zip(gates, ups)]
        if line:
            got = trade(first, jnp.stack([gates[2], ups[2]]), "row")
            passed = lax.ppermute(jnp.stack([gates[1], ups[1]]), "row", [(1, 2), (2, 1)])
            first = both(first, got)
            saved += [[passed], [got.reshape(passed.shape)]]
        else:
            first = sum_in(first, "row", n_row)
        second = hidden_grad_terms(1, pieces, others, "col", down_weight)
        first, second, saved = hold(first, second, saved)

        if line:
            got = trade(second, saved[3][0], "row")
            second = both(second, got)
            saved += [[got.reshape(saved[3][0].shape)]]
        else:
            second = sum_in(second, "row", n_row)
        first = sum_swap(first, "row", n_row)
        first, second, grad, saved = hold(first, second, grad, saved)

        first = sum_out(first, "row", n_row)
        second = sum_swap(second, "row", n_row)
        grad = grad.reshape(n_col, CHUNKS, rows, depth)
        down_weight_grad, *factors = down_weight_grads(
            saved, gather_places(n_row), grad, "row", scale
        )
        first, second, down_weight_grad, factors, inputs = hold(
            first, second, down_weight_grad, factors, inputs
        )

        second = sum_out(second, "row", n_row)
        *made, keep, send = input_grad_terms(0, first, *factors, *weights, ())
        inputs = inputs.T
        second, made, keep, send, inputs = hold(second, made, keep, send, inputs)

        early = scatter_halves(keep, send, "col", n_col)
        *made, keep, send = input_grad_terms(1, second, *factors, *weights, made)
        early, made, keep, send = hold(early, made, keep, send)
        late = scatter_halves(keep, send, "col", n_col)
        late, made = hold(late, made)
        input_grad = scatter_sum([early, late], "col", n_col)
        made = [x.reshape(tokens, wide) for x in made]
        gate_weight_grad, up_weight_grad = projection_grads(inputs, *made, scale)
        return input_grad, gate_weight_grad, up_weight_grad, down_weight_grad

    by_token, by_unit = P("col", "row"), P("row", "col")
    return jax.shard_map(
        shards,
        mesh=mesh,
        in_specs=(by_token, by_token, by_unit, by_unit, by_unit, by_unit, by_token),
        out_specs=(by_token, by_unit, by_unit, by_token),
        check_vma=False,
    )
```

```python
import jax
import jax.numpy as jnp
from jax import lax
from jax.experimental import pallas as pl
from jax.experimental.pallas import tpu as pltpu
from jax.sharding import PartitionSpec as P

CHUNKS = 2
VMEM = 60 * 1024 * 1024


def tile_of(size, limit):
    return max(t for t in range(128, limit + 1, 128) if size % t == 0)


def params():
    return pltpu.CompilerParams(vmem_limit_bytes=VMEM)


def cost(flops, moved):
    return pl.CostEstimate(flops=flops, bytes_accessed=moved, transcendentals=0)


def dot(left, right, dims):
    return lax.dot_general(left, right, (dims, ((), ())), preferred_element_type=jnp.float32)


def halves_of(size):
    cut = max(size // 2 // 256 * 256, 128)
    return slice(0, size - cut), slice(size - cut, size)


def sigmoid(gate):
    return 1.0 / (1.0 + jnp.exp(-gate))


def hidden_grad_terms(q, pieces, others, axis, down):
    half = len(pieces)
    _, rows, depth = pieces[0].shape
    wide = down.shape[0]
    tokens = 2 * half * rows
    tile = tile_of(wide, 896)

    def body(*refs):
        down_ref, out_ref, grad_ref = refs[2 * half :]

        @pl.when(pl.program_id(0) == 0)
        def _():
            here = lax.axis_index(axis)
            for k in range(half):
                grad_ref[here ^ (2 * k)] = refs[k][...]
                grad_ref[here ^ (2 * k + 1)] = refs[half + k][...]

        left = grad_ref[...].reshape(tokens, depth)
        out_ref[...] = dot(left, down_ref[...], ((1,), (1,))).astype(jnp.bfloat16)

    return pl.pallas_call(
        body,
        grid=(wide // tile,),
        in_specs=[pl.BlockSpec((None, rows, depth), lambda i: (q, 0, 0))] * (2 * half)
        + [pl.BlockSpec((tile, depth), lambda i: (i, 0))],
        out_specs=[
            pl.BlockSpec((tokens, tile), lambda i: (0, i)),
            pl.BlockSpec((2 * half, rows, depth), lambda i: (0, 0, 0)),
        ],
        out_shape=[
            jax.ShapeDtypeStruct((tokens, wide), jnp.bfloat16),
            jax.ShapeDtypeStruct((2 * half, rows, depth), jnp.bfloat16),
        ],
        compiler_params=params(),
        cost_estimate=cost(2 * tokens * depth * wide, 2 * (down.size + tokens * depth)),
        name="hidden_grad_terms",
    )(*pieces, *others, down)


def down_weight_grads(saved, places, grads, axis, scale):
    blocks, _, _, wide = saved[0][0].shape
    cols, rows, depth = grads[0].shape
    chunks = len(grads)
    tokens = chunks * cols * rows
    tile = tile_of(wide, 256)
    flat = [x for shard in saved for x in shard]
    n = len(flat)

    def body(*refs):
        saved_refs = list(refs[:n])
        grad_refs, refs = refs[n : n + chunks], refs[n + chunks :]
        out_ref, by_gate_ref, by_up_ref, hidden_ref = refs
        for k, (shard, there) in enumerate(places(lax.axis_index(axis))):
            pair = [saved_refs.pop(0) for _ in saved[k]]
            gate_ref, up_ref = pair if len(pair) == 2 else (pair[0].at[0], pair[0].at[1])

            @pl.when(there)
            def _():
                gate_val = gate_ref[...].astype(jnp.float32)
                up_val = up_ref[...].astype(jnp.float32)
                sigma = sigmoid(gate_val)
                silu = gate_val * sigma
                slope = sigma * (1.0 + gate_val * (1.0 - sigma))
                to = pl.ds(shard * blocks, blocks)
                hidden_ref[to] = (silu * up_val).astype(jnp.bfloat16)
                by_gate_ref[to] = (up_val * slope).astype(jnp.bfloat16)
                by_up_ref[to] = silu.astype(jnp.bfloat16)

        res = 0.0
        for q in range(chunks):
            left = hidden_ref[:, q].reshape(cols * rows, tile)
            res += dot(left, grad_refs[q][...].reshape(cols * rows, depth), ((0,), (0,)))
        out_ref[...] = scale * res

    one = pl.BlockSpec((blocks, chunks, rows, tile), lambda i: (0, 0, 0, i))
    two = pl.BlockSpec((2, blocks, chunks, rows, tile), lambda i: (0, 0, 0, 0, i))
    factor = pl.BlockSpec((cols, chunks, rows, tile), lambda i: (0, 0, 0, i))
    factors = jax.ShapeDtypeStruct((cols, chunks, rows, wide), jnp.bfloat16)
    return pl.pallas_call(
        body,
        grid=(wide // tile,),
        in_specs=[one if x.ndim == 4 else two for x in flat]
        + [pl.BlockSpec((cols, rows, depth), lambda i: (0, 0, 0))] * chunks,
        out_specs=[pl.BlockSpec((tile, depth), lambda i: (i, 0)), factor, factor],
        out_shape=[jax.ShapeDtypeStruct((wide, depth), jnp.float32), factors, factors],
        scratch_shapes=[pltpu.VMEM((cols, chunks, rows, tile), jnp.bfloat16)],
        compiler_params=params(),
        cost_estimate=cost(2 * tokens * wide * depth, 4 * wide * depth),
        name="down_weight_grads",
    )(*flat, *grads)


def input_grad_terms(q, sums, by_gate, by_up, gate_weight, up_weight, axes, made):
    cols, chunks, rows, wide = by_gate.shape
    depth = gate_weight.shape[0]
    tokens = cols * rows
    levels = len(sums)
    tile = tile_of(depth, 512)

    def body(*refs):
        sums_refs, refs = refs[:levels], refs[levels:]
        by_gate_ref, by_up_ref, gate_w_ref, up_w_ref = refs[:4]
        gate_out, up_out, keep_ref, send_ref = refs[-4:]

        @pl.when(pl.program_id(0) == 0)
        def _():
            here = lax.axis_index(axes[0])
            hidden_grad = sums_refs[0][...].astype(jnp.float32)
            for level in range(1, levels):
                at_level = (here == levels - 1 - level) | (here == levels + level)
                other = sums_refs[level][...].astype(jnp.float32)
                hidden_grad = jnp.where(at_level, other, hidden_grad)
            for by_ref, out in ((by_gate_ref, gate_out), (by_up_ref, up_out)):
                by = by_ref[...].reshape(tokens, wide).astype(jnp.float32)
                out[...] = (hidden_grad * by).astype(jnp.bfloat16).reshape(cols, rows, wide)

        odd = lax.axis_index(axes[1]) % 2 == 1
        gate_grad = gate_out[...].reshape(tokens, wide)
        up_grad = up_out[...].reshape(tokens, wide)
        for part in halves_of(tile):
            res = dot(gate_grad, gate_w_ref[part], ((1,), (1,)))
            res += dot(up_grad, up_w_ref[part], ((1,), (1,)))
            res = res.astype(jnp.bfloat16).reshape(cols // 2, 2, rows, part.stop - part.start)
            keep_ref[:, :, part] = jnp.where(odd, res[:, 1], res[:, 0])
            send_ref[:, :, part] = jnp.where(odd, res[:, 0], res[:, 1])

    into = pl.BlockSpec((cols, None, rows, wide), lambda i: (0, q, 0, 0))
    weight = pl.BlockSpec((tile, wide), lambda i: (i, 0))
    half = pl.BlockSpec((cols // 2, rows, tile), lambda i: (0, 0, i))
    halves = jax.ShapeDtypeStruct((cols // 2, rows, depth), jnp.bfloat16)
    whole = jax.ShapeDtypeStruct((cols, chunks, rows, wide), jnp.bfloat16)
    return pl.pallas_call(
        body,
        grid=(depth // tile,),
        in_specs=[pl.BlockSpec((tokens, wide), lambda i: (0, 0))] * levels
        + [into, into, weight, weight]
        + [pl.BlockSpec(memory_space=pl.ANY)] * len(made),
        out_specs=[into, into, half, half],
        out_shape=[whole, whole, halves, halves],
        input_output_aliases={levels + 4 + j: j for j in range(len(made))},
        compiler_params=params(),
        cost_estimate=cost(4 * tokens * wide * depth, 4 * wide * depth),
        name="input_grad_terms",
    )(*sums, by_gate, by_up, gate_weight, up_weight, *made)


def projection_grads(inputs, gate_grad, up_grad, scale):
    depth, tokens = inputs.shape
    wide = gate_grad.shape[1]
    tile = tile_of(depth, 256)

    def body(inputs_ref, gate_ref, up_ref, gate_out, up_out):
        left = inputs_ref[...]
        gate_out[...] = scale * dot(left, gate_ref[...], ((1,), (0,)))
        up_out[...] = scale * dot(left, up_ref[...], ((1,), (0,)))

    once = pl.BlockSpec((tokens, wide), lambda i: (0, 0))
    out = pl.BlockSpec((tile, wide), lambda i: (i, 0))
    return pl.pallas_call(
        body,
        grid=(depth // tile,),
        in_specs=[pl.BlockSpec((tile, tokens), lambda i: (i, 0)), once, once],
        out_specs=[out, out],
        out_shape=[jax.ShapeDtypeStruct((depth, wide), jnp.float32)] * 2,
        compiler_params=params(),
        cost_estimate=cost(4 * tokens * wide * depth, 8 * wide * depth),
        name="projection_grads",
    )(inputs, gate_grad, up_grad)


def turned(pieces, others, axis):
    half = len(pieces)
    rows, depth = pieces[0].shape
    tile = tile_of(depth, 512)

    def body(*refs):
        out_ref, whole_ref = refs[2 * half :]
        here = lax.axis_index(axis)
        for k in range(half):
            whole_ref[here ^ (2 * k)] = refs[k][...]
            whole_ref[here ^ (2 * k + 1)] = refs[half + k][...]
        out_ref[...] = whole_ref[...].reshape(2 * half * rows, tile).T

    tokens = 2 * half * rows
    return pl.pallas_call(
        body,
        grid=(depth // tile,),
        in_specs=[pl.BlockSpec((rows, tile), lambda i: (0, i))] * (2 * half),
        out_specs=pl.BlockSpec((tile, tokens), lambda i: (i, 0)),
        out_shape=jax.ShapeDtypeStruct((depth, tokens), jnp.bfloat16),
        scratch_shapes=[pltpu.VMEM((2 * half, rows, tile), jnp.bfloat16)],
        compiler_params=params(),
        cost_estimate=cost(1, 4 * depth * tokens),
        name="turned",
    )(*pieces, *others)


def gather_parity(own, axis, size):
    return [own] + [
        lax.ppermute(own, axis, [(i, i ^ (2 * k)) for i in range(size)]) for k in range(1, size // 2)
    ]


def gather_others(pieces, axis, size):
    return [lax.ppermute(x, axis, [(i, i ^ 1) for i in range(size)]) for x in pieces]


def gather_places(size):
    def places(here):
        if size != 4:
            return [(here ^ k, True) for k in range(size)]
        outer = (here == 0) | (here == 3)
        inner = jnp.logical_not(outer)
        return [
            (here, True),
            (here ^ 1, True),
            (here ^ 3, inner),
            (here ^ 2, inner),
            (here ^ 2, outer),
            (here ^ 3, outer),
        ]

    return places


def gather_near(shard, axis, size):
    if size == 4:
        swaps = [[(i, i ^ 1) for i in range(size)], [(1, 2), (2, 1)]]
    else:
        swaps = [[(i, i ^ k) for i in range(size)] for k in range(1, size)]
    return [shard] + [lax.ppermute(shard, axis, pairs) for pairs in swaps]


def trade(term, shards, axis):
    here = lax.axis_index(axis)
    outer = (here == 0) | (here == 3)
    given = jnp.where(outer, term, shards.reshape(term.shape))
    return lax.ppermute(given, axis, [(i, i ^ 1) for i in range(4)])


def both(left, right):
    return (left.astype(jnp.float32) + right.astype(jnp.float32)).astype(jnp.bfloat16)


def sum_in(term, axis, size):
    total = term
    for k in range(size // 2 - 1):
        got = lax.ppermute(total, axis, [(k, k + 1), (size - 1 - k, size - 2 - k)])
        total = both(term, got)
    return total


def sum_swap(total, axis, size):
    half = size // 2
    return both(total, lax.ppermute(total, axis, [(half - 1, half), (half, half - 1)]))


def sum_out(total, axis, size):
    found = [total]
    for k in reversed(range(size // 2 - 1)):
        found.append(lax.ppermute(found[-1], axis, [(k + 1, k), (size - 2 - k, size - 1 - k)]))
    return found


def scatter_halves(keep, send, axis, size):
    return both(keep, lax.ppermute(send, axis, [(i, i ^ 1) for i in range(size)]))


def scatter_sum(halves, axis, size):
    here = lax.axis_index(axis)

    def block(k):
        at = (here // 2) ^ k
        return jnp.concatenate(
            [lax.dynamic_index_in_dim(x, at, 0, keepdims=False) for x in halves], axis=0
        )

    total = block(0).astype(jnp.float32)
    for k in range(1, size // 2):
        got = lax.ppermute(block(k), axis, [(i, i ^ (2 * k)) for i in range(size)])
        total += got.astype(jnp.float32)
    return total.astype(jnp.bfloat16)


def hold(*values):
    return lax.optimization_barrier(values)


def solution(mesh):
    n_row, n_col = mesh.shape["row"], mesh.shape["col"]

    def shards(layer_input, out_grad, gate_saved, up_saved, gate_weight, up_weight, down_weight):
        block, depth = layer_input.shape
        row_tokens, wide = gate_saved.shape
        tokens = block * n_col
        rows = block // CHUNKS
        scale = float(tokens) ** (-0.5)
        weights = (gate_weight, up_weight, ("row", "col"))

        view = (row_tokens // block, CHUNKS, rows, wide)
        gates = gather_near(gate_saved.reshape(view), "row", n_row)
        up_saved = up_saved.reshape(view)
        pieces = gather_parity(out_grad.reshape(CHUNKS, rows, depth), "col", n_col)
        pieces, gates, up_saved, layer_input = hold(pieces, gates, up_saved, layer_input)
        ups = gather_near(up_saved, "row", n_row)
        others = gather_others(pieces, "col", n_col)
        first, grad = hidden_grad_terms(0, pieces, others, "col", down_weight)
        grads = [grad]
        first, gates, ups, pieces, others, layer_input = hold(
            first, gates, ups, pieces, others, layer_input
        )

        line = n_row == 4 and 2 * row_tokens * CHUNKS == tokens
        saved = [list(pair) for pair in zip(gates, ups)]
        if line:
            got = trade(first, jnp.stack([gates[2], ups[2]]), "row")
            passed = lax.ppermute(jnp.stack([gates[1], ups[1]]), "row", [(1, 2), (2, 1)])
            first = both(first, got)
            saved += [[passed], [got.reshape(passed.shape)]]
        else:
            first = sum_in(first, "row", n_row)
        second, grad = hidden_grad_terms(1, pieces, others, "col", down_weight)
        grads.append(grad)
        first, second, saved, layer_input = hold(first, second, saved, layer_input)

        if line:
            got = trade(second, saved[3][0], "row")
            second = both(second, got)
            saved += [[got.reshape(saved[3][0].shape)]]
        else:
            second = sum_in(second, "row", n_row)
        first = sum_swap(first, "row", n_row)
        inputs = gather_parity(layer_input, "col", n_col)
        first, second, saved, inputs = hold(first, second, saved, inputs)

        first = sum_out(first, "row", n_row)
        second = sum_swap(second, "row", n_row)
        down_weight_grad, *factors = down_weight_grads(
            saved, gather_places(n_row), grads, "row", scale
        )
        other_inputs = gather_others(inputs, "col", n_col)
        first, second, down_weight_grad, factors, other_inputs = hold(
            first, second, down_weight_grad, factors, other_inputs
        )

        second = sum_out(second, "row", n_row)
        *made, keep, send = input_grad_terms(0, first, *factors, *weights, ())
        inputs = turned(inputs, other_inputs, "col")
        second, made, keep, send, inputs = hold(second, made, keep, send, inputs)

        early = scatter_halves(keep, send, "col", n_col)
        *made, keep, send = input_grad_terms(1, second, *factors, *weights, made)
        early, made, keep, send = hold(early, made, keep, send)
        late = scatter_halves(keep, send, "col", n_col)
        late, made = hold(late, made)
        input_grad = scatter_sum([early, late], "col", n_col)
        made = [x.reshape(tokens, wide) for x in made]
        gate_weight_grad, up_weight_grad = projection_grads(inputs, *made, scale)
        return input_grad, gate_weight_grad, up_weight_grad, down_weight_grad

    by_token, by_unit = P("col", "row"), P("row", "col")
    return jax.shard_map(
        shards,
        mesh=mesh,
        in_specs=(by_token, by_token, by_unit, by_unit, by_unit, by_unit, by_token),
        out_specs=(by_token, by_unit, by_unit, by_token),
        check_vma=False,
    )
```

```python
import jax
import jax.numpy as jnp
from jax import lax
from jax.experimental import pallas as pl
from jax.experimental.pallas import tpu as pltpu
from jax.sharding import PartitionSpec as P

CHUNKS = 2
VMEM = 60 * 1024 * 1024


def tile_of(size, limit):
    return max(t for t in range(128, limit + 1, 128) if size % t == 0)


def params():
    return pltpu.CompilerParams(vmem_limit_bytes=VMEM)


def cost(flops, moved):
    return pl.CostEstimate(flops=flops, bytes_accessed=moved, transcendentals=0)


def dot(left, right, dims):
    return lax.dot_general(left, right, (dims, ((), ())), preferred_element_type=jnp.float32)


def halves_of(size):
    cut = max(size // 2 // 256 * 256, 128)
    return slice(0, size - cut), slice(size - cut, size)


def sigmoid(gate):
    return 1.0 / (1.0 + jnp.exp(-gate))


def hidden_grad_terms(pieces, others, axis, down):
    half = len(pieces)
    rows, depth = pieces[0].shape
    wide = down.shape[0]
    tokens = 2 * half * rows
    tile = tile_of(wide, 896)

    def body(*refs):
        down_ref, out_ref, grad_ref = refs[2 * half :]

        @pl.when(pl.program_id(0) == 0)
        def _():
            here = lax.axis_index(axis)
            for k in range(half):
                grad_ref[here ^ (2 * k)] = refs[k][...]
                grad_ref[here ^ (2 * k + 1)] = refs[half + k][...]

        left = grad_ref[...].reshape(tokens, depth)
        out_ref[...] = dot(left, down_ref[...], ((1,), (1,))).astype(jnp.bfloat16)

    return pl.pallas_call(
        body,
        grid=(wide // tile,),
        in_specs=[pl.BlockSpec((rows, depth), lambda i: (0, 0))] * (2 * half)
        + [pl.BlockSpec((tile, depth), lambda i: (i, 0))],
        out_specs=[
            pl.BlockSpec((tokens, tile), lambda i: (0, i)),
            pl.BlockSpec((2 * half, rows, depth), lambda i: (0, 0, 0)),
        ],
        out_shape=[
            jax.ShapeDtypeStruct((tokens, wide), jnp.bfloat16),
            jax.ShapeDtypeStruct((2 * half, rows, depth), jnp.bfloat16),
        ],
        compiler_params=params(),
        cost_estimate=cost(2 * tokens * depth * wide, 2 * (down.size + tokens * depth)),
        name="hidden_grad_terms",
    )(*pieces, *others, down)


def down_weight_grads(saved, places, grads, axis, scale):
    blocks, _, _, wide = saved[0][0].shape
    cols, rows, depth = grads[0].shape
    chunks = len(grads)
    tokens = chunks * cols * rows
    tile = tile_of(wide, 256)
    flat = [x for shard in saved for x in shard]
    n = len(flat)

    def body(*refs):
        saved_refs = list(refs[:n])
        grad_refs, refs = refs[n : n + chunks], refs[n + chunks :]
        out_ref, by_gate_ref, by_up_ref, hidden_ref = refs
        for k, (shard, there) in enumerate(places(lax.axis_index(axis))):
            pair = [saved_refs.pop(0) for _ in saved[k]]
            gate_ref, up_ref = pair if len(pair) == 2 else (pair[0].at[0], pair[0].at[1])

            @pl.when(there)
            def _():
                gate_val = gate_ref[...].astype(jnp.float32)
                up_val = up_ref[...].astype(jnp.float32)
                sigma = sigmoid(gate_val)
                silu = gate_val * sigma
                slope = sigma * (1.0 + gate_val * (1.0 - sigma))
                to = pl.ds(shard * blocks, blocks)
                hidden_ref[to] = (silu * up_val).astype(jnp.bfloat16)
                by_gate_ref[to] = (up_val * slope).astype(jnp.bfloat16)
                by_up_ref[to] = silu.astype(jnp.bfloat16)

        res = 0.0
        for q in range(chunks):
            left = hidden_ref[:, q].reshape(cols * rows, tile)
            res += dot(left, grad_refs[q][...].reshape(cols * rows, depth), ((0,), (0,)))
        out_ref[...] = scale * res

    one = pl.BlockSpec((blocks, chunks, rows, tile), lambda i: (0, 0, 0, i))
    two = pl.BlockSpec((2, blocks, chunks, rows, tile), lambda i: (0, 0, 0, 0, i))
    factor = pl.BlockSpec((cols, chunks, rows, tile), lambda i: (0, 0, 0, i))
    factors = jax.ShapeDtypeStruct((cols, chunks, rows, wide), jnp.bfloat16)
    return pl.pallas_call(
        body,
        grid=(wide // tile,),
        in_specs=[one if x.ndim == 4 else two for x in flat]
        + [pl.BlockSpec((cols, rows, depth), lambda i: (0, 0, 0))] * chunks,
        out_specs=[pl.BlockSpec((tile, depth), lambda i: (i, 0)), factor, factor],
        out_shape=[jax.ShapeDtypeStruct((wide, depth), jnp.float32), factors, factors],
        scratch_shapes=[pltpu.VMEM((cols, chunks, rows, tile), jnp.bfloat16)],
        compiler_params=params(),
        cost_estimate=cost(2 * tokens * wide * depth, 4 * wide * depth),
        name="down_weight_grads",
    )(*flat, *grads)


def input_grad_terms(q, sums, by_gate, by_up, gate_weight, up_weight, axes, made):
    cols, chunks, rows, wide = by_gate.shape
    depth = gate_weight.shape[0]
    tokens = cols * rows
    levels = len(sums)
    tile = tile_of(depth, 512)

    def body(*refs):
        sums_refs, refs = refs[:levels], refs[levels:]
        by_gate_ref, by_up_ref, gate_w_ref, up_w_ref = refs[:4]
        gate_out, up_out, keep_ref, send_ref = refs[-4:]

        @pl.when(pl.program_id(0) == 0)
        def _():
            here = lax.axis_index(axes[0])
            hidden_grad = sums_refs[0][...].astype(jnp.float32)
            for level in range(1, levels):
                at_level = (here == levels - 1 - level) | (here == levels + level)
                other = sums_refs[level][...].astype(jnp.float32)
                hidden_grad = jnp.where(at_level, other, hidden_grad)
            for by_ref, out in ((by_gate_ref, gate_out), (by_up_ref, up_out)):
                by = by_ref[...].reshape(tokens, wide).astype(jnp.float32)
                out[...] = (hidden_grad * by).astype(jnp.bfloat16).reshape(cols, rows, wide)

        odd = lax.axis_index(axes[1]) % 2 == 1
        gate_grad = gate_out[...].reshape(tokens, wide)
        up_grad = up_out[...].reshape(tokens, wide)
        for part in halves_of(tile):
            res = dot(gate_grad, gate_w_ref[part], ((1,), (1,)))
            res += dot(up_grad, up_w_ref[part], ((1,), (1,)))
            res = res.astype(jnp.bfloat16).reshape(cols // 2, 2, rows, part.stop - part.start)
            keep_ref[:, :, part] = jnp.where(odd, res[:, 1], res[:, 0])
            send_ref[:, :, part] = jnp.where(odd, res[:, 0], res[:, 1])

    into = pl.BlockSpec((cols, None, rows, wide), lambda i: (0, q, 0, 0))
    weight = pl.BlockSpec((tile, wide), lambda i: (i, 0))
    half = pl.BlockSpec((cols // 2, rows, tile), lambda i: (0, 0, i))
    halves = jax.ShapeDtypeStruct((cols // 2, rows, depth), jnp.bfloat16)
    whole = jax.ShapeDtypeStruct((cols, chunks, rows, wide), jnp.bfloat16)
    return pl.pallas_call(
        body,
        grid=(depth // tile,),
        in_specs=[pl.BlockSpec((tokens, wide), lambda i: (0, 0))] * levels
        + [into, into, weight, weight]
        + [pl.BlockSpec(memory_space=pl.ANY)] * len(made),
        out_specs=[into, into, half, half],
        out_shape=[whole, whole, halves, halves],
        input_output_aliases={levels + 4 + j: j for j in range(len(made))},
        compiler_params=params(),
        cost_estimate=cost(4 * tokens * wide * depth, 4 * wide * depth),
        name="input_grad_terms",
    )(*sums, by_gate, by_up, gate_weight, up_weight, *made)


def projection_grads(inputs, gate_grad, up_grad, scale):
    depth, tokens = inputs.shape
    wide = gate_grad.shape[1]
    tile = tile_of(depth, 256)

    def body(inputs_ref, gate_ref, up_ref, gate_out, up_out):
        left = inputs_ref[...]
        gate_out[...] = scale * dot(left, gate_ref[...], ((1,), (0,)))
        up_out[...] = scale * dot(left, up_ref[...], ((1,), (0,)))

    once = pl.BlockSpec((tokens, wide), lambda i: (0, 0))
    out = pl.BlockSpec((tile, wide), lambda i: (i, 0))
    return pl.pallas_call(
        body,
        grid=(depth // tile,),
        in_specs=[pl.BlockSpec((tile, tokens), lambda i: (i, 0)), once, once],
        out_specs=[out, out],
        out_shape=[jax.ShapeDtypeStruct((depth, wide), jnp.float32)] * 2,
        compiler_params=params(),
        cost_estimate=cost(4 * tokens * wide * depth, 8 * wide * depth),
        name="projection_grads",
    )(inputs, gate_grad, up_grad)


def turned(pieces, others, axis):
    half = len(pieces)
    rows, depth = pieces[0].shape
    tile = tile_of(depth, 512)

    def body(*refs):
        out_ref, whole_ref = refs[2 * half :]
        here = lax.axis_index(axis)
        for k in range(half):
            whole_ref[here ^ (2 * k)] = refs[k][...]
            whole_ref[here ^ (2 * k + 1)] = refs[half + k][...]
        out_ref[...] = whole_ref[...].reshape(2 * half * rows, tile).T

    tokens = 2 * half * rows
    return pl.pallas_call(
        body,
        grid=(depth // tile,),
        in_specs=[pl.BlockSpec((rows, tile), lambda i: (0, i))] * (2 * half),
        out_specs=pl.BlockSpec((tile, tokens), lambda i: (i, 0)),
        out_shape=jax.ShapeDtypeStruct((depth, tokens), jnp.bfloat16),
        scratch_shapes=[pltpu.VMEM((2 * half, rows, tile), jnp.bfloat16)],
        compiler_params=params(),
        cost_estimate=cost(1, 4 * depth * tokens),
        name="turned",
    )(*pieces, *others)


def gather_parity(own, axis, size):
    return [own] + [
        lax.ppermute(own, axis, [(i, i ^ (2 * k)) for i in range(size)]) for k in range(1, size // 2)
    ]


def gather_others(pieces, axis, size):
    return [lax.ppermute(x, axis, [(i, i ^ 1) for i in range(size)]) for x in pieces]


def gather_places(size):
    def places(here):
        if size != 4:
            return [(here ^ k, True) for k in range(size)]
        outer = (here == 0) | (here == 3)
        inner = jnp.logical_not(outer)
        return [
            (here, True),
            (here ^ 1, True),
            (here ^ 3, inner),
            (here ^ 2, inner),
            (here ^ 2, outer),
            (here ^ 3, outer),
        ]

    return places


def gather_near(shard, axis, size):
    if size == 4:
        swaps = [[(i, i ^ 1) for i in range(size)], [(1, 2), (2, 1)]]
    else:
        swaps = [[(i, i ^ k) for i in range(size)] for k in range(1, size)]
    return [shard] + [lax.ppermute(shard, axis, pairs) for pairs in swaps]


def trade(term, shards, axis):
    here = lax.axis_index(axis)
    outer = (here == 0) | (here == 3)
    given = jnp.where(outer, term, shards.reshape(term.shape))
    return lax.ppermute(given, axis, [(i, i ^ 1) for i in range(4)])


def both(left, right):
    return (left.astype(jnp.float32) + right.astype(jnp.float32)).astype(jnp.bfloat16)


def sum_in(term, axis, size):
    total = term
    for k in range(size // 2 - 1):
        got = lax.ppermute(total, axis, [(k, k + 1), (size - 1 - k, size - 2 - k)])
        total = both(term, got)
    return total


def sum_swap(total, axis, size):
    half = size // 2
    return both(total, lax.ppermute(total, axis, [(half - 1, half), (half, half - 1)]))


def sum_out(total, axis, size):
    found = [total]
    for k in reversed(range(size // 2 - 1)):
        found.append(lax.ppermute(found[-1], axis, [(k + 1, k), (size - 2 - k, size - 1 - k)]))
    return found


def scatter_halves(keep, send, axis, size):
    return both(keep, lax.ppermute(send, axis, [(i, i ^ 1) for i in range(size)]))


def scatter_sum(halves, axis, size):
    here = lax.axis_index(axis)

    def block(k):
        at = (here // 2) ^ k
        return jnp.concatenate(
            [lax.dynamic_index_in_dim(x, at, 0, keepdims=False) for x in halves], axis=0
        )

    total = block(0).astype(jnp.float32)
    for k in range(1, size // 2):
        got = lax.ppermute(block(k), axis, [(i, i ^ (2 * k)) for i in range(size)])
        total += got.astype(jnp.float32)
    return total.astype(jnp.bfloat16)


def hold(*values):
    return lax.optimization_barrier(values)


def solution(mesh):
    n_row, n_col = mesh.shape["row"], mesh.shape["col"]

    def shards(layer_input, out_grad, gate_saved, up_saved, gate_weight, up_weight, down_weight):
        block, depth = layer_input.shape
        row_tokens, wide = gate_saved.shape
        tokens = block * n_col
        rows = block // CHUNKS
        scale = float(tokens) ** (-0.5)
        weights = (gate_weight, up_weight, ("row", "col"))

        view = (row_tokens // block, CHUNKS, rows, wide)
        gates = gather_near(gate_saved.reshape(view), "row", n_row)
        up_saved = up_saved.reshape(view)
        pieces = gather_parity(out_grad[:rows], "col", n_col)
        pieces, gates, up_saved, out_grad, layer_input = hold(
            pieces, gates, up_saved, out_grad, layer_input
        )
        ups = gather_near(up_saved, "row", n_row)
        others = gather_others(pieces, "col", n_col)
        first, grad = hidden_grad_terms(pieces, others, "col", down_weight)
        grads = [grad]
        pieces = gather_parity(out_grad[rows:], "col", n_col)
        first, gates, ups, pieces, layer_input = hold(first, gates, ups, pieces, layer_input)

        line = n_row == 4 and 2 * row_tokens * CHUNKS == tokens
        saved = [list(pair) for pair in zip(gates, ups)]
        if line:
            got = trade(first, jnp.stack([gates[2], ups[2]]), "row")
            passed = lax.ppermute(jnp.stack([gates[1], ups[1]]), "row", [(1, 2), (2, 1)])
            first = both(first, got)
            saved += [[passed], [got.reshape(passed.shape)]]
        else:
            first = sum_in(first, "row", n_row)
        others = gather_others(pieces, "col", n_col)
        second, grad = hidden_grad_terms(pieces, others, "col", down_weight)
        grads.append(grad)
        first, second, saved, layer_input = hold(first, second, saved, layer_input)

        if line:
            got = trade(second, saved[3][0], "row")
            second = both(second, got)
            saved += [[got.reshape(saved[3][0].shape)]]
        else:
            second = sum_in(second, "row", n_row)
        first = sum_swap(first, "row", n_row)
        inputs = gather_parity(layer_input, "col", n_col)
        first, second, saved, inputs = hold(first, second, saved, inputs)

        first = sum_out(first, "row", n_row)
        second = sum_swap(second, "row", n_row)
        down_weight_grad, *factors = down_weight_grads(
            saved, gather_places(n_row), grads, "row", scale
        )
        other_inputs = gather_others(inputs, "col", n_col)
        first, second, down_weight_grad, factors, other_inputs = hold(
            first, second, down_weight_grad, factors, other_inputs
        )

        second = sum_out(second, "row", n_row)
        *made, keep, send = input_grad_terms(0, first, *factors, *weights, ())
        inputs = turned(inputs, other_inputs, "col")
        second, made, keep, send, inputs = hold(second, made, keep, send, inputs)

        early = scatter_halves(keep, send, "col", n_col)
        *made, keep, send = input_grad_terms(1, second, *factors, *weights, made)
        early, made, keep, send = hold(early, made, keep, send)
        late = scatter_halves(keep, send, "col", n_col)
        late, made = hold(late, made)
        input_grad = scatter_sum([early, late], "col", n_col)
        made = [x.reshape(tokens, wide) for x in made]
        gate_weight_grad, up_weight_grad = projection_grads(inputs, *made, scale)
        return input_grad, gate_weight_grad, up_weight_grad, down_weight_grad

    by_token, by_unit = P("col", "row"), P("row", "col")
    return jax.shard_map(
        shards,
        mesh=mesh,
        in_specs=(by_token, by_token, by_unit, by_unit, by_unit, by_unit, by_token),
        out_specs=(by_token, by_unit, by_unit, by_token),
        check_vma=False,
    )
```

```python
import jax
import jax.numpy as jnp
from jax import lax
from jax.experimental import pallas as pl
from jax.experimental.pallas import tpu as pltpu
from jax.sharding import PartitionSpec as P

CHUNKS = 2
VMEM = 60 * 1024 * 1024


def tile_of(size, limit):
    return max(t for t in range(128, limit + 1, 128) if size % t == 0)


def params():
    return pltpu.CompilerParams(vmem_limit_bytes=VMEM)


def cost(flops, moved):
    return pl.CostEstimate(flops=flops, bytes_accessed=moved, transcendentals=0)


def dot(left, right, dims):
    return lax.dot_general(left, right, (dims, ((), ())), preferred_element_type=jnp.float32)


def halves_of(size):
    cut = max(size // 2 // 256 * 256, 128)
    return slice(0, size - cut), slice(size - cut, size)


def sigmoid(gate):
    return 1.0 / (1.0 + jnp.exp(-gate))


def hidden_grad_terms(q, pieces, others, axis, down):
    half = len(pieces)
    _, rows, depth = pieces[0].shape
    wide = down.shape[0]
    tokens = 2 * half * rows
    tile = tile_of(wide, 896)

    def body(*refs):
        down_ref, out_ref, grad_ref = refs[2 * half :]

        @pl.when(pl.program_id(0) == 0)
        def _():
            here = lax.axis_index(axis)
            for k in range(half):
                grad_ref[here ^ (2 * k)] = refs[k][...]
                grad_ref[here ^ (2 * k + 1)] = refs[half + k][...]

        left = grad_ref[...].reshape(tokens, depth)
        out_ref[...] = dot(left, down_ref[...], ((1,), (1,))).astype(jnp.bfloat16)

    return pl.pallas_call(
        body,
        grid=(wide // tile,),
        in_specs=[pl.BlockSpec((None, rows, depth), lambda i: (q, 0, 0))] * (2 * half)
        + [pl.BlockSpec((tile, depth), lambda i: (i, 0))],
        out_specs=[
            pl.BlockSpec((tokens, tile), lambda i: (0, i)),
            pl.BlockSpec((2 * half, rows, depth), lambda i: (0, 0, 0)),
        ],
        out_shape=[
            jax.ShapeDtypeStruct((tokens, wide), jnp.bfloat16),
            jax.ShapeDtypeStruct((2 * half, rows, depth), jnp.bfloat16),
        ],
        compiler_params=params(),
        cost_estimate=cost(2 * tokens * depth * wide, 2 * (down.size + tokens * depth)),
        name="hidden_grad_terms",
    )(*pieces, *others, down)


def down_weight_grads(saved, places, grads, axis, scale):
    blocks, _, _, wide = saved[0][0].shape
    cols, rows, depth = grads[0].shape
    chunks = len(grads)
    tokens = chunks * cols * rows
    tile = tile_of(wide, 256)
    flat = [x for shard in saved for x in shard]
    n = len(flat)

    def body(*refs):
        saved_refs = list(refs[:n])
        grad_refs, refs = refs[n : n + chunks], refs[n + chunks :]
        out_ref, by_gate_ref, by_up_ref, hidden_ref = refs
        for k, (shard, there) in enumerate(places(lax.axis_index(axis))):
            pair = [saved_refs.pop(0) for _ in saved[k]]
            gate_ref, up_ref = pair if len(pair) == 2 else (pair[0].at[0], pair[0].at[1])

            @pl.when(there)
            def _():
                gate_val = gate_ref[...].astype(jnp.float32)
                up_val = up_ref[...].astype(jnp.float32)
                sigma = sigmoid(gate_val)
                silu = gate_val * sigma
                slope = sigma * (1.0 + gate_val * (1.0 - sigma))
                to = pl.ds(shard * blocks, blocks)
                hidden_ref[to] = (silu * up_val).astype(jnp.bfloat16)
                by_gate_ref[to] = (up_val * slope).astype(jnp.bfloat16)
                by_up_ref[to] = silu.astype(jnp.bfloat16)

        res = 0.0
        for q in range(chunks):
            left = hidden_ref[:, q].reshape(cols * rows, tile)
            res += dot(left, grad_refs[q][...].reshape(cols * rows, depth), ((0,), (0,)))
        out_ref[...] = scale * res

    one = pl.BlockSpec((blocks, chunks, rows, tile), lambda i: (0, 0, 0, i))
    two = pl.BlockSpec((2, blocks, chunks, rows, tile), lambda i: (0, 0, 0, 0, i))
    factor = pl.BlockSpec((cols, chunks, rows, tile), lambda i: (0, 0, 0, i))
    factors = jax.ShapeDtypeStruct((cols, chunks, rows, wide), jnp.bfloat16)
    return pl.pallas_call(
        body,
        grid=(wide // tile,),
        in_specs=[one if x.ndim == 4 else two for x in flat]
        + [pl.BlockSpec((cols, rows, depth), lambda i: (0, 0, 0))] * chunks,
        out_specs=[pl.BlockSpec((tile, depth), lambda i: (i, 0)), factor, factor],
        out_shape=[jax.ShapeDtypeStruct((wide, depth), jnp.float32), factors, factors],
        scratch_shapes=[pltpu.VMEM((cols, chunks, rows, tile), jnp.bfloat16)],
        compiler_params=params(),
        cost_estimate=cost(2 * tokens * wide * depth, 4 * wide * depth),
        name="down_weight_grads",
    )(*flat, *grads)


def input_grad_terms(q, sums, by_gate, by_up, gate_weight, up_weight, axes, made):
    cols, chunks, rows, wide = by_gate.shape
    depth = gate_weight.shape[0]
    tokens = cols * rows
    levels = len(sums)
    tile = tile_of(depth, 512)
    steps = depth // tile

    def body(*refs):
        sums_refs, by_refs, weight_refs = refs[:levels], refs[levels : levels + 2], refs[levels + 2 :][:2]
        outs, keep_ref, send_ref = refs[-11:-9], refs[-9], refs[-8]
        sums_in, by_in, weights_in, grads, first_sems, weight_sems, out_sems = refs[-7:]

        def weight_copy(k, i):
            part = pl.ds(pl.multiple_of(i * tile, tile), tile)
            return pltpu.make_async_copy(
                weight_refs[k].at[part], weights_in.at[k, part], weight_sems.at[k, i]
            )

        firsts = [
            pltpu.make_async_copy(sums_refs[k], sums_in.at[k], first_sems.at[k]) for k in range(levels)
        ]
        firsts += [
            pltpu.make_async_copy(by_refs[k].at[:, q], by_in.at[k], first_sems.at[levels + k])
            for k in range(2)
        ]
        for copy in firsts:
            copy.start()
        for i in range(steps):
            for k in range(2):
                weight_copy(k, i).start()
        for copy in firsts:
            copy.wait()

        here = lax.axis_index(axes[0])
        hidden_grad = sums_in[0].astype(jnp.float32)
        for level in range(1, levels):
            at_level = (here == levels - 1 - level) | (here == levels + level)
            hidden_grad = jnp.where(at_level, sums_in[level].astype(jnp.float32), hidden_grad)
        for k in range(2):
            by = by_in[k].reshape(tokens, wide).astype(jnp.float32)
            grads[k] = (hidden_grad * by).astype(jnp.bfloat16).reshape(cols, rows, wide)
        out_copies = [
            pltpu.make_async_copy(grads.at[k], outs[k].at[:, q], out_sems.at[k]) for k in range(2)
        ]
        for copy in out_copies:
            copy.start()

        odd = lax.axis_index(axes[1]) % 2 == 1
        gate_grad = grads[0].reshape(tokens, wide)
        up_grad = grads[1].reshape(tokens, wide)

        @pl.loop(0, steps)
        def _(i):
            for k in range(2):
                weight_copy(k, i).wait()
            for part in halves_of(tile):
                size = part.stop - part.start
                at = pl.ds(pl.multiple_of(i * tile + part.start, 128), size)
                res = dot(gate_grad, weights_in[0, at], ((1,), (1,)))
                res += dot(up_grad, weights_in[1, at], ((1,), (1,)))
                res = res.astype(jnp.bfloat16).reshape(cols // 2, 2, rows, size)
                keep_ref[:, :, at] = jnp.where(odd, res[:, 1], res[:, 0])
                send_ref[:, :, at] = jnp.where(odd, res[:, 0], res[:, 1])

        for copy in out_copies:
            copy.wait()

    anywhere = pl.BlockSpec(memory_space=pl.ANY)
    in_vmem = pl.BlockSpec(memory_space=pltpu.VMEM)
    halves = jax.ShapeDtypeStruct((cols // 2, rows, depth), jnp.bfloat16)
    whole = jax.ShapeDtypeStruct((cols, chunks, rows, wide), jnp.bfloat16)
    return pl.pallas_call(
        body,
        in_specs=[anywhere] * (levels + 4 + len(made)),
        out_specs=[anywhere, anywhere, in_vmem, in_vmem],
        out_shape=[whole, whole, halves, halves],
        input_output_aliases={levels + 4 + j: j for j in range(len(made))},
        scratch_shapes=[
            pltpu.VMEM((levels, tokens, wide), jnp.bfloat16),
            pltpu.VMEM((2, cols, rows, wide), jnp.bfloat16),
            pltpu.VMEM((2, depth, wide), jnp.bfloat16),
            pltpu.VMEM((2, cols, rows, wide), jnp.bfloat16),
            pltpu.SemaphoreType.DMA((levels + 2,)),
            pltpu.SemaphoreType.DMA((2, steps)),
            pltpu.SemaphoreType.DMA((2,)),
        ],
        compiler_params=params(),
        cost_estimate=cost(4 * tokens * wide * depth, 4 * wide * depth),
        name="input_grad_terms",
    )(*sums, by_gate, by_up, gate_weight, up_weight, *made)


def projection_grads(inputs, gate_grad, up_grad, scale):
    depth, tokens = inputs.shape
    wide = gate_grad.shape[1]
    tile = tile_of(depth, 256)

    def body(inputs_ref, gate_ref, up_ref, gate_out, up_out):
        left = inputs_ref[...]
        gate_out[...] = scale * dot(left, gate_ref[...], ((1,), (0,)))
        up_out[...] = scale * dot(left, up_ref[...], ((1,), (0,)))

    once = pl.BlockSpec((tokens, wide), lambda i: (0, 0))
    out = pl.BlockSpec((tile, wide), lambda i: (i, 0))
    return pl.pallas_call(
        body,
        grid=(depth // tile,),
        in_specs=[pl.BlockSpec((tile, tokens), lambda i: (i, 0)), once, once],
        out_specs=[out, out],
        out_shape=[jax.ShapeDtypeStruct((depth, wide), jnp.float32)] * 2,
        compiler_params=params(),
        cost_estimate=cost(4 * tokens * wide * depth, 8 * wide * depth),
        name="projection_grads",
    )(inputs, gate_grad, up_grad)


def turned(pieces, others, axis):
    half = len(pieces)
    rows, depth = pieces[0].shape
    tile = tile_of(depth, 512)

    def body(*refs):
        out_ref, whole_ref = refs[2 * half :]
        here = lax.axis_index(axis)
        for k in range(half):
            whole_ref[here ^ (2 * k)] = refs[k][...]
            whole_ref[here ^ (2 * k + 1)] = refs[half + k][...]
        out_ref[...] = whole_ref[...].reshape(2 * half * rows, tile).T

    tokens = 2 * half * rows
    return pl.pallas_call(
        body,
        grid=(depth // tile,),
        in_specs=[pl.BlockSpec((rows, tile), lambda i: (0, i))] * (2 * half),
        out_specs=pl.BlockSpec((tile, tokens), lambda i: (i, 0)),
        out_shape=jax.ShapeDtypeStruct((depth, tokens), jnp.bfloat16),
        scratch_shapes=[pltpu.VMEM((2 * half, rows, tile), jnp.bfloat16)],
        compiler_params=params(),
        cost_estimate=cost(1, 4 * depth * tokens),
        name="turned",
    )(*pieces, *others)


def gather_parity(own, axis, size):
    return [own] + [
        lax.ppermute(own, axis, [(i, i ^ (2 * k)) for i in range(size)]) for k in range(1, size // 2)
    ]


def gather_others(pieces, axis, size):
    return [lax.ppermute(x, axis, [(i, i ^ 1) for i in range(size)]) for x in pieces]


def gather_places(size):
    def places(here):
        if size != 4:
            return [(here ^ k, True) for k in range(size)]
        outer = (here == 0) | (here == 3)
        inner = jnp.logical_not(outer)
        return [
            (here, True),
            (here ^ 1, True),
            (here ^ 3, inner),
            (here ^ 2, inner),
            (here ^ 2, outer),
            (here ^ 3, outer),
        ]

    return places


def gather_near(shard, axis, size):
    if size == 4:
        swaps = [[(i, i ^ 1) for i in range(size)], [(1, 2), (2, 1)]]
    else:
        swaps = [[(i, i ^ k) for i in range(size)] for k in range(1, size)]
    return [shard] + [lax.ppermute(shard, axis, pairs) for pairs in swaps]


def trade(term, shards, axis):
    here = lax.axis_index(axis)
    outer = (here == 0) | (here == 3)
    given = jnp.where(outer, term, shards.reshape(term.shape))
    return lax.ppermute(given, axis, [(i, i ^ 1) for i in range(4)])


def both(left, right):
    return (left.astype(jnp.float32) + right.astype(jnp.float32)).astype(jnp.bfloat16)


def sum_in(term, axis, size):
    total = term
    for k in range(size // 2 - 1):
        got = lax.ppermute(total, axis, [(k, k + 1), (size - 1 - k, size - 2 - k)])
        total = both(term, got)
    return total


def sum_swap(total, axis, size):
    half = size // 2
    return both(total, lax.ppermute(total, axis, [(half - 1, half), (half, half - 1)]))


def sum_out(total, axis, size):
    found = [total]
    for k in reversed(range(size // 2 - 1)):
        found.append(lax.ppermute(found[-1], axis, [(k + 1, k), (size - 2 - k, size - 1 - k)]))
    return found


def scatter_halves(keep, send, axis, size):
    return both(keep, lax.ppermute(send, axis, [(i, i ^ 1) for i in range(size)]))


def scatter_sum(halves, axis, size):
    here = lax.axis_index(axis)

    def block(k):
        at = (here // 2) ^ k
        return jnp.concatenate(
            [lax.dynamic_index_in_dim(x, at, 0, keepdims=False) for x in halves], axis=0
        )

    total = block(0).astype(jnp.float32)
    for k in range(1, size // 2):
        got = lax.ppermute(block(k), axis, [(i, i ^ (2 * k)) for i in range(size)])
        total += got.astype(jnp.float32)
    return total.astype(jnp.bfloat16)


def hold(*values):
    return lax.optimization_barrier(values)


def solution(mesh):
    n_row, n_col = mesh.shape["row"], mesh.shape["col"]

    def shards(layer_input, out_grad, gate_saved, up_saved, gate_weight, up_weight, down_weight):
        block, depth = layer_input.shape
        row_tokens, wide = gate_saved.shape
        tokens = block * n_col
        rows = block // CHUNKS
        scale = float(tokens) ** (-0.5)
        weights = (gate_weight, up_weight, ("row", "col"))

        view = (row_tokens // block, CHUNKS, rows, wide)
        gates = gather_near(gate_saved.reshape(view), "row", n_row)
        up_saved = up_saved.reshape(view)
        pieces = gather_parity(out_grad.reshape(CHUNKS, rows, depth), "col", n_col)
        pieces, gates, up_saved, layer_input = hold(pieces, gates, up_saved, layer_input)
        ups = gather_near(up_saved, "row", n_row)
        others = gather_others(pieces, "col", n_col)
        first, grad = hidden_grad_terms(0, pieces, others, "col", down_weight)
        grads = [grad]
        first, gates, ups, pieces, others, layer_input = hold(
            first, gates, ups, pieces, others, layer_input
        )

        line = n_row == 4 and 2 * row_tokens * CHUNKS == tokens
        saved = [list(pair) for pair in zip(gates, ups)]
        if line:
            got = trade(first, jnp.stack([gates[2], ups[2]]), "row")
            passed = lax.ppermute(jnp.stack([gates[1], ups[1]]), "row", [(1, 2), (2, 1)])
            first = both(first, got)
            saved += [[passed], [got.reshape(passed.shape)]]
        else:
            first = sum_in(first, "row", n_row)
        second, grad = hidden_grad_terms(1, pieces, others, "col", down_weight)
        grads.append(grad)
        first, second, saved, layer_input = hold(first, second, saved, layer_input)

        if line:
            got = trade(second, saved[3][0], "row")
            second = both(second, got)
            saved += [[got.reshape(saved[3][0].shape)]]
        else:
            second = sum_in(second, "row", n_row)
        first = sum_swap(first, "row", n_row)
        inputs = gather_parity(layer_input, "col", n_col)
        first, second, saved, inputs = hold(first, second, saved, inputs)

        first = sum_out(first, "row", n_row)
        second = sum_swap(second, "row", n_row)
        down_weight_grad, *factors = down_weight_grads(
            saved, gather_places(n_row), grads, "row", scale
        )
        other_inputs = gather_others(inputs, "col", n_col)
        first, second, down_weight_grad, factors, other_inputs = hold(
            first, second, down_weight_grad, factors, other_inputs
        )

        second = sum_out(second, "row", n_row)
        *made, keep, send = input_grad_terms(0, first, *factors, *weights, ())
        inputs = turned(inputs, other_inputs, "col")
        second, made, keep, send, inputs = hold(second, made, keep, send, inputs)

        early = scatter_halves(keep, send, "col", n_col)
        *made, keep, send = input_grad_terms(1, second, *factors, *weights, made)
        early, made, keep, send = hold(early, made, keep, send)
        late = scatter_halves(keep, send, "col", n_col)
        late, made = hold(late, made)
        input_grad = scatter_sum([early, late], "col", n_col)
        made = [x.reshape(tokens, wide) for x in made]
        gate_weight_grad, up_weight_grad = projection_grads(inputs, *made, scale)
        return input_grad, gate_weight_grad, up_weight_grad, down_weight_grad

    by_token, by_unit = P("col", "row"), P("row", "col")
    return jax.shard_map(
        shards,
        mesh=mesh,
        in_specs=(by_token, by_token, by_unit, by_unit, by_unit, by_unit, by_token),
        out_specs=(by_token, by_unit, by_unit, by_token),
        check_vma=False,
    )
```
